32 devices in a mesh: req: 8 (over z, x), tp: 4 (over y, core).
Axes of the slice: x: 2, y: 2, z: 4, core: 2. Of those that a mesh axis runs over, the one named last changes fastest.
Arguments:
- tokens: bfloat16 [8192, 1280], P('req'), may hold values from -14 to 14
- segments: int32 [8192], P('req'), may hold values from 0 to 6, never falling along the last dimension, each value on 1 to 2048 neighbouring positions
- attend_gain: bfloat16 [1280], replicated, may hold values from 0.25 to 1.75
- attend_weight: bfloat16 [1280, 3, 1280], P(None, None, 'tp'), may hold values from -1 to 1
- output_weight: bfloat16 [1280, 1280], P('tp'), may hold values from -0.15625 to 0.15625
- mixer_gain: bfloat16 [1280], replicated, may hold values from 0.25 to 1.75
- expand_weight: bfloat16 [1280, 5120], P(None, 'tp'), may hold values from -0.15625 to 0.15625
- reduce_weight: bfloat16 [5120, 1280], P('tp'), may hold values from -0.078125 to 0.078125
- output_gain: bfloat16 [1280], replicated, may hold values from 0.25 to 1.75
- merge_weight: bfloat16 [5120, 1280], P(None, 'tp'), may hold values from -0.078125 to 0.078125
- merge_index: int32 [2048, 4], P('req'), may hold values from 0 to 8191, as said below
- owners: int32 [2048, 1], P('req'), may hold values from 0 to 7; in each aligned block of 256 rows (0 to 255, 256 to 511, ...) at most 64 rows name the same one
Outputs:
- owned: bfloat16 [8, 8, 64, 1280], P('req', None, None, 'tp')
The draws below stay inside these ranges and needn't reach their ends.
Inputs may be any that keep to these rules, and one draw needn't show every extreme that they name: segments never fall along the tokens; every image has at most 2048 tokens. `merge_index`: merged rows 256 * j to 256 * (j + 1) - 1 name the tokens 1024 * j to 1024 * (j + 1) - 1, each exactly once. `owners`: within the rows of one index of req each owner is named at most 64 times.
All inputs are finite; a program needn't handle non-finite values.
Results may differ from the reference program's by a relative error of at most 0.014.
Values may be sent and summed in bfloat16 or wider, within the bound.
No kernel may reach another device: no remote copies, remote signals or barrier semaphores. Data moves between devices by JAX's collectives and lax.ppermute only.
A program may use at most 128 MiB of HBM per device.

```python
import math
import jax
import jax.numpy as jnp
import numpy as np
from jax import lax

D = 1280
HEADS = 16
HD = 80
FF = 5120
TOK_DEV = 1024
TOKENS = 8192
M_DEV = 256
MERGED = 2048
CAP = 64
N_REQ = 8
N_TP = 4


def draw_tokens(key, part):
    first = jax.random.fold_in(key, 0)
    values = jax.random.normal(first, (TOKENS, D), jnp.float32)
    return jnp.clip(values, -14.0, 14.0).astype(jnp.bfloat16)


def draw_attend_weight(key, part):
    first = jax.random.fold_in(key, 0)
    spread = jnp.clip(jax.random.normal(first, (D, 3, D), jnp.float32), -6.0, 6.0) / math.sqrt(D)
    values = 2.0 * spread
    return jnp.clip(values, -1.0, 1.0).astype(jnp.bfloat16)


def shuffle_block(stream):
    return jax.random.permutation(stream, TOK_DEV)


def draw_merge_index(key, part):
    blocks = TOKENS // TOK_DEV
    streams = jax.random.split(key, blocks)
    orders = jax.vmap(shuffle_block)(streams).astype(jnp.int32)
    starts = (jnp.arange(blocks, dtype=jnp.int32) * TOK_DEV)[:, None]
    return (orders + starts).reshape(MERGED, 4)


def shard_levels(own_key, dims, shards, low, high):
    loudness = 1.0
    for axis_at, shards_of in shards:
        heights = jax.random.uniform(jax.random.fold_in(jax.random.fold_in(own_key, 6), axis_at), (shards_of,), jnp.float32, low / len(shards), high / len(shards))
        loudness = loudness * jnp.repeat(jnp.exp(heights), dims[axis_at] // shards_of).reshape((-1,) + (1,) * (len(dims) - 1 - axis_at))
    return loudness


def length_profile(count, total, bound, slope):
    loads = [(1 << 20) // math.isqrt(standing ** slope) + 1 for standing in range(2, count + 1)]
    spare, holding = total - bound - (count - 1), [1] * (count - 1)
    while spare > 0:
        free = [i for i in range(count - 1) if holding[i] < bound]
        whole, remaining = sum([loads[i] for i in free]), spare
        for i in free:
            more = min(bound - holding[i], max(1, remaining * loads[i] // whole), spare)
            holding[i] = holding[i] + more
            spare = spare - more
    return np.array([bound] + holding)


def ragged(stream_key, number_of, total, limit, slope):
    if number_of == 2:
        one = jax.random.randint(stream_key, (), max(1, total - limit), min(limit, total - 1) + 1)
        return jnp.stack([one, total - one])
    lengths = jnp.asarray(length_profile(number_of, total, limit, slope), jnp.int32)
    couples = (number_of - 1) // 2
    giver, receiver = lengths[1:1 + 2 * couples:2], lengths[2:2 + 2 * couples:2]
    room = jnp.minimum(giver - 1, limit - receiver)
    moved = jax.random.randint(jax.random.fold_in(stream_key, 1), (couples,), 0, 1 << 20) % (room + 1)
    lengths = lengths.at[1:1 + 2 * couples:2].set(giver - moved).at[2:2 + 2 * couples:2].set(receiver + moved)
    return lengths[jax.random.permutation(jax.random.fold_in(stream_key, 2), number_of)]


def shared_out(key, own, number, rows, number_of, top, limit, skew):
    order = jax.random.permutation(key, number_of)
    packed, usual = portions_of(number_of, rows * top, limit, skew, True), portions_of(number_of, rows * top, limit, skew, False)
    places = jnp.arange(number_of)

    def named(sizes, turn):
        used = int((sizes > 0).sum())
        fixed = max(1, used // 4)
        moved = fixed + (places - fixed + turn * (used - fixed)) % max(1, number_of - fixed)
        return jnp.zeros((number_of,), jnp.int32).at[order[jnp.where(places < fixed, places, moved)]].set(jnp.asarray(sizes, jnp.int32))

    sizes = jnp.where(number % 4 == 0, named(packed, number // 4), named(usual, number - number // 4 - 1))
    mixed = jax.random.permutation(jax.random.fold_in(own, 3), number_of)
    donor, sink = mixed[0:number_of // 2 * 2:2], mixed[1:number_of // 2 * 2:2]
    slack = jnp.minimum(sizes[donor] - 1, limit - sizes[sink]) // 2
    slack = jnp.where((donor == order[0]) | (sink == order[0]) | (sizes[sink] == 0), 0, jnp.maximum(slack, 0))
    moved = jax.random.randint(jax.random.fold_in(own, 4), (number_of // 2,), 0, 1 << 20) % (slack + 1)
    sizes = sizes.at[donor].add(-moved).at[sink].add(moved)
    members = jnp.searchsorted(jnp.cumsum(sizes), jnp.arange(rows * top), side="right").astype(jnp.int32)
    listing = members.reshape(top, rows).T
    listing = listing[jax.random.permutation(jax.random.fold_in(own, 1), rows)]
    turn = jax.random.randint(jax.random.fold_in(own, 2), (rows, 1), 0, top)
    return jnp.take_along_axis(listing, (jnp.arange(top)[None, :] + turn) % top, axis=1)


def portions_of(amount, total, limit, skew, full):
    weights = [(1 << 20) // math.isqrt(grade ** skew) + 1 for grade in range(1, amount + 1)]
    largest = limit if full else min(limit, max(-(-total // amount), total * weights[0] // sum(weights)))
    least = 1 if total - largest >= amount - 1 else 0
    holding, surplus = [largest] + [least] * (amount - 1), total - largest - least * (amount - 1)
    while surplus > 0:
        free = [i for i in range(1, amount) if holding[i] < largest] or [i for i in range(1, amount) if holding[i] < limit]
        whole, left = sum([weights[i] for i in free]), surplus
        for i in free:
            addition = min(limit - holding[i], max(1, left * weights[i] // whole), surplus)
            holding[i] = holding[i] + addition
            surplus = surplus - addition
    return np.array(holding)


def noise(rng, dims, width, most, shards=(), kind=jnp.bfloat16):
    factor_of = shard_levels(rng, dims, shards, -0.22, 0.18) if shards else 1.0
    values = jax.random.normal(rng, dims, jnp.float32) * width * factor_of
    return jnp.minimum(jnp.maximum(values, -most), most).astype(kind)


def setup_inputs(seed: int = 0) -> dict:
    arg_keys = jax.random.split(jax.random.key(seed), 13)
    tokens = draw_tokens(jax.random.fold_in(arg_keys[12], 71), 0)
    segments = jnp.searchsorted(jnp.cumsum(ragged(arg_keys[1], N_REQ - 1, TOKENS, 2 * TOK_DEV, 2)), jnp.arange(TOKENS), side="right").astype(jnp.int32)
    attend_gain = jnp.clip(1.0 + 0.15 * jax.random.normal(arg_keys[2], (D,), jnp.float32), 0.25, 1.75).astype(jnp.bfloat16)
    attend_weight = draw_attend_weight(jax.random.fold_in(arg_keys[12], 71), 0)
    output_weight = noise(arg_keys[4], (D, D), D ** -0.5, 0.15625, ((0, 4),))
    mixer_gain = jnp.clip(1.0 + 0.15 * jax.random.normal(arg_keys[5], (D,), jnp.float32), 0.25, 1.75).astype(jnp.bfloat16)
    expand_weight = noise(arg_keys[6], (D, FF), D ** -0.5, 0.15625, ((1, 4),))
    reduce_weight = noise(arg_keys[7], (FF, D), FF ** -0.5, 0.078125, ((0, 4),))
    output_gain = jnp.clip(1.0 + 0.15 * jax.random.normal(arg_keys[8], (D,), jnp.float32), 0.25, 1.75).astype(jnp.bfloat16)
    merge_weight = noise(arg_keys[9], (4 * D, D), (4 * D) ** -0.5, 0.078125, ((1, 4),))
    merge_index = draw_merge_index(jax.random.fold_in(arg_keys[12], 71), 0)
    owners_keys = jax.random.split(jax.random.fold_in(arg_keys[11], 1), MERGED // M_DEV)
    owners_turns = jax.random.permutation(jax.random.fold_in(arg_keys[11], 3), MERGED // M_DEV)
    owners = jax.vmap(lambda own, number: shared_out(jax.random.fold_in(arg_keys[11], 2), own, number, M_DEV, N_REQ, 1, CAP, 2))(owners_keys, owners_turns).reshape((MERGED, 1))
    return dict(tokens=tokens, segments=segments, attend_gain=attend_gain, attend_weight=attend_weight, output_weight=output_weight, mixer_gain=mixer_gain, expand_weight=expand_weight, reduce_weight=reduce_weight, output_gain=output_gain, merge_weight=merge_weight, merge_index=merge_index, owners=owners)


def layer_norm(stream, gain):
    center = lax.optimization_barrier(jnp.mean(stream, axis=-1, keepdims=True))
    shifted = stream - center
    spread = lax.optimization_barrier(jnp.mean(shifted * shifted, axis=-1, keepdims=True))
    return shifted * lax.rsqrt(spread + 1e-06) * gain.astype(jnp.float32)

def round_trip(values):
    return lax.optimization_barrier(values.astype(jnp.bfloat16)).astype(jnp.float32)

def reference(tokens, segments, attend_gain, attend_weight, output_weight, mixer_gain, expand_weight, reduce_weight, output_gain, merge_weight, merge_index, owners):
    stream = tokens.astype(jnp.float32)
    attend_in = layer_norm(stream, attend_gain).astype(jnp.bfloat16)
    projected = jnp.dot(attend_in, attend_weight.reshape(D, 3 * D), preferred_element_type=jnp.float32).astype(jnp.bfloat16)
    queries = projected[:, :D].reshape(TOKENS, HEADS, HD)
    key_rows = projected[:, D:2 * D].reshape(TOKENS, HEADS, HD)
    value_rows = projected[:, 2 * D:].reshape(TOKENS, HEADS, HD)
    margin = 2 * TOK_DEV
    key_padded = jnp.pad(key_rows, ((margin, margin), (0, 0), (0, 0)))
    value_padded = jnp.pad(value_rows, ((margin, margin), (0, 0), (0, 0)))
    segment_padded = jnp.pad(segments, (margin, margin), constant_values=-1)
    factor = 1.0 / math.sqrt(HD)

    def block_context(block):
        start = (block * TOK_DEV).astype(jnp.int32)
        query_block = lax.dynamic_slice_in_dim(queries, start, TOK_DEV, 0).astype(jnp.float32)
        query_segment = lax.dynamic_slice_in_dim(segments, start, TOK_DEV, 0)
        key_block = lax.dynamic_slice_in_dim(key_padded, start, 5 * TOK_DEV, 0).astype(jnp.float32)
        value_block = lax.dynamic_slice_in_dim(value_padded, start, 5 * TOK_DEV, 0).astype(jnp.float32)
        key_segment = lax.dynamic_slice_in_dim(segment_padded, start, 5 * TOK_DEV, 0)
        scores = jnp.einsum('qhd,khd->hqk', query_block, key_block) * factor
        matches = (query_segment[:, None] == key_segment[None, :])[None]
        largest = lax.optimization_barrier(jnp.max(jnp.where(matches, scores, -1e+30), axis=-1, keepdims=True))
        probs = jnp.where(matches, jnp.exp(scores - largest), 0.0)
        norms = lax.optimization_barrier(jnp.sum(probs, axis=-1))
        weighted = jnp.einsum('hqk,khd->qhd', round_trip(probs), value_block)
        return (weighted / jnp.transpose(norms)[:, :, None]).astype(jnp.bfloat16)
    context = lax.map(block_context, jnp.arange(N_REQ, dtype=jnp.int32)).reshape(TOKENS, N_TP, D // N_TP)
    head_terms = jnp.einsum('tgc,gcd->gtd', context.astype(jnp.float32), output_weight.astype(jnp.float32).reshape(N_TP, D // N_TP, D))
    middle = stream + lax.optimization_barrier(jnp.sum(round_trip(head_terms), axis=0))
    mixer_in = layer_norm(middle, mixer_gain).astype(jnp.bfloat16)
    expanded = jax.nn.gelu(jnp.dot(mixer_in, expand_weight, preferred_element_type=jnp.float32), approximate=False).astype(jnp.bfloat16)
    hidden_terms = jnp.einsum('tgc,gcd->gtd', expanded.astype(jnp.float32).reshape(TOKENS, N_TP, FF // N_TP), reduce_weight.astype(jnp.float32).reshape(N_TP, FF // N_TP, D))
    final_stream = middle + lax.optimization_barrier(jnp.sum(round_trip(hidden_terms), axis=0))
    final_normed = layer_norm(final_stream, output_gain).astype(jnp.bfloat16)
    merged = jnp.take(final_normed, merge_index.reshape(-1), axis=0).reshape(MERGED, 4 * D)
    feature = jnp.dot(merged, merge_weight, preferred_element_type=jnp.float32).astype(jnp.bfloat16)
    target = owners[:, 0].reshape(N_REQ, M_DEV)
    choose = (target[:, :, None] == jnp.arange(N_REQ, dtype=jnp.int32)[None, None, :]).astype(jnp.int32)
    slot = lax.optimization_barrier(jnp.sum((jnp.cumsum(choose, axis=1) - 1) * choose, axis=2)).astype(jnp.int32)
    source = jnp.repeat(jnp.arange(N_REQ, dtype=jnp.int32), M_DEV)
    owned = jnp.zeros((N_REQ, N_REQ, CAP, D), jnp.bfloat16)
    owned = owned.at[target.reshape(-1), source, slot.reshape(-1)].set(feature)
    return owned
```

```python
import functools
import math

import jax
import jax.numpy as jnp
from jax import lax
from jax.experimental import pallas as pl
from jax.experimental.pallas import tpu as pltpu
from jax.sharding import PartitionSpec as P

HD = 80
TILE = 512
MASKED = -1e30
START = -1e28
FACTOR = 1.0 / math.sqrt(HD)
MIB = 1 << 20


def swap(block, axis, flip):
    return lax.ppermute(block, axis, [(i, i ^ flip) for i in range(lax.axis_size(axis))])


def shifted(block, axis, distance):
    devices = range(lax.axis_size(axis))
    route = [(i - distance, i) for i in devices if i - distance in devices]
    return lax.ppermute(block, axis, route)


def normalized(stream, gain):
    center = jnp.mean(stream, axis=-1, keepdims=True)
    moved = stream - center
    spread = jnp.mean(moved * moved, axis=-1, keepdims=True)
    return (moved * lax.rsqrt(spread + 1e-06) * gain).astype(jnp.bfloat16)


def dot(a, b, contract):
    return lax.dot_general(a, b, (contract, ((), ())), preferred_element_type=jnp.float32)


NN = ((1,), (0,))
NT = ((1,), (1,))


def vmem(limit):
    return pltpu.CompilerParams(vmem_limit_bytes=limit * MIB)


def project_kernel(par_ref, x_ref, gain_ref, w_ref, kv_keep, kv_send, q_keep, q_send):
    par = par_ref[0]
    half = w_ref.shape[2]
    rows = normalized(x_ref[...].astype(jnp.float32), gain_ref[...])
    for which, kv, q in ((par, kv_keep, q_keep), (1 - par, kv_send, q_send)):
        for part in (1, 2):
            out = dot(w_ref[part, which], rows, NT).astype(jnp.bfloat16)
            kv[(part - 1) * half : part * half, :] = out
        q[...] = dot(w_ref[0, which], rows, NT).astype(jnp.bfloat16)


def project(par, tokens, gain, weight):
    rows, width = tokens.shape
    half = weight.shape[2]
    step = 256
    shapes = [(2 * half, rows), (2 * half, rows), (half, rows), (half, rows)]
    return pl.pallas_call(
        project_kernel,
        grid_spec=pltpu.PrefetchScalarGridSpec(
            num_scalar_prefetch=1,
            grid=(rows // step,),
            in_specs=[
                pl.BlockSpec((step, width), lambda i, s: (i, 0)),
                pl.BlockSpec((1, width), lambda i, s: (0, 0)),
                pl.BlockSpec(weight.shape, lambda i, s: (0, 0, 0, 0)),
            ],
            out_specs=[pl.BlockSpec((s[0], step), lambda i, s: (0, i)) for s in shapes],
        ),
        out_shape=[jax.ShapeDtypeStruct(s, jnp.bfloat16) for s in shapes],
        compiler_params=vmem(32),
        name="project",
    )(par, tokens, gain, weight)


def attend_kernel(blocks, base, first, last, meta, *refs):
    q_refs, refs = refs[:2], refs[2:]
    kv_refs, refs = refs[:blocks], refs[blocks:]
    q_segment, k_segment, refs = refs[0], refs[1], refs[2:]
    if first:
        acc_out, ml_out, refs = refs[0], refs[1], refs[2:]
    else:
        acc_in, ml_in, ctx_out, refs = refs[0], refs[1], refs[2], refs[3:]
    keys, values, columns, acc, ml = refs
    heads = 2
    tiles_of = kv_refs[0].shape[1] // TILE
    tiles = blocks * tiles_of
    j = pl.program_id(0)

    @pl.when(j == 0)
    def _():
        for b in range(blocks):
            for t in range(tiles_of):
                at = slice(t * TILE, (t + 1) * TILE)
                for h in range(heads):
                    block = kv_refs[b][h * HD : (h + 1) * HD, at].astype(jnp.float32)
                    keys[b * tiles_of + t, h] = jnp.transpose(block).astype(jnp.bfloat16)
                    values[b * tiles_of + t, h] = kv_refs[b][
                        (heads + h) * HD : (heads + h + 1) * HD, at
                    ]
                row = jnp.broadcast_to(k_segment[b : b + 1, at], (128, TILE))
                columns[b * tiles_of + t] = jnp.transpose(row)

    if first:
        acc[...] = jnp.zeros_like(acc)
        ml[0:2, :] = jnp.full((2, TILE), START, jnp.float32)
        ml[2:4, :] = jnp.zeros((2, TILE), jnp.float32)
    else:
        acc[...] = acc_in[0]
        ml[...] = ml_in[0]

    queries = jnp.where(j < 2, q_refs[0][...], q_refs[1][...])
    q_low, q_high = meta[2 + 2 * j], meta[3 + 2 * j]
    q_row = q_segment[0]

    def update(t, masked):
        if masked:
            column = columns[t]
            matches = jnp.concatenate([column] * (TILE // 128), axis=1) == q_row
        for h in range(heads):
            scores = dot(keys[t, h], queries[h * HD : (h + 1) * HD, :], NN)
            if masked:
                scores = jnp.where(matches, scores, MASKED)
            old = ml[h : h + 1, :]
            new = jnp.maximum(old, jnp.max(scores, axis=0, keepdims=True))
            probs = jnp.exp((scores - new) * FACTOR)
            shrink = jnp.exp((old - new) * FACTOR)
            ml[h : h + 1, :] = new
            ml[2 + h : 3 + h, :] = ml[2 + h : 3 + h, :] * shrink + jnp.sum(
                probs, axis=0, keepdims=True
            )
            acc[h * HD : (h + 1) * HD, :] = acc[h * HD : (h + 1) * HD, :] * shrink + dot(
                values[t, h], probs.astype(jnp.bfloat16), NN
            )

    def visit(t, carry):
        at = 10 + 2 * (base * tiles_of + t)
        k_low, k_high = meta[at], meta[at + 1]
        touches = (k_high >= q_low) & (k_low <= q_high)
        whole = (k_low == k_high) & (q_low == q_high)

        @pl.when(touches & whole)
        def _():
            update(t, False)

        @pl.when(touches & jnp.logical_not(whole))
        def _():
            update(t, True)

        return carry

    lax.fori_loop(0, tiles, visit, 0)
    if first:
        acc_out[0] = acc[...]
        ml_out[0] = ml[...]
    else:
        for h in range(heads):
            at = slice(h * HD, (h + 1) * HD)
            ctx_out[0, at, :] = (acc[at, :] / ml[2 + h : 3 + h, :]).astype(jnp.bfloat16)


def attend(meta, q_own, q_peer, key_values, q_segment, k_segment, base, state=None):
    half, rows = q_own.shape
    blocks = len(key_values)
    tiles = blocks * rows // TILE
    q_spec = pl.BlockSpec((half, TILE), lambda j, s: (0, (j % 2) ^ s[1]))
    whole = lambda a: pl.BlockSpec(a.shape, lambda j, s: (0,) * a.ndim)
    acc_spec = pl.BlockSpec((1, half, TILE), lambda j, s: (j, 0, 0))
    ml_spec = pl.BlockSpec((1, 4, TILE), lambda j, s: (j, 0, 0))
    in_specs = [q_spec, q_spec] + [whole(kv) for kv in key_values]
    in_specs += [pl.BlockSpec((1, 1, TILE), lambda j, s: (j, 0, 0)), whole(k_segment)]
    operands = [q_own, q_peer, *key_values, q_segment, k_segment]
    if state is None:
        out_specs = [acc_spec, ml_spec]
        out_shape = [
            jax.ShapeDtypeStruct((4, half, TILE), jnp.float32),
            jax.ShapeDtypeStruct((4, 4, TILE), jnp.float32),
        ]
    else:
        in_specs += [acc_spec, ml_spec]
        operands += list(state)
        out_specs = acc_spec
        out_shape = jax.ShapeDtypeStruct((4, half, TILE), jnp.bfloat16)
    return pl.pallas_call(
        functools.partial(attend_kernel, blocks, base, state is None, state is not None),
        grid_spec=pltpu.PrefetchScalarGridSpec(
            num_scalar_prefetch=1,
            grid=(4,),
            in_specs=in_specs,
            out_specs=out_specs,
            scratch_shapes=[
                pltpu.VMEM((tiles, 2, TILE, HD), jnp.bfloat16),
                pltpu.VMEM((tiles, 2, HD, TILE), jnp.bfloat16),
                pltpu.VMEM((tiles, TILE, 128), jnp.float32),
                pltpu.VMEM((half, TILE), jnp.float32),
                pltpu.VMEM((4, TILE), jnp.float32),
            ],
        ),
        out_shape=out_shape,
        compiler_params=vmem(40),
        cost_estimate=pl.CostEstimate(
            flops=8_000_000_000, bytes_accessed=8_000_000, transcendentals=8_000_000
        ),
        name="attend_local" if state is None else "attend_far",
    )(meta, *operands)


def mixer_kernel(place, *refs):
    pieces, refs = refs[:8], refs[8:]
    x_ref, gain_ref, refs = refs[0], refs[1], refs[2:]
    wo_hbm, refs = refs[:4], refs[4:]
    (we_own, we_other, wr_own, wr_other, sent, kept, refs) = (*refs[:6], refs[6:])
    context, wo, we, wr, sems = refs
    par = place[0]
    half = pieces[0].shape[0]
    copies = []
    for t in range(4):
        copies.append(pltpu.make_async_copy(wo_hbm[t], wo.at[t], sems.at[t]))
    copies.append(pltpu.make_async_copy(we_own, we.at[0], sems.at[4]))
    copies.append(pltpu.make_async_copy(we_other, we.at[1], sems.at[5]))
    copies.append(pltpu.make_async_copy(wr_own, wr.at[0], sems.at[6]))
    copies.append(pltpu.make_async_copy(wr_other, wr.at[1], sems.at[7]))
    for copy in copies:
        copy.start()
    total = x_ref[...].astype(jnp.float32)
    for t in range(4):
        copies[t].wait()
        for h in range(2):
            piece = jnp.transpose(pieces[2 * t + h][...].astype(jnp.float32))
            total += dot(piece.astype(jnp.bfloat16), wo[t, par ^ h], NN)
    rows = normalized(total, gain_ref[...])
    for s in range(2):
        copies[4 + s].wait()
        copies[6 + s].wait()
        hidden = we.shape[2]
        step = 256
        for n in range(hidden // step):
            at = slice(n * step, (n + 1) * step)
            inner = dot(rows, we[s, :, at], NN)
            grown = 0.5 * inner * (1.0 + lax.erf(inner * (1.0 / math.sqrt(2.0))))
            context[:, s * hidden + n * step : s * hidden + (n + 1) * step] = grown.astype(
                jnp.bfloat16
            )
    hidden = we.shape[2]
    out = dot(context[:, :hidden], wr[0], NN) + dot(context[:, hidden:], wr[1], NN)
    sent[...] = out.astype(jnp.bfloat16)
    kept[...] = total + out


def mixer(place, pieces, tokens, gain, wo, weights, chunk, chunk_rows):
    half = pieces[0].shape[0]
    width = tokens.shape[1]
    per_core = pieces[0].shape[1]
    chunks = per_core // chunk_rows
    hidden = weights[0].shape[1]
    piece_spec = pl.BlockSpec((half, chunk_rows), lambda i, s: (0, chunk))
    any_spec = pl.BlockSpec(memory_space=pl.ANY)
    out_spec = pl.BlockSpec((chunk_rows, width), lambda i, s: (0, 0))
    return pl.pallas_call(
        mixer_kernel,
        grid_spec=pltpu.PrefetchScalarGridSpec(
            num_scalar_prefetch=1,
            grid=(1,),
            in_specs=[piece_spec] * 8
            + [
                pl.BlockSpec((chunk_rows, width), lambda i, s: (s[1] * chunks + chunk, 0)),
                pl.BlockSpec((1, width), lambda i, s: (0, 0)),
            ]
            + [any_spec] * 8,
            out_specs=[out_spec, out_spec],
            scratch_shapes=[
                pltpu.VMEM((chunk_rows, 2 * hidden), jnp.bfloat16),
                pltpu.VMEM((4,) + wo[0].shape, jnp.bfloat16),
                pltpu.VMEM((2,) + weights[0].shape, jnp.bfloat16),
                pltpu.VMEM((2,) + weights[2].shape, jnp.bfloat16),
                pltpu.SemaphoreType.DMA((8,)),
            ],
        ),
        out_shape=[
            jax.ShapeDtypeStruct((chunk_rows, width), jnp.bfloat16),
            jax.ShapeDtypeStruct((chunk_rows, width), jnp.float32),
        ],
        compiler_params=vmem(48),
        cost_estimate=pl.CostEstimate(
            flops=5_000_000_000, bytes_accessed=20_000_000, transcendentals=0
        ),
        name="mixer",
    )(place, *pieces, tokens, gain, *wo, *weights)


def one_hot_rows(index_ref, k, first, rows):
    column = jnp.transpose(jnp.broadcast_to(index_ref[k : k + 1, :], (128, index_ref.shape[1])))
    lanes = lax.broadcasted_iota(jnp.int32, (1, 128), 1)
    parts = [column == lanes + (first + 128 * n) for n in range(rows // 128)]
    return jnp.concatenate(parts, axis=1).astype(jnp.float32).astype(jnp.bfloat16)


def gather_kernel(place, index_ref, kept, received, gain_ref, merged):
    rows = kept.shape[0]
    final = normalized(kept[...] + received[...].astype(jnp.float32), gain_ref[...])
    for k in range(4):
        merged[k] = dot(one_hot_rows(index_ref, k, place[2], rows), final, NN).astype(jnp.bfloat16)


def gather(place, index, kept, received, gain):
    rows, width = kept.shape
    merged_rows = index.shape[1]
    whole = lambda a: pl.BlockSpec(a.shape, lambda i, s: (0,) * a.ndim)
    return pl.pallas_call(
        gather_kernel,
        grid_spec=pltpu.PrefetchScalarGridSpec(
            num_scalar_prefetch=1,
            grid=(1,),
            in_specs=[whole(index), whole(kept), whole(received), whole(gain)],
            out_specs=pl.BlockSpec((4, merged_rows, width), lambda i, s: (0, 0, 0)),
        ),
        out_shape=jax.ShapeDtypeStruct((4, merged_rows, width), jnp.bfloat16),
        compiler_params=vmem(32),
        cost_estimate=pl.CostEstimate(
            flops=1_000_000_000, bytes_accessed=5_000_000, transcendentals=0
        ),
        name="gather",
    )(place, index, kept, received, gain)


def merge_kernel(place, index_ref, kept, received, gain_ref, earlier, w_own, w_other, own, other):
    rows = kept.shape[0]
    width = kept.shape[1]
    final = normalized(kept[...] + received[...].astype(jnp.float32), gain_ref[...])
    own[...] = jnp.zeros_like(own)
    other[...] = jnp.zeros_like(other)
    for k in range(4):
        part = dot(one_hot_rows(index_ref, k, place[3], rows), final, NN)
        part = (part + earlier[k].astype(jnp.float32)).astype(jnp.bfloat16)
        own[...] += dot(part, w_own[:, k * width : (k + 1) * width], NT)
        other[...] += dot(part, w_other[:, k * width : (k + 1) * width], NT)


def merge(place, index, kept, received, gain, earlier, w_own, w_other):
    merged_rows = index.shape[1]
    columns = w_own.shape[0]
    whole = lambda a: pl.BlockSpec(a.shape, lambda i, s: (0,) * a.ndim)
    out_spec = pl.BlockSpec((merged_rows, columns), lambda i, s: (0, 0))
    operands = [index, kept, received, gain, earlier, w_own, w_other]
    return pl.pallas_call(
        merge_kernel,
        grid_spec=pltpu.PrefetchScalarGridSpec(
            num_scalar_prefetch=1,
            grid=(1,),
            in_specs=[whole(a) for a in operands],
            out_specs=[out_spec, out_spec],
        ),
        out_shape=[jax.ShapeDtypeStruct((merged_rows, columns), jnp.float32)] * 2,
        compiler_params=vmem(40),
        cost_estimate=pl.CostEstimate(
            flops=3_000_000_000, bytes_accessed=12_000_000, transcendentals=0
        ),
        name="merge",
    )(place, *operands)


def place_kernel(position, own, received, out):
    feature = (own[...] + received[...]).astype(jnp.bfloat16)
    slots = lax.broadcasted_iota(jnp.int32, (out.shape[0], 1), 0)
    chosen = (slots == position[...]).astype(jnp.float32).astype(jnp.bfloat16)
    out[...] = dot(chosen, feature, NN).astype(jnp.bfloat16)


def body(
    tokens,
    segments,
    attend_gain,
    attend_weight,
    output_weight,
    mixer_gain,
    expand_weight,
    reduce_weight,
    output_gain,
    merge_weight,
    merge_index,
    owners,
):
    rows, width = tokens.shape
    head_width = attend_weight.shape[2]
    half = head_width // 2
    peers = lax.axis_size("req")
    req = lax.axis_index("req")
    par = req % 2
    core = lax.axis_index("tp") % 2

    with jax.named_scope("project"):
        weight = jnp.transpose(attend_weight, (1, 2, 0)).reshape(3, 2, half, width)
        kv_own, kv_send, q_own, q_send = project(
            par.reshape(1), tokens, attend_gain.astype(jnp.float32)[None, :], weight
        )

    with jax.named_scope("exchange_keys"):
        kv_peer = swap(kv_send, "req", 1)
        kv_before = shifted(kv_own, "req", 2)
        kv_after = shifted(kv_own, "req", -2)
        q_peer = swap(q_send, "req", 1)
        kv_before_peer = shifted(kv_peer, "req", 2)
        kv_after_peer = shifted(kv_peer, "req", -2)

    with jax.named_scope("segments"):
        every = lax.all_gather(segments, "req", axis=0, tiled=True)
        every = jnp.pad(every, (2 * rows, 2 * rows), constant_values=-1)
        window = lax.dynamic_slice_in_dim(every, (req - par) * rows, 6 * rows, 0)
        window = window.reshape(3, 2, rows)
        window = jnp.where(par == 0, window, window[:, ::-1])
        key_rows = jnp.concatenate([window[1], window[0], window[2]], axis=0)
        tiles = window[1].reshape(2, rows // TILE, TILE)
        tiles = jnp.where(core == 0, tiles, tiles[:, ::-1]).reshape(4, TILE)
        key_tiles = key_rows.reshape(-1, TILE)
        meta = jnp.concatenate(
            [
                jnp.stack([par, core]),
                tiles[:, :: TILE - 1].reshape(-1),
                key_tiles[:, :: TILE - 1].reshape(-1),
            ]
        )
        q_segment = tiles.astype(jnp.float32)[:, None, :]
        key_rows = key_rows.astype(jnp.float32)

    with jax.named_scope("weights"):
        wo = [output_weight.reshape(2, half, width)]
        wo.append(swap(wo[0], "tp", 1))
        wo.append(swap(wo[0], "tp", 2))
        wo.append(swap(wo[2], "tp", 1))
        expand_other = swap(expand_weight, "tp", 1)
        reduce_other = swap(reduce_weight, "tp", 1)
        merge_own = jnp.transpose(merge_weight)
        merge_other = swap(merge_own, "tp", 1)

    with jax.named_scope("attention"):
        state = attend(meta, q_own, q_peer, [kv_own, kv_peer], q_segment, key_rows[:2], 0)
        context = attend(
            meta,
            q_own,
            q_peer,
            [kv_before, kv_before_peer, kv_after, kv_after_peer],
            q_segment,
            key_rows[2:],
            2,
            state,
        )

    with jax.named_scope("exchange_context"):
        from_peer = swap(context[2:], "req", 1)
        pieces = []
        for source in (context, from_peer):
            pieces.append(
                [
                    source[0],
                    swap(source[1], "tp", 1),
                    swap(source[0], "tp", 2),
                    swap(source[1], "tp", 3),
                ]
            )
        pieces = [pieces[h][t] for t in range(4) for h in range(2)]

    chunk_rows = 256
    per_core = rows // 2
    place = jnp.stack([par, core, core * per_core, core * per_core + chunk_rows])
    with jax.named_scope("mixer"):
        gain = mixer_gain.astype(jnp.float32)[None, :]
        weights = [expand_weight, expand_other, reduce_weight, reduce_other]
        sent, kept, received = [], [], []
        for chunk in range(2):
            s, k = mixer(place, pieces, tokens, gain, wo, weights, chunk, chunk_rows)
            kept.append(k)
            received.append(swap(s, "tp", 2))

    with jax.named_scope("merge"):
        index = jnp.transpose(merge_index) - req * rows
        gain = output_gain.astype(jnp.float32)[None, :]
        earlier = gather(place, index, kept[0], received[0], gain)
        own, other = merge(
            place, index, kept[1], received[1], gain, earlier, merge_own, merge_other
        )
        other = swap(other, "tp", 1)

    with jax.named_scope("place"):
        capacity = 2 * merge_index.shape[0] // peers
        target = owners[:, 0]
        choose = (target[:, None] == jnp.arange(peers, dtype=jnp.int32)[None, :]).astype(jnp.int32)
        slot = jnp.sum((jnp.cumsum(choose, axis=0) - 1) * choose, axis=1)
        position = (target * capacity + slot)[None, :]
        columns = own.shape[1]
        outgoing = pl.pallas_call(
            place_kernel,
            out_shape=jax.ShapeDtypeStruct((peers * capacity, columns), jnp.bfloat16),
            name="place",
        )(position, own, other)
        outgoing = outgoing.reshape(peers, capacity, columns)
        arrived = lax.all_to_all(outgoing, "req", split_axis=0, concat_axis=0, tiled=True)
    return arrived.reshape(1, peers, capacity, columns)


def solution(mesh):
    placed = (
        P("req", None),
        P("req"),
        P(),
        P(None, None, "tp"),
        P("tp", None),
        P(),
        P(None, "tp"),
        P("tp", None),
        P(),
        P(None, "tp"),
        P("req", None),
        P("req", None),
    )
    return jax.shard_map(
        body, mesh=mesh, in_specs=placed, out_specs=P("req", None, None, "tp"), check_vma=False
    )
```

```python
import functools
import math

import jax
import jax.numpy as jnp
from jax import lax
from jax.experimental import pallas as pl
from jax.experimental.pallas import tpu as pltpu
from jax.sharding import PartitionSpec as P

HD = 80
TILE = 512
MASKED = -1e30
START = -1e28
FACTOR = 1.0 / math.sqrt(HD)
SEGMENT_ROWS = 16
VROWS = 96


def swap(block, axis, flip):
    return lax.ppermute(block, axis, [(i, i ^ flip) for i in range(lax.axis_size(axis))])


def shifted(block, axis, distance):
    devices = range(lax.axis_size(axis))
    route = [(i - distance, i) for i in devices if i - distance in devices]
    return lax.ppermute(block, axis, route)


def normalized(stream, gain):
    center = jnp.mean(stream, axis=-1, keepdims=True)
    moved = stream - center
    spread = jnp.mean(moved * moved, axis=-1, keepdims=True)
    return (moved * lax.rsqrt(spread + 1e-06) * gain).astype(jnp.bfloat16)


def dot(a, b, contract):
    return lax.dot_general(a, b, (contract, ((), ())), preferred_element_type=jnp.float32)


NN = ((1,), (0,))
NT = ((1,), (1,))


def vmem():
    return pltpu.CompilerParams(vmem_limit_bytes=60 << 20)


def project_kernel(par_ref, x_ref, segment_ref, gain_ref, w_ref, kv_keep, kv_send, q_keep, q_send):
    par = par_ref[0]
    half = w_ref.shape[2]
    rows = normalized(x_ref[...].astype(jnp.float32), gain_ref[...])
    number = segment_ref[...] + 1
    row = lax.broadcasted_iota(jnp.int32, (SEGMENT_ROWS, 1), 0)
    number = jnp.where(row == 0, number & 255, jnp.where(row == 1, number >> 8, 0))
    number = number.astype(jnp.float32).astype(jnp.bfloat16)
    for which, kv, q in ((par, kv_keep, q_keep), (1 - par, kv_send, q_send)):
        for part in (1, 2):
            out = dot(w_ref[part, which], rows, NT).astype(jnp.bfloat16)
            kv[(part - 1) * half : part * half, :] = out
        kv[2 * half :, :] = number
        q[...] = dot(w_ref[0, which], rows, NT).astype(jnp.bfloat16)


def project(par, tokens, segments, gain, weight):
    rows, width = tokens.shape
    half = weight.shape[2]
    step = 256
    tall = 2 * half + SEGMENT_ROWS
    shapes = [(tall, rows), (tall, rows), (half, rows), (half, rows)]
    return pl.pallas_call(
        project_kernel,
        grid_spec=pltpu.PrefetchScalarGridSpec(
            num_scalar_prefetch=1,
            grid=(rows // step,),
            in_specs=[
                pl.BlockSpec((step, width), lambda i, s: (i, 0)),
                pl.BlockSpec((1, step), lambda i, s: (0, i)),
                pl.BlockSpec((1, width), lambda i, s: (0, 0)),
                pl.BlockSpec(weight.shape, lambda i, s: (0, 0, 0, 0)),
            ],
            out_specs=[pl.BlockSpec((s[0], step), lambda i, s: (0, i)) for s in shapes],
        ),
        out_shape=[jax.ShapeDtypeStruct(s, jnp.bfloat16) for s in shapes],
        compiler_params=vmem(),
        name="project",
    )(par, tokens, segments, gain, weight)


def numbers_of(ref, at):
    two = ref[:, at].astype(jnp.float32)
    return two[0:1] + 256.0 * two[1:2]


def attend_kernel(blocks, fresh, skip, last, place, *refs):
    q_refs, number_refs, refs = refs[:2], refs[2:4], refs[4:]
    kv_refs, refs = refs[:blocks], refs[blocks:]
    if fresh:
        acc_in, peak_in, refs = refs[0], refs[1], refs[2:]
    if last:
        ctx_out, refs = refs[0], refs[1:]
    else:
        acc_out, peak_out, refs = refs[0], refs[1], refs[2:]
    keys, values, columns, acc, peak, bounds = refs
    tiles_of = kv_refs[0].shape[1] // TILE
    tiles = blocks * tiles_of
    tall = kv_refs[0].shape[0] - SEGMENT_ROWS
    j = pl.program_id(0)

    @pl.when(j == 0)
    def _():
        for b in range(blocks):
            for t in range(tiles_of):
                n = b * tiles_of + t
                at = slice(t * TILE, (t + 1) * TILE)
                for h in range(2):
                    block = kv_refs[b][h * HD : (h + 1) * HD, at].astype(jnp.float32)
                    keys[n, h] = jnp.transpose(block).astype(jnp.bfloat16)
                    values[n, h, :HD] = kv_refs[b][(2 + h) * HD : (3 + h) * HD, at]
                    values[n, h, HD:] = jnp.ones((VROWS - HD, TILE), jnp.bfloat16)
                number = numbers_of(kv_refs[b].at[tall:], at)
                bounds[2 * n] = jnp.min(number)
                bounds[2 * n + 1] = jnp.max(number)
                columns[n] = jnp.transpose(jnp.broadcast_to(number, (128, TILE)))

    def start():
        acc[...] = jnp.zeros_like(acc)
        peak[...] = jnp.full_like(peak, START)

    def go_on():
        acc[...] = acc_in[0]
        peak[...] = peak_in[0]

    if fresh:
        pl.when(j < fresh)(go_on)
        pl.when(j >= fresh)(start)
    else:
        start()

    queries = jnp.where(j < 2, q_refs[0][...], q_refs[1][...])
    whole_tile = slice(0, TILE)
    q_row = jnp.where(
        j < 2, numbers_of(number_refs[0], whole_tile), numbers_of(number_refs[1], whole_tile)
    )
    q_low, q_high = jnp.min(q_row), jnp.max(q_row)

    def update(t, masked):
        if masked:
            column = columns[t]
            matches = jnp.concatenate([column] * (TILE // 128), axis=1) == q_row
        scores = [dot(keys[t, h], queries[h * HD : (h + 1) * HD, :], NN) for h in range(2)]
        for h in range(2):
            here = scores[h]
            if masked:
                here = jnp.where(matches, here, MASKED)
            old = peak[h : h + 1, :]
            new = jnp.maximum(old, jnp.max(here, axis=0, keepdims=True))
            probs = jnp.exp((here - new) * FACTOR)
            shrink = jnp.exp((old - new) * FACTOR)
            peak[h : h + 1, :] = new
            acc[h] = acc[h] * shrink + dot(values[t, h], probs.astype(jnp.bfloat16), NN)

    def visit(t, carry):
        k_low, k_high = bounds[2 * t], bounds[2 * t + 1]
        touches = (k_high >= q_low) & (k_low <= q_high)
        whole = (k_low == k_high) & (q_low == q_high)

        @pl.when(touches & whole)
        def _():
            update(t, False)

        @pl.when(touches & jnp.logical_not(whole))
        def _():
            update(t, True)

        return carry

    lax.fori_loop(jnp.where(j < fresh, skip, 0), tiles, visit, 0)
    if last:
        for h in range(2):
            at = slice(h * HD, (h + 1) * HD)
            ctx_out[0, at, :] = (acc[h, :HD] / acc[h, HD : HD + 1]).astype(jnp.bfloat16)
    else:
        acc_out[0] = acc[...]
        peak_out[0] = peak[...]


def attend(place, queries, numbers, key_values, name, state=None, skip=0, last=False):
    half, rows = queries[0].shape
    steps = 2 * len(queries)
    blocks = len(key_values)
    tiles = blocks * rows // TILE
    tall = key_values[0].shape[0] - SEGMENT_ROWS
    fresh = 0 if state is None else state[0].shape[0]
    queries = [queries[0], queries[-1]]
    numbers = [numbers[0], numbers[-1]]
    q_spec = pl.BlockSpec((half, TILE), lambda j, s: (0, (j % 2) ^ s[1]))
    n_spec = pl.BlockSpec((SEGMENT_ROWS, TILE), lambda j, s: (tall // SEGMENT_ROWS, (j % 2) ^ s[1]))
    whole = lambda a: pl.BlockSpec(a.shape, lambda j, s: (0,) * a.ndim)
    acc_shape, peak_shape = (2, VROWS, TILE), (2, TILE)
    in_specs = [q_spec, q_spec, n_spec, n_spec] + [whole(kv) for kv in key_values]
    operands = [*queries, *numbers, *key_values]
    if state is not None:
        in_specs += [
            pl.BlockSpec((1,) + acc_shape, lambda j, s: (jnp.minimum(j, fresh - 1), 0, 0, 0)),
            pl.BlockSpec((1,) + peak_shape, lambda j, s: (jnp.minimum(j, fresh - 1), 0, 0)),
        ]
        operands += list(state)
    if last:
        out_specs = pl.BlockSpec((1, half, TILE), lambda j, s: (j, 0, 0))
        out_shape = jax.ShapeDtypeStruct((steps, half, TILE), jnp.bfloat16)
    else:
        out_specs = [
            pl.BlockSpec((1,) + acc_shape, lambda j, s: (j, 0, 0, 0)),
            pl.BlockSpec((1,) + peak_shape, lambda j, s: (j, 0, 0)),
        ]
        out_shape = [
            jax.ShapeDtypeStruct((steps,) + acc_shape, jnp.float32),
            jax.ShapeDtypeStruct((steps,) + peak_shape, jnp.float32),
        ]
    return pl.pallas_call(
        functools.partial(attend_kernel, blocks, fresh, skip, last),
        grid_spec=pltpu.PrefetchScalarGridSpec(
            num_scalar_prefetch=1,
            grid=(steps,),
            in_specs=in_specs,
            out_specs=out_specs,
            scratch_shapes=[
                pltpu.VMEM((tiles, 2, TILE, HD), jnp.bfloat16),
                pltpu.VMEM((tiles, 2, VROWS, TILE), jnp.bfloat16),
                pltpu.VMEM((tiles, TILE, 128), jnp.float32),
                pltpu.VMEM(acc_shape, jnp.float32),
                pltpu.VMEM(peak_shape, jnp.float32),
                pltpu.SMEM((2 * tiles,), jnp.float32),
            ],
        ),
        out_shape=out_shape,
        compiler_params=vmem(),
        cost_estimate=pl.CostEstimate(
            flops=1_000_000_000 * steps * blocks // 2, bytes_accessed=4_000_000, transcendentals=0
        ),
        name=name,
    )(place, *operands)


def mixer_kernel(place, *refs):
    pieces, refs = refs[:8], refs[8:]
    x_ref, gain_ref, refs = refs[0], refs[1], refs[2:]
    wo_hbm, refs = refs[:4], refs[4:]
    (we_own, we_other, wr_own, wr_other, sent, kept, refs) = (*refs[:6], refs[6:])
    context, wo, we, wr, sems = refs
    par = place[0]
    half = pieces[0].shape[0]
    copies = []
    for t in range(4):
        copies.append(pltpu.make_async_copy(wo_hbm[t], wo.at[t], sems.at[t]))
    copies.append(pltpu.make_async_copy(we_own, we.at[0], sems.at[4]))
    copies.append(pltpu.make_async_copy(we_other, we.at[1], sems.at[5]))
    copies.append(pltpu.make_async_copy(wr_own, wr.at[0], sems.at[6]))
    copies.append(pltpu.make_async_copy(wr_other, wr.at[1], sems.at[7]))
    for copy in copies:
        copy.start()
    total = x_ref[...].astype(jnp.float32)
    for t in range(4):
        copies[t].wait()
        for h in range(2):
            piece = jnp.transpose(pieces[2 * t + h][...].astype(jnp.float32))
            total += dot(piece.astype(jnp.bfloat16), wo[t, par ^ h], NN)
    rows = normalized(total, gain_ref[...])
    for s in range(2):
        copies[4 + s].wait()
        copies[6 + s].wait()
        hidden = we.shape[2]
        step = 256
        for n in range(hidden // step):
            at = slice(n * step, (n + 1) * step)
            inner = dot(rows, we[s, :, at], NN)
            grown = 0.5 * inner * (1.0 + lax.erf(inner * (1.0 / math.sqrt(2.0))))
            context[:, s * hidden + n * step : s * hidden + (n + 1) * step] = grown.astype(
                jnp.bfloat16
            )
    hidden = we.shape[2]
    out = dot(context[:, :hidden], wr[0], NN) + dot(context[:, hidden:], wr[1], NN)
    sent[...] = out.astype(jnp.bfloat16)
    kept[...] = total + out


def mixer(place, pieces, tokens, gain, wo, weights, chunk, chunk_rows):
    half = pieces[0].shape[0]
    width = tokens.shape[1]
    per_core = pieces[0].shape[1]
    chunks = per_core // chunk_rows
    hidden = weights[0].shape[1]
    piece_spec = pl.BlockSpec((half, chunk_rows), lambda i, s: (0, chunk))
    any_spec = pl.BlockSpec(memory_space=pl.ANY)
    out_spec = pl.BlockSpec((chunk_rows, width), lambda i, s: (0, 0))
    return pl.pallas_call(
        mixer_kernel,
        grid_spec=pltpu.PrefetchScalarGridSpec(
            num_scalar_prefetch=1,
            grid=(1,),
            in_specs=[piece_spec] * 8
            + [
                pl.BlockSpec((chunk_rows, width), lambda i, s: (s[1] * chunks + chunk, 0)),
                pl.BlockSpec((1, width), lambda i, s: (0, 0)),
            ]
            + [any_spec] * 8,
            out_specs=[out_spec, out_spec],
            scratch_shapes=[
                pltpu.VMEM((chunk_rows, 2 * hidden), jnp.bfloat16),
                pltpu.VMEM((4,) + wo[0].shape, jnp.bfloat16),
                pltpu.VMEM((2,) + weights[0].shape, jnp.bfloat16),
                pltpu.VMEM((2,) + weights[2].shape, jnp.bfloat16),
                pltpu.SemaphoreType.DMA((8,)),
            ],
        ),
        out_shape=[
            jax.ShapeDtypeStruct((chunk_rows, width), jnp.bfloat16),
            jax.ShapeDtypeStruct((chunk_rows, width), jnp.float32),
        ],
        compiler_params=vmem(),
        cost_estimate=pl.CostEstimate(
            flops=5_000_000_000, bytes_accessed=20_000_000, transcendentals=0
        ),
        name="mixer",
    )(place, *pieces, tokens, gain, *wo, *weights)


def one_hot_rows(index_ref, k, first, rows):
    column = jnp.transpose(jnp.broadcast_to(index_ref[k : k + 1, :], (128, index_ref.shape[1])))
    lanes = lax.broadcasted_iota(jnp.int32, (1, 128), 1)
    parts = [column == lanes + (first + 128 * n) for n in range(rows // 128)]
    return jnp.concatenate(parts, axis=1).astype(jnp.float32).astype(jnp.bfloat16)


def gather_kernel(place, index_ref, kept, received, gain_ref, merged):
    rows = kept.shape[0]
    final = normalized(kept[...] + received[...].astype(jnp.float32), gain_ref[...])
    for k in range(4):
        merged[k] = dot(one_hot_rows(index_ref, k, place[2], rows), final, NN).astype(jnp.bfloat16)


def gather(place, index, kept, received, gain):
    rows, width = kept.shape
    merged_rows = index.shape[1]
    whole = lambda a: pl.BlockSpec(a.shape, lambda i, s: (0,) * a.ndim)
    return pl.pallas_call(
        gather_kernel,
        grid_spec=pltpu.PrefetchScalarGridSpec(
            num_scalar_prefetch=1,
            grid=(1,),
            in_specs=[whole(index), whole(kept), whole(received), whole(gain)],
            out_specs=pl.BlockSpec((4, merged_rows, width), lambda i, s: (0, 0, 0)),
        ),
        out_shape=jax.ShapeDtypeStruct((4, merged_rows, width), jnp.bfloat16),
        compiler_params=vmem(),
        cost_estimate=pl.CostEstimate(
            flops=1_000_000_000, bytes_accessed=5_000_000, transcendentals=0
        ),
        name="gather",
    )(place, index, kept, received, gain)


def merge_kernel(place, index_ref, kept, received, gain_ref, earlier, w_own, w_other, own, other):
    rows = kept.shape[0]
    width = kept.shape[1]
    final = normalized(kept[...] + received[...].astype(jnp.float32), gain_ref[...])
    own[...] = jnp.zeros_like(own)
    other[...] = jnp.zeros_like(other)
    for k in range(4):
        part = dot(one_hot_rows(index_ref, k, place[3], rows), final, NN)
        part = (part + earlier[k].astype(jnp.float32)).astype(jnp.bfloat16)
        own[...] += dot(part, w_own[:, k * width : (k + 1) * width], NT)
        other[...] += dot(part, w_other[:, k * width : (k + 1) * width], NT)


def merge(place, index, kept, received, gain, earlier, w_own, w_other):
    merged_rows = index.shape[1]
    columns = w_own.shape[0]
    whole = lambda a: pl.BlockSpec(a.shape, lambda i, s: (0,) * a.ndim)
    out_spec = pl.BlockSpec((merged_rows, columns), lambda i, s: (0, 0))
    operands = [index, kept, received, gain, earlier, w_own, w_other]
    return pl.pallas_call(
        merge_kernel,
        grid_spec=pltpu.PrefetchScalarGridSpec(
            num_scalar_prefetch=1,
            grid=(1,),
            in_specs=[whole(a) for a in operands],
            out_specs=[out_spec, out_spec],
        ),
        out_shape=[jax.ShapeDtypeStruct((merged_rows, columns), jnp.float32)] * 2,
        compiler_params=vmem(),
        cost_estimate=pl.CostEstimate(
            flops=3_000_000_000, bytes_accessed=12_000_000, transcendentals=0
        ),
        name="merge",
    )(place, *operands)


def place_kernel(position, own, received, out):
    feature = (own[...] + received[...]).astype(jnp.bfloat16)
    slots = lax.broadcasted_iota(jnp.int32, (out.shape[0], 1), 0)
    chosen = (slots == position[...]).astype(jnp.float32).astype(jnp.bfloat16)
    out[...] = dot(chosen, feature, NN).astype(jnp.bfloat16)


def body(
    tokens,
    segments,
    attend_gain,
    attend_weight,
    output_weight,
    mixer_gain,
    expand_weight,
    reduce_weight,
    output_gain,
    merge_weight,
    merge_index,
    owners,
):
    rows, width = tokens.shape
    head_width = attend_weight.shape[2]
    half = head_width // 2
    peers = lax.axis_size("req")
    req = lax.axis_index("req")
    par = req % 2
    core = lax.axis_index("tp") % 2

    place = jnp.stack([par, core])
    with jax.named_scope("project"):
        weight = jnp.transpose(attend_weight, (1, 2, 0)).reshape(3, 2, half, width)
        kv_own, kv_send, q_own, q_send = project(
            place, tokens, segments[None, :], attend_gain.astype(jnp.float32)[None, :], weight
        )

    with jax.named_scope("exchange_keys"):
        kv_peer = swap(kv_send, "req", 1)
        kv_before = shifted(kv_own, "req", 2)
        kv_after = shifted(kv_own, "req", -2)
        q_send, kv_peer = lax.optimization_barrier((q_send, kv_peer))
        kv_before_peer = shifted(kv_peer, "req", 2)
        kv_after_peer = shifted(kv_peer, "req", -2)
        q_peer = swap(q_send, "req", 1)

    with jax.named_scope("weights"):
        wo = [output_weight.reshape(2, half, width)]
        wo.append(swap(wo[0], "tp", 1))
        wo.append(swap(wo[0], "tp", 2))
        wo.append(swap(wo[2], "tp", 1))
        expand_other = swap(expand_weight, "tp", 1)
        reduce_other = swap(reduce_weight, "tp", 1)
        merge_own = jnp.transpose(merge_weight)
        merge_other = swap(merge_own, "tp", 1)

    with jax.named_scope("attention"):
        numbers = [kv_own, kv_peer]
        state = attend(place, [q_own], [kv_own], [kv_own], "attend_own")
        state = attend(
            place,
            [q_own, q_peer],
            numbers,
            [kv_own, kv_peer, kv_before, kv_after],
            "attend_near",
            state,
            skip=rows // TILE,
        )
        context = attend(
            place,
            [q_own, q_peer],
            numbers,
            [kv_before_peer, kv_after_peer],
            "attend_far",
            state,
            last=True,
        )

    with jax.named_scope("exchange_context"):
        from_peer = swap(context[2:], "req", 1)
        pieces = []
        for source in (context, from_peer):
            pieces.append(
                [
                    source[0],
                    swap(source[1], "tp", 1),
                    swap(source[0], "tp", 2),
                    swap(source[1], "tp", 3),
                ]
            )
        pieces = [pieces[h][t] for t in range(4) for h in range(2)]

    chunk_rows = 256
    per_core = rows // 2
    place = jnp.stack([par, core, core * per_core, core * per_core + chunk_rows])
    with jax.named_scope("mixer"):
        gain = mixer_gain.astype(jnp.float32)[None, :]
        weights = [expand_weight, expand_other, reduce_weight, reduce_other]
        sent, kept, received = [], [], []
        for chunk in range(2):
            s, k = mixer(place, pieces, tokens, gain, wo, weights, chunk, chunk_rows)
            kept.append(k)
            received.append(swap(s, "tp", 2))

    with jax.named_scope("merge"):
        index = jnp.transpose(merge_index) - req * rows
        gain = output_gain.astype(jnp.float32)[None, :]
        earlier = gather(place, index, kept[0], received[0], gain)
        own, other = merge(
            place, index, kept[1], received[1], gain, earlier, merge_own, merge_other
        )
        other = swap(other, "tp", 1)

    with jax.named_scope("place"):
        capacity = 2 * merge_index.shape[0] // peers
        target = owners[:, 0]
        choose = (target[:, None] == jnp.arange(peers, dtype=jnp.int32)[None, :]).astype(jnp.int32)
        slot = jnp.sum((jnp.cumsum(choose, axis=0) - 1) * choose, axis=1)
        position = (target * capacity + slot)[None, :]
        columns = own.shape[1]
        outgoing = pl.pallas_call(
            place_kernel,
            out_shape=jax.ShapeDtypeStruct((peers * capacity, columns), jnp.bfloat16),
            name="place",
        )(position, own, other)
        outgoing = outgoing.reshape(peers, capacity, columns)
        arrived = lax.all_to_all(outgoing, "req", split_axis=0, concat_axis=0, tiled=True)
    return arrived.reshape(1, peers, capacity, columns)


def solution(mesh):
    placed = (
        P("req", None),
        P("req"),
        P(),
        P(None, None, "tp"),
        P("tp", None),
        P(),
        P(None, "tp"),
        P("tp", None),
        P(),
        P(None, "tp"),
        P("req", None),
        P("req", None),
    )
    return jax.shard_map(
        body, mesh=mesh, in_specs=placed, out_specs=P("req", None, None, "tp"), check_vma=False
    )
```

```python
import functools
import math

import jax
import jax.numpy as jnp
from jax import lax
from jax.experimental import pallas as pl
from jax.experimental.pallas import tpu as pltpu
from jax.sharding import PartitionSpec as P

HD = 80
TILE = 512
MASKED = -1e30
START = -1e28
FACTOR = 1.0 / math.sqrt(HD)
SEGMENT_ROWS = 16
VROWS = 96
LANES = 256
AHEAD = 2
SMALL = 60.0


def swap(block, axis, flip):
    return lax.ppermute(block, axis, [(i, i ^ flip) for i in range(lax.axis_size(axis))])


def shifted(block, axis, distance):
    devices = range(lax.axis_size(axis))
    route = [(i - distance, i) for i in devices if i - distance in devices]
    return lax.ppermute(block, axis, route)


def normalized(stream, gain):
    center = jnp.mean(stream, axis=-1, keepdims=True)
    moved = stream - center
    spread = jnp.mean(moved * moved, axis=-1, keepdims=True)
    return (moved * lax.rsqrt(spread + 1e-06) * gain).astype(jnp.bfloat16)


def dot(a, b, contract):
    return lax.dot_general(a, b, (contract, ((), ())), preferred_element_type=jnp.float32)


NN = ((1,), (0,))
NT = ((1,), (1,))


def row_of(gain_ref):
    return gain_ref[...].astype(jnp.float32).reshape(1, gain_ref.shape[0])


def vmem():
    return pltpu.CompilerParams(vmem_limit_bytes=60 << 20)


def project_kernel(x_ref, segment_ref, gain_ref, w_ref, kv_keep, kv_send, q_keep, q_send):
    first = lax.axis_index("req") % 2 == 0
    half = q_keep.shape[0]
    rows = normalized(x_ref[...].astype(jnp.float32), row_of(gain_ref))
    number = segment_ref[...] + 1
    row = lax.broadcasted_iota(jnp.int32, (SEGMENT_ROWS, 1), 0)
    number = jnp.where(row == 0, number & 255, jnp.where(row == 1, number >> 8, 0))
    number = number.astype(jnp.float32).astype(jnp.bfloat16)
    out = dot(w_ref[...], rows, NT)
    for part, keep, send in ((0, q_keep, q_send), (1, kv_keep, kv_send), (2, kv_keep, kv_send)):
        low = out[2 * part * half : (2 * part + 1) * half]
        high = out[(2 * part + 1) * half : (2 * part + 2) * half]
        at = slice(max(part - 1, 0) * half, max(part, 1) * half)
        keep[at, :] = jnp.where(first, low, high).astype(jnp.bfloat16)
        send[at, :] = jnp.where(first, high, low).astype(jnp.bfloat16)
    kv_keep[2 * half :, :] = number
    kv_send[2 * half :, :] = number


def project(tokens, segments, gain, weight):
    rows, width = tokens.shape
    half = weight.shape[0] // 6
    step = 256
    tall = 2 * half + SEGMENT_ROWS
    shapes = [(tall, rows), (tall, rows), (half, rows), (half, rows)]
    return pl.pallas_call(
        project_kernel,
        grid=(rows // step,),
        in_specs=[
            pl.BlockSpec((step, width), lambda i: (i, 0)),
            pl.BlockSpec((1, step), lambda i: (0, i)),
            pl.BlockSpec(gain.shape, lambda i: (0,)),
            pl.BlockSpec(weight.shape, lambda i: (0, 0)),
        ],
        out_specs=[pl.BlockSpec((s[0], step), lambda i: (0, i)) for s in shapes],
        out_shape=[jax.ShapeDtypeStruct(s, jnp.bfloat16) for s in shapes],
        compiler_params=vmem(),
        name="project",
    )(tokens, segments, gain, weight)


def numbers_of(ref, at):
    two = ref[:, at].astype(jnp.float32)
    return two[0:1] + 256.0 * two[1:2]


def largest_norm(first, second):
    squares = []
    for block in (first, second):
        block = block.astype(jnp.float32)
        squares.append(jnp.sum(block * block, axis=0, keepdims=True))
    return jnp.max(jnp.maximum(squares[0], squares[1]))


def attend_kernel(blocks, resumed, last, place, q_ref, number_ref, *refs):
    kv_refs, refs = refs[:blocks], refs[blocks:]
    if resumed:
        acc_in, peak_in, refs = refs[0], refs[1], refs[2:]
    if last:
        ctx_out, refs = refs[0], refs[1:]
    else:
        acc_out, peak_out, refs = refs[0], refs[1], refs[2:]
    keys, values, columns, acc, peak, bounds, plain = refs
    tiles_of = kv_refs[0].shape[1] // TILE
    tiles = blocks * tiles_of
    tall = kv_refs[0].shape[0] - SEGMENT_ROWS

    @pl.when(pl.program_id(0) == 0)
    def _():
        for b in range(blocks):
            for t in range(tiles_of):
                n = b * tiles_of + t
                at = slice(t * TILE, (t + 1) * TILE)
                for h in range(2):
                    block = kv_refs[b][h * HD : (h + 1) * HD, at].astype(jnp.float32)
                    keys[n, h] = jnp.transpose(block).astype(jnp.bfloat16)
                    values[n, h, :HD] = kv_refs[b][(2 + h) * HD : (3 + h) * HD, at]
                    values[n, h, HD:] = jnp.ones((VROWS - HD, TILE), jnp.bfloat16)
                number = numbers_of(kv_refs[b].at[tall:], at)
                bounds[3 * n] = jnp.min(number)
                bounds[3 * n + 1] = jnp.max(number)
                bounds[3 * n + 2] = largest_norm(kv_refs[b][:HD, at], kv_refs[b][HD : 2 * HD, at])
                columns[n] = jnp.transpose(jnp.broadcast_to(number, (128, TILE)))

    if resumed:
        acc[...] = acc_in[0]
        peak[...] = peak_in[0]
        plain[0] = (jnp.max(jnp.abs(peak_in[0])) == 0.0).astype(jnp.int32)
    else:
        acc[...] = jnp.zeros_like(acc)
        peak[...] = jnp.zeros_like(peak)
        plain[0] = 1

    q_row = numbers_of(number_ref, slice(0, TILE))
    q_low, q_high = jnp.min(q_row), jnp.max(q_row)
    q_norm = largest_norm(q_ref[:HD, :], q_ref[HD:, :])

    def scores_of(t, h, at, matches):
        scores = dot(keys[t, h], q_ref[h * HD : (h + 1) * HD, at], NN)
        return scores if matches is None else jnp.where(matches, scores, MASKED)

    def matches_of(t, at):
        column = columns[t]
        return jnp.concatenate([column] * (LANES // 128), axis=1) == q_row[:, at]

    units = [(slice(c, c + LANES), h) for c in range(0, TILE, LANES) for h in range(2)]

    def unshifted(t, masked):
        scores, probs, matches = {}, {}, None
        for i in range(len(units) + AHEAD + 1):
            if i < len(units):
                at, h = units[i]
                if masked and h == 0:
                    matches = matches_of(t, at)
                scores[i] = scores_of(t, h, at, matches)
            if 0 <= i - AHEAD < len(units):
                probs[i - AHEAD] = jnp.exp(scores.pop(i - AHEAD) * FACTOR).astype(jnp.bfloat16)
            if 0 <= i - AHEAD - 1 < len(units):
                at, h = units[i - AHEAD - 1]
                acc[h, :, at] += dot(values[t, h], probs.pop(i - AHEAD - 1), NN)

    def shifted_by_peak(t):
        for at, h in units:
            scores = scores_of(t, h, at, matches_of(t, at))
            old = jnp.where(acc[h, HD : HD + 1, at] > 0.0, peak[h : h + 1, at], START)
            new = jnp.maximum(old, jnp.max(scores, axis=0, keepdims=True))
            probs = jnp.exp((scores - new) * FACTOR).astype(jnp.bfloat16)
            shrink = jnp.exp((old - new) * FACTOR)
            peak[h : h + 1, at] = new
            acc[h, :, at] = acc[h, :, at] * shrink + dot(values[t, h], probs, NN)
        plain[0] = 0

    def visit(t, carry):
        k_low, k_high = bounds[3 * t], bounds[3 * t + 1]
        touches = (k_high >= q_low) & (k_low <= q_high)
        whole = (k_low == k_high) & (q_low == q_high)
        small = (plain[0] == 1) & (q_norm * bounds[3 * t + 2] <= SMALL * SMALL * HD)

        @pl.when(touches & small & whole)
        def _():
            unshifted(t, False)

        @pl.when(touches & small & jnp.logical_not(whole))
        def _():
            unshifted(t, True)

        @pl.when(touches & jnp.logical_not(small))
        def _():
            shifted_by_peak(t)

        return carry

    lax.fori_loop(0, tiles, visit, 0)
    if last:
        for h in range(2):
            at = slice(h * HD, (h + 1) * HD)
            ctx_out[0, at, :] = (acc[h, :HD] / acc[h, HD : HD + 1]).astype(jnp.bfloat16)
    else:
        acc_out[0] = acc[...]
        peak_out[0] = peak[...]


def attend(place, queries, numbers, key_values, name, state=None, last=False):
    half, rows = queries.shape
    steps = rows // TILE
    blocks = len(key_values)
    tiles = blocks * steps
    tall = numbers.shape[0] - SEGMENT_ROWS
    whole = lambda a: pl.BlockSpec(a.shape, lambda j, s: (0,) * a.ndim)
    acc_shape, peak_shape = (2, VROWS, TILE), (2, TILE)
    acc_spec = pl.BlockSpec((1,) + acc_shape, lambda j, s: (j, 0, 0, 0))
    peak_spec = pl.BlockSpec((1,) + peak_shape, lambda j, s: (j, 0, 0))
    in_specs = [
        pl.BlockSpec((half, TILE), lambda j, s: (0, j ^ s[1])),
        pl.BlockSpec((SEGMENT_ROWS, TILE), lambda j, s: (tall // SEGMENT_ROWS, j ^ s[1])),
    ] + [whole(kv) for kv in key_values]
    operands = [queries, numbers, *key_values]
    if state is not None:
        in_specs += [acc_spec, peak_spec]
        operands += list(state)
    if last:
        out_specs = pl.BlockSpec((1, half, TILE), lambda j, s: (j, 0, 0))
        out_shape = jax.ShapeDtypeStruct((steps, half, TILE), jnp.bfloat16)
    else:
        out_specs = [acc_spec, peak_spec]
        out_shape = [
            jax.ShapeDtypeStruct((steps,) + acc_shape, jnp.float32),
            jax.ShapeDtypeStruct((steps,) + peak_shape, jnp.float32),
        ]
    return pl.pallas_call(
        functools.partial(attend_kernel, blocks, state is not None, last),
        grid_spec=pltpu.PrefetchScalarGridSpec(
            num_scalar_prefetch=1,
            grid=(steps,),
            in_specs=in_specs,
            out_specs=out_specs,
            scratch_shapes=[
                pltpu.VMEM((tiles, 2, TILE, HD), jnp.bfloat16),
                pltpu.VMEM((tiles, 2, VROWS, TILE), jnp.bfloat16),
                pltpu.VMEM((tiles, TILE, 128), jnp.float32),
                pltpu.VMEM(acc_shape, jnp.float32),
                pltpu.VMEM(peak_shape, jnp.float32),
                pltpu.SMEM((3 * tiles,), jnp.float32),
                pltpu.SMEM((1,), jnp.int32),
            ],
        ),
        out_shape=out_shape,
        compiler_params=vmem(),
        cost_estimate=pl.CostEstimate(
            flops=1_000_000_000 * blocks, bytes_accessed=4_000_000, transcendentals=0
        ),
        name=name,
    )(place, *operands)


def mixer_kernel(place, *refs):
    sources, refs = refs[:8], refs[8:]
    x_ref, gain_ref, refs = refs[0], refs[1], refs[2:]
    wo_hbm, refs = refs[:4], refs[4:]
    (we_own, we_other, wr_own, wr_other, sent, kept, refs) = (*refs[:6], refs[6:])
    context, hidden, wo, we, wr, sems = refs
    par = place[0]
    half = sources[0].shape[1]
    width = we.shape[2]
    copies = []
    for i in range(8):
        copies.append(
            pltpu.make_async_copy(
                wo_hbm[i // 2].at[par ^ (i % 2)], wo.at[pl.ds(i * half, half)], sems.at[i]
            )
        )
    for i, (source, target) in enumerate(
        [(we_own, we.at[0]), (we_other, we.at[1]), (wr_own, wr.at[0]), (wr_other, wr.at[1])]
    ):
        copies.append(pltpu.make_async_copy(source, target, sems.at[8 + i]))
    for copy in copies:
        copy.start()
    for i in range(8):
        context[i * half : (i + 1) * half, :] = sources[i][0].astype(jnp.float32)
    rows = jnp.transpose(context[...]).astype(jnp.bfloat16)
    for i in range(8):
        copies[i].wait()
    total = x_ref[...].astype(jnp.float32) + dot(rows, wo[...], NN)
    rows = normalized(total, row_of(gain_ref))
    for i in range(2):
        copies[8 + i].wait()
        inner = dot(rows, we[i], NN)
        grown = 0.5 * inner * (1.0 + lax.erf(inner * (1.0 / math.sqrt(2.0))))
        hidden[:, i * width : (i + 1) * width] = grown.astype(jnp.bfloat16)
    for i in range(2):
        copies[10 + i].wait()
    out = dot(hidden[:, :width], wr[0], NN) + dot(hidden[:, width:], wr[1], NN)
    sent[...] = out.astype(jnp.bfloat16)
    kept[...] = total + out


def mixer(place, pieces, tokens, gain, wo, weights, chunk, chunk_rows):
    width = tokens.shape[1]
    half, per_core = pieces[0][0].shape[1:]
    chunks = per_core // chunk_rows
    hidden = weights[0].shape[1]
    piece_spec = lambda which: pl.BlockSpec((1, half, chunk_rows), lambda i, s: (which, 0, chunk))
    any_spec = pl.BlockSpec(memory_space=pl.ANY)
    out_spec = pl.BlockSpec((chunk_rows, width), lambda i, s: (0, 0))
    return pl.pallas_call(
        mixer_kernel,
        grid_spec=pltpu.PrefetchScalarGridSpec(
            num_scalar_prefetch=1,
            grid=(1,),
            in_specs=[piece_spec(which) for _, which in pieces]
            + [
                pl.BlockSpec((chunk_rows, width), lambda i, s: (s[1] * chunks + chunk, 0)),
                pl.BlockSpec(gain.shape, lambda i, s: (0,)),
            ]
            + [any_spec] * 8,
            out_specs=[out_spec, out_spec],
            scratch_shapes=[
                pltpu.VMEM((8 * half, chunk_rows), jnp.float32),
                pltpu.VMEM((chunk_rows, 2 * hidden), jnp.bfloat16),
                pltpu.VMEM((8 * half, width), jnp.bfloat16),
                pltpu.VMEM((2,) + weights[0].shape, jnp.bfloat16),
                pltpu.VMEM((2,) + weights[2].shape, jnp.bfloat16),
                pltpu.SemaphoreType.DMA((12,)),
            ],
        ),
        out_shape=[
            jax.ShapeDtypeStruct((chunk_rows, width), jnp.bfloat16),
            jax.ShapeDtypeStruct((chunk_rows, width), jnp.float32),
        ],
        compiler_params=vmem(),
        cost_estimate=pl.CostEstimate(
            flops=5_000_000_000, bytes_accessed=20_000_000, transcendentals=0
        ),
        name="mixer",
    )(place, *[source for source, _ in pieces], tokens, gain, *wo, *weights)


def one_hot_rows(index_ref, k, first, rows):
    column = jnp.transpose(jnp.broadcast_to(index_ref[k : k + 1, :], (128, index_ref.shape[1])))
    lanes = lax.broadcasted_iota(jnp.int32, (1, 128), 1)
    parts = [column == lanes + (first + 128 * n) for n in range(rows // 128)]
    return jnp.concatenate(parts, axis=1).astype(jnp.float32).astype(jnp.bfloat16)


def gather_kernel(place, index_ref, kept, received, gain_ref, merged):
    rows = kept.shape[0]
    final = normalized(kept[...] + received[...].astype(jnp.float32), row_of(gain_ref))
    for k in range(4):
        merged[k] = dot(one_hot_rows(index_ref, k, place[2], rows), final, NN).astype(jnp.bfloat16)


def gather(place, index, kept, received, gain):
    rows, width = kept.shape
    merged_rows = index.shape[1]
    whole = lambda a: pl.BlockSpec(a.shape, lambda i, s: (0,) * a.ndim)
    return pl.pallas_call(
        gather_kernel,
        grid_spec=pltpu.PrefetchScalarGridSpec(
            num_scalar_prefetch=1,
            grid=(1,),
            in_specs=[whole(index), whole(kept), whole(received), whole(gain)],
            out_specs=pl.BlockSpec((4, merged_rows, width), lambda i, s: (0, 0, 0)),
        ),
        out_shape=jax.ShapeDtypeStruct((4, merged_rows, width), jnp.bfloat16),
        compiler_params=vmem(),
        cost_estimate=pl.CostEstimate(
            flops=1_000_000_000, bytes_accessed=5_000_000, transcendentals=0
        ),
        name="gather",
    )(place, index, kept, received, gain)


def merge_kernel(place, index_ref, kept, received, gain_ref, *refs):
    earlier_hbm, w_own, w_other, own, other, earlier, weights, sems = refs
    rows, width = kept.shape
    copies = [pltpu.make_async_copy(earlier_hbm, earlier, sems.at[0])]
    for k in range(4):
        at = pl.ds(k * width, width)
        for i, source in enumerate((w_own, w_other)):
            target = weights.at[k, pl.ds(i * own.shape[1], own.shape[1])]
            copies.append(pltpu.make_async_copy(source.at[:, at], target, sems.at[1 + 2 * k + i]))
    for copy in copies:
        copy.start()
    final = normalized(kept[...] + received[...].astype(jnp.float32), row_of(gain_ref))
    copies[0].wait()
    total = None
    for k in range(4):
        part = dot(one_hot_rows(index_ref, k, place[3], rows), final, NN)
        part = (part + earlier[k].astype(jnp.float32)).astype(jnp.bfloat16)
        copies[1 + 2 * k].wait()
        copies[2 + 2 * k].wait()
        term = dot(part, weights[k], NT)
        total = term if total is None else total + term
    own[...] = total[:, : own.shape[1]]
    other[...] = total[:, own.shape[1] :]


def merge(place, index, kept, received, gain, earlier, w_own, w_other):
    merged_rows = index.shape[1]
    columns = w_own.shape[0]
    width = kept.shape[1]
    whole = lambda a: pl.BlockSpec(a.shape, lambda i, s: (0,) * a.ndim)
    any_spec = pl.BlockSpec(memory_space=pl.ANY)
    out_spec = pl.BlockSpec((merged_rows, columns), lambda i, s: (0, 0))
    return pl.pallas_call(
        merge_kernel,
        grid_spec=pltpu.PrefetchScalarGridSpec(
            num_scalar_prefetch=1,
            grid=(1,),
            in_specs=[whole(a) for a in (index, kept, received, gain)] + [any_spec] * 3,
            out_specs=[out_spec, out_spec],
            scratch_shapes=[
                pltpu.VMEM(earlier.shape, jnp.bfloat16),
                pltpu.VMEM((4, 2 * columns, width), jnp.bfloat16),
                pltpu.SemaphoreType.DMA((9,)),
            ],
        ),
        out_shape=[jax.ShapeDtypeStruct((merged_rows, columns), jnp.float32)] * 2,
        compiler_params=vmem(),
        cost_estimate=pl.CostEstimate(
            flops=3_000_000_000, bytes_accessed=12_000_000, transcendentals=0
        ),
        name="merge",
    )(place, index, kept, received, gain, earlier, w_own, w_other)


def place_kernel(position, own, received, out):
    feature = (own[...] + received[...]).astype(jnp.bfloat16)
    slots = lax.broadcasted_iota(jnp.int32, (out.shape[0], 1), 0)
    chosen = (slots == position[...]).astype(jnp.float32).astype(jnp.bfloat16)
    out[...] = dot(chosen, feature, NN).astype(jnp.bfloat16)


def body(
    tokens,
    segments,
    attend_gain,
    attend_weight,
    output_weight,
    mixer_gain,
    expand_weight,
    reduce_weight,
    output_gain,
    merge_weight,
    merge_index,
    owners,
):
    rows, width = tokens.shape
    head_width = attend_weight.shape[2]
    half = head_width // 2
    peers = lax.axis_size("req")
    req = lax.axis_index("req")
    par = req % 2
    core = lax.axis_index("tp") % 2

    chunk_rows = 256
    per_core = rows // 2
    place = jnp.stack([par, core, core * per_core, core * per_core + chunk_rows])
    with jax.named_scope("project"):
        weight = jnp.transpose(attend_weight, (1, 2, 0)).reshape(6 * half, width)
        kv_own, kv_send, q_own, q_send = project(tokens, segments[None, :], attend_gain, weight)

    with jax.named_scope("exchange_keys"):
        kv_peer = swap(kv_send, "req", 1)
        kv_before = shifted(kv_own, "req", 2)
        kv_after = shifted(kv_own, "req", -2)
        state_own = attend(place, q_own, kv_own, [kv_own], "attend_own")
        q_send, kv_peer, state_own = lax.optimization_barrier((q_send, kv_peer, state_own))
        q_peer = swap(q_send, "req", 1)
        kv_before_peer = shifted(kv_peer, "req", 2)
        kv_after_peer = shifted(kv_peer, "req", -2)

    with jax.named_scope("weights"):
        wo = [output_weight.reshape(2, half, width)]
        wo.append(swap(wo[0], "tp", 1))
        wo.append(swap(wo[0], "tp", 2))
        wo.append(swap(wo[2], "tp", 1))
        expand_other = swap(expand_weight, "tp", 1)
        reduce_other = swap(reduce_weight, "tp", 1)
        merge_own = jnp.transpose(merge_weight)
        merge_other = swap(merge_own, "tp", 1)

    with jax.named_scope("attention"):
        near = [kv_peer, kv_before, kv_after]
        far = [kv_before_peer, kv_after_peer]
        state_own = attend(place, q_own, kv_own, near, "attend_near", state_own)
        state_peer = attend(place, q_peer, kv_peer, [kv_own] + near, "attend_near_peer")
        for_peer = attend(place, q_peer, kv_peer, far, "attend_far_peer", state_peer, True)
        from_peer = swap(for_peer, "req", 1)
        context = attend(place, q_own, kv_own, far, "attend_far", state_own, True)

    with jax.named_scope("exchange_context"):
        sides = []
        for source in (context, from_peer):
            across = swap(source, "tp", 2)
            sides.append(
                [(source, 0), (swap(source, "tp", 1), 1), (across, 0), (swap(across, "tp", 1), 1)]
            )
        pieces = [sides[h][t] for t in range(4) for h in range(2)]

    with jax.named_scope("mixer"):
        weights = [expand_weight, expand_other, reduce_weight, reduce_other]
        sent, kept, received = [], [], []
        for chunk in range(2):
            s, k = mixer(place, pieces, tokens, mixer_gain, wo, weights, chunk, chunk_rows)
            kept.append(k)
            received.append(swap(s, "tp", 2))

    with jax.named_scope("merge"):
        index = jnp.transpose(merge_index) - req * rows
        earlier = gather(place, index, kept[0], received[0], output_gain)
        own, other = merge(
            place, index, kept[1], received[1], output_gain, earlier, merge_own, merge_other
        )
        other = swap(other, "tp", 1)

    with jax.named_scope("place"):
        capacity = 2 * merge_index.shape[0] // peers
        target = owners[:, 0]
        choose = (target[:, None] == jnp.arange(peers, dtype=jnp.int32)[None, :]).astype(jnp.int32)
        slot = jnp.sum((jnp.cumsum(choose, axis=0) - 1) * choose, axis=1)
        position = (target * capacity + slot)[None, :]
        columns = own.shape[1]
        outgoing = pl.pallas_call(
            place_kernel,
            out_shape=jax.ShapeDtypeStruct((peers * capacity, columns), jnp.bfloat16),
            name="place",
        )(position, own, other)
        outgoing = outgoing.reshape(peers, capacity, columns)
        arrived = lax.all_to_all(outgoing, "req", split_axis=0, concat_axis=0, tiled=True)
    return arrived.reshape(1, peers, capacity, columns)


def solution(mesh):
    placed = (
        P("req", None),
        P("req"),
        P(),
        P(None, None, "tp"),
        P("tp", None),
        P(),
        P(None, "tp"),
        P("tp", None),
        P(),
        P(None, "tp"),
        P("req", None),
        P("req", None),
    )
    return jax.shard_map(
        body, mesh=mesh, in_specs=placed, out_specs=P("req", None, None, "tp"), check_vma=False
    )
```

```python
import functools
import math

import jax
import jax.numpy as jnp
from jax import lax
from jax.experimental import pallas as pl
from jax.experimental.pallas import tpu as pltpu
from jax.sharding import PartitionSpec as P

HD = 80
TILE = 512
MASKED = -1e30
START = -1e28
FACTOR = 1.0 / math.sqrt(HD)
SEGMENT_ROWS = 16
VROWS = 96
LANES = 256
AHEAD = 2
SMALL = 72.0


def swap(block, axis, flip):
    return lax.ppermute(block, axis, [(i, i ^ flip) for i in range(lax.axis_size(axis))])


def shifted(block, axis, distance):
    devices = range(lax.axis_size(axis))
    route = [(i - distance, i) for i in devices if i - distance in devices]
    return lax.ppermute(block, axis, route)


def normalized(stream, gain):
    center = jnp.mean(stream, axis=-1, keepdims=True)
    moved = stream - center
    spread = jnp.mean(moved * moved, axis=-1, keepdims=True)
    return (moved * lax.rsqrt(spread + 1e-06) * gain).astype(jnp.bfloat16)


def dot(a, b, contract):
    return lax.dot_general(a, b, (contract, ((), ())), preferred_element_type=jnp.float32)


NN = ((1,), (0,))
NT = ((1,), (1,))


def row_of(gain_ref):
    return gain_ref[...].astype(jnp.float32).reshape(1, gain_ref.shape[0])


def vmem():
    return pltpu.CompilerParams(vmem_limit_bytes=60 << 20)


def project_kernel(x_ref, segment_ref, gain_ref, w_ref, kv_keep, kv_send, q_keep, q_send):
    first = lax.axis_index("req") % 2 == 0
    half = q_keep.shape[0]
    rows = normalized(x_ref[...].astype(jnp.float32), row_of(gain_ref))
    number = segment_ref[...] + 1
    row = lax.broadcasted_iota(jnp.int32, (SEGMENT_ROWS, 1), 0)
    number = jnp.where(row == 0, number & 255, jnp.where(row == 1, number >> 8, 0))
    number = number.astype(jnp.float32).astype(jnp.bfloat16)
    out = dot(w_ref[...], rows, NT)
    for part, keep, send in ((0, q_keep, q_send), (1, kv_keep, kv_send), (2, kv_keep, kv_send)):
        low = out[2 * part * half : (2 * part + 1) * half]
        high = out[(2 * part + 1) * half : (2 * part + 2) * half]
        at = slice(max(part - 1, 0) * half, max(part, 1) * half)
        keep[at, :] = jnp.where(first, low, high).astype(jnp.bfloat16)
        send[at, :] = jnp.where(first, high, low).astype(jnp.bfloat16)
    kv_keep[2 * half :, :] = number
    kv_send[2 * half :, :] = number


def project(tokens, segments, gain, weight):
    rows, width = tokens.shape
    half = weight.shape[0] // 6
    step = 256
    tall = 2 * half + SEGMENT_ROWS
    shapes = [(tall, rows), (tall, rows), (half, rows), (half, rows)]
    return pl.pallas_call(
        project_kernel,
        grid=(rows // step,),
        in_specs=[
            pl.BlockSpec((step, width), lambda i: (i, 0)),
            pl.BlockSpec((1, step), lambda i: (0, i)),
            pl.BlockSpec(gain.shape, lambda i: (0,)),
            pl.BlockSpec(weight.shape, lambda i: (0, 0)),
        ],
        out_specs=[pl.BlockSpec((s[0], step), lambda i: (0, i)) for s in shapes],
        out_shape=[jax.ShapeDtypeStruct(s, jnp.bfloat16) for s in shapes],
        compiler_params=vmem(),
        name="project",
    )(tokens, segments, gain, weight)


def numbers_of(ref, at):
    two = ref[:, at].astype(jnp.float32)
    return two[0:1] + 256.0 * two[1:2]


def largest_norm(first, second):
    squares = []
    for block in (first, second):
        block = block.astype(jnp.float32)
        squares.append(jnp.sum(block * block, axis=0, keepdims=True))
    return jnp.max(jnp.maximum(squares[0], squares[1]))


def attend_kernel(blocks, resumed, last, place, q_ref, number_ref, *refs):
    kv_refs, refs = refs[:blocks], refs[blocks:]
    if resumed:
        acc_in, peak_in, refs = refs[0], refs[1], refs[2:]
    if last:
        ctx_out, refs = refs[0], refs[1:]
    else:
        acc_out, peak_out, refs = refs[0], refs[1], refs[2:]
    keys, values, columns, acc, peak, bounds, plain = refs
    tiles_of = kv_refs[0].shape[1] // TILE
    tiles = blocks * tiles_of
    tall = kv_refs[0].shape[0] - SEGMENT_ROWS

    @pl.when(pl.program_id(0) == 0)
    def _():
        for b in range(blocks):
            for t in range(tiles_of):
                n = b * tiles_of + t
                at = slice(t * TILE, (t + 1) * TILE)
                for h in range(2):
                    block = kv_refs[b][h * HD : (h + 1) * HD, at].astype(jnp.float32)
                    keys[n, h] = jnp.transpose(block).astype(jnp.bfloat16)
                    values[n, h, :HD] = kv_refs[b][(2 + h) * HD : (3 + h) * HD, at]
                    values[n, h, HD:] = jnp.ones((VROWS - HD, TILE), jnp.bfloat16)
                number = numbers_of(kv_refs[b].at[tall:], at)
                bounds[3 * n] = jnp.min(number)
                bounds[3 * n + 1] = jnp.max(number)
                bounds[3 * n + 2] = largest_norm(kv_refs[b][:HD, at], kv_refs[b][HD : 2 * HD, at])
                columns[n] = jnp.transpose(jnp.broadcast_to(number, (128, TILE)))

    if resumed:
        acc[...] = acc_in[0]
        peak[...] = peak_in[0]
        plain[0] = (jnp.max(jnp.abs(peak_in[0])) == 0.0).astype(jnp.int32)
    else:
        acc[...] = jnp.zeros_like(acc)
        peak[...] = jnp.zeros_like(peak)
        plain[0] = 1

    q_row = numbers_of(number_ref, slice(0, TILE))
    q_low, q_high = jnp.min(q_row), jnp.max(q_row)
    q_norm = largest_norm(q_ref[:HD, :], q_ref[HD:, :])

    def scores_of(t, h, at, matches):
        scores = dot(keys[t, h], q_ref[h * HD : (h + 1) * HD, at], NN)
        return scores if matches is None else jnp.where(matches, scores, MASKED)

    def matches_of(t, at):
        column = columns[t]
        return jnp.concatenate([column] * (LANES // 128), axis=1) == q_row[:, at]

    units = [(slice(c, c + LANES), h) for c in range(0, TILE, LANES) for h in range(2)]

    def unshifted(t, masked):
        scores, probs, matches = {}, {}, None
        for i in range(len(units) + AHEAD + 1):
            if i < len(units):
                at, h = units[i]
                if masked and h == 0:
                    matches = matches_of(t, at)
                scores[i] = scores_of(t, h, at, matches)
            if 0 <= i - AHEAD < len(units):
                probs[i - AHEAD] = jnp.exp(scores.pop(i - AHEAD) * FACTOR).astype(jnp.bfloat16)
            if 0 <= i - AHEAD - 1 < len(units):
                at, h = units[i - AHEAD - 1]
                acc[h, :, at] += dot(values[t, h], probs.pop(i - AHEAD - 1), NN)

    def shifted_by_peak(t):
        for at, h in units:
            scores = scores_of(t, h, at, matches_of(t, at))
            old = jnp.where(acc[h, HD : HD + 1, at] > 0.0, peak[h : h + 1, at], START)
            new = jnp.maximum(old, jnp.max(scores, axis=0, keepdims=True))
            probs = jnp.exp((scores - new) * FACTOR).astype(jnp.bfloat16)
            shrink = jnp.exp((old - new) * FACTOR)
            peak[h : h + 1, at] = new
            acc[h, :, at] = acc[h, :, at] * shrink + dot(values[t, h], probs, NN)
        plain[0] = 0

    def visit(t, carry):
        k_low, k_high = bounds[3 * t], bounds[3 * t + 1]
        touches = (k_high >= q_low) & (k_low <= q_high)
        whole = (k_low == k_high) & (q_low == q_high)
        small = (plain[0] == 1) & (q_norm * bounds[3 * t + 2] <= SMALL * SMALL * HD)

        @pl.when(touches & small & whole)
        def _():
            unshifted(t, False)

        @pl.when(touches & small & jnp.logical_not(whole))
        def _():
            unshifted(t, True)

        @pl.when(touches & jnp.logical_not(small))
        def _():
            shifted_by_peak(t)

        return carry

    lax.fori_loop(0, tiles, visit, 0)
    if last:
        for h in range(2):
            at = slice(h * HD, (h + 1) * HD)
            ctx_out[0, at, :] = (acc[h, :HD] / acc[h, HD : HD + 1]).astype(jnp.bfloat16)
    else:
        acc_out[0] = acc[...]
        peak_out[0] = peak[...]


def attend(place, queries, numbers, key_values, name, state=None, last=False):
    half, rows = queries.shape
    steps = rows // TILE
    blocks = len(key_values)
    tiles = blocks * steps
    tall = numbers.shape[0] - SEGMENT_ROWS
    whole = lambda a: pl.BlockSpec(a.shape, lambda j, s: (0,) * a.ndim)
    acc_shape, peak_shape = (2, VROWS, TILE), (2, TILE)
    acc_spec = pl.BlockSpec((1,) + acc_shape, lambda j, s: (j, 0, 0, 0))
    peak_spec = pl.BlockSpec((1,) + peak_shape, lambda j, s: (j, 0, 0))
    in_specs = [
        pl.BlockSpec((half, TILE), lambda j, s: (0, j ^ s[1])),
        pl.BlockSpec((SEGMENT_ROWS, TILE), lambda j, s: (tall // SEGMENT_ROWS, j ^ s[1])),
    ] + [whole(kv) for kv in key_values]
    operands = [queries, numbers, *key_values]
    if state is not None:
        in_specs += [acc_spec, peak_spec]
        operands += list(state)
    if last:
        out_specs = pl.BlockSpec((1, half, TILE), lambda j, s: (j, 0, 0))
        out_shape = jax.ShapeDtypeStruct((steps, half, TILE), jnp.bfloat16)
    else:
        out_specs = [acc_spec, peak_spec]
        out_shape = [
            jax.ShapeDtypeStruct((steps,) + acc_shape, jnp.float32),
            jax.ShapeDtypeStruct((steps,) + peak_shape, jnp.float32),
        ]
    return pl.pallas_call(
        functools.partial(attend_kernel, blocks, state is not None, last),
        grid_spec=pltpu.PrefetchScalarGridSpec(
            num_scalar_prefetch=1,
            grid=(steps,),
            in_specs=in_specs,
            out_specs=out_specs,
            scratch_shapes=[
                pltpu.VMEM((tiles, 2, TILE, HD), jnp.bfloat16),
                pltpu.VMEM((tiles, 2, VROWS, TILE), jnp.bfloat16),
                pltpu.VMEM((tiles, TILE, 128), jnp.float32),
                pltpu.VMEM(acc_shape, jnp.float32),
                pltpu.VMEM(peak_shape, jnp.float32),
                pltpu.SMEM((3 * tiles,), jnp.float32),
                pltpu.SMEM((1,), jnp.int32),
            ],
        ),
        out_shape=out_shape,
        compiler_params=vmem(),
        cost_estimate=pl.CostEstimate(
            flops=1_000_000_000 * blocks, bytes_accessed=4_000_000, transcendentals=0
        ),
        name=name,
    )(place, *operands)


def mixer_kernel(place, *refs):
    sources, refs = refs[:8], refs[8:]
    x_ref, gain_ref, refs = refs[0], refs[1], refs[2:]
    wo_hbm, we_hbm, wr_hbm, sent, kept, context, hidden, wo, we, wr, sems = refs
    par, tp = place[0], place[4]
    half = sources[0].shape[1]
    width = we.shape[2]
    copies = []
    for i in range(8):
        copies.append(
            pltpu.make_async_copy(
                wo_hbm.at[tp ^ (i // 2), par ^ (i % 2)], wo.at[pl.ds(i * half, half)], sems.at[i]
            )
        )
    for i in range(2):
        copies.append(pltpu.make_async_copy(we_hbm.at[i], we.at[i], sems.at[8 + i]))
    for i in range(2):
        copies.append(pltpu.make_async_copy(wr_hbm.at[i], wr.at[i], sems.at[10 + i]))
    for copy in copies:
        copy.start()
    for i in range(8):
        context[i * half : (i + 1) * half, :] = sources[i][0].astype(jnp.float32)
    rows = jnp.transpose(context[...]).astype(jnp.bfloat16)
    for i in range(8):
        copies[i].wait()
    total = x_ref[...].astype(jnp.float32) + dot(rows, wo[...], NN)
    rows = normalized(total, row_of(gain_ref))
    for i in range(2):
        copies[8 + i].wait()
        inner = dot(rows, we[i], NN)
        grown = 0.5 * inner * (1.0 + lax.erf(inner * (1.0 / math.sqrt(2.0))))
        hidden[:, i * width : (i + 1) * width] = grown.astype(jnp.bfloat16)
    for i in range(2):
        copies[10 + i].wait()
    out = dot(hidden[:, :width], wr[0], NN) + dot(hidden[:, width:], wr[1], NN)
    sent[...] = out.astype(jnp.bfloat16)
    kept[...] = total + out


def mixer(place, pieces, tokens, gain, wo, expand, reduce, chunk, chunk_rows):
    width = tokens.shape[1]
    half, per_core = pieces[0][0].shape[1:]
    chunks = per_core // chunk_rows
    hidden = expand.shape[2]
    piece_spec = lambda which: pl.BlockSpec((1, half, chunk_rows), lambda i, s: (which, 0, chunk))
    any_spec = pl.BlockSpec(memory_space=pl.ANY)
    out_spec = pl.BlockSpec((chunk_rows, width), lambda i, s: (0, 0))
    return pl.pallas_call(
        mixer_kernel,
        grid_spec=pltpu.PrefetchScalarGridSpec(
            num_scalar_prefetch=1,
            grid=(1,),
            in_specs=[piece_spec(which) for _, which in pieces]
            + [
                pl.BlockSpec((chunk_rows, width), lambda i, s: (s[1] * chunks + chunk, 0)),
                pl.BlockSpec(gain.shape, lambda i, s: (0,)),
            ]
            + [any_spec] * 3,
            out_specs=[out_spec, out_spec],
            scratch_shapes=[
                pltpu.VMEM((8 * half, chunk_rows), jnp.float32),
                pltpu.VMEM((chunk_rows, 2 * hidden), jnp.bfloat16),
                pltpu.VMEM((8 * half, width), jnp.bfloat16),
                pltpu.VMEM(expand.shape, jnp.bfloat16),
                pltpu.VMEM(reduce.shape, jnp.bfloat16),
                pltpu.SemaphoreType.DMA((12,)),
            ],
        ),
        out_shape=[
            jax.ShapeDtypeStruct((chunk_rows, width), jnp.bfloat16),
            jax.ShapeDtypeStruct((chunk_rows, width), jnp.float32),
        ],
        compiler_params=vmem(),
        cost_estimate=pl.CostEstimate(
            flops=5_000_000_000, bytes_accessed=20_000_000, transcendentals=0
        ),
        name="mixer",
    )(place, *[source for source, _ in pieces], tokens, gain, wo, expand, reduce)


def one_hot_rows(index_ref, k, first, rows):
    column = jnp.transpose(jnp.broadcast_to(index_ref[k : k + 1, :], (128, index_ref.shape[1])))
    lanes = lax.broadcasted_iota(jnp.int32, (1, 128), 1)
    parts = [column == lanes + (first + 128 * n) for n in range(rows // 128)]
    return jnp.concatenate(parts, axis=1).astype(jnp.float32).astype(jnp.bfloat16)


def gather_kernel(place, index_ref, kept, received, gain_ref, merged):
    rows = kept.shape[0]
    final = normalized(kept[...] + received[...].astype(jnp.float32), row_of(gain_ref))
    for k in range(4):
        merged[k] = dot(one_hot_rows(index_ref, k, place[2], rows), final, NN).astype(jnp.bfloat16)


def gather(place, index, kept, received, gain):
    rows, width = kept.shape
    merged_rows = index.shape[1]
    whole = lambda a: pl.BlockSpec(a.shape, lambda i, s: (0,) * a.ndim)
    return pl.pallas_call(
        gather_kernel,
        grid_spec=pltpu.PrefetchScalarGridSpec(
            num_scalar_prefetch=1,
            grid=(1,),
            in_specs=[whole(index), whole(kept), whole(received), whole(gain)],
            out_specs=pl.BlockSpec((4, merged_rows, width), lambda i, s: (0, 0, 0)),
        ),
        out_shape=jax.ShapeDtypeStruct((4, merged_rows, width), jnp.bfloat16),
        compiler_params=vmem(),
        cost_estimate=pl.CostEstimate(
            flops=1_000_000_000, bytes_accessed=5_000_000, transcendentals=0
        ),
        name="gather",
    )(place, index, kept, received, gain)


def merge_kernel(place, index_ref, kept, received, gain_ref, *refs):
    earlier_hbm, w_hbm, own, other, earlier, weights, sems = refs
    rows, width = kept.shape
    copies = [pltpu.make_async_copy(earlier_hbm, earlier, sems.at[0])]
    for k in range(4):
        at = pl.ds(k * width, width)
        for i in range(2):
            source = w_hbm.at[place[1] ^ i, :, at]
            target = weights.at[k, pl.ds(i * own.shape[1], own.shape[1])]
            copies.append(pltpu.make_async_copy(source, target, sems.at[1 + 2 * k + i]))
    for copy in copies:
        copy.start()
    final = normalized(kept[...] + received[...].astype(jnp.float32), row_of(gain_ref))
    copies[0].wait()
    total = None
    for k in range(4):
        part = dot(one_hot_rows(index_ref, k, place[3], rows), final, NN)
        part = (part + earlier[k].astype(jnp.float32)).astype(jnp.bfloat16)
        copies[1 + 2 * k].wait()
        copies[2 + 2 * k].wait()
        term = dot(part, weights[k], NT)
        total = term if total is None else total + term
    own[...] = total[:, : own.shape[1]]
    other[...] = total[:, own.shape[1] :]


def merge(place, index, kept, received, gain, earlier, weights):
    merged_rows = index.shape[1]
    columns = weights.shape[1]
    width = kept.shape[1]
    whole = lambda a: pl.BlockSpec(a.shape, lambda i, s: (0,) * a.ndim)
    any_spec = pl.BlockSpec(memory_space=pl.ANY)
    out_spec = pl.BlockSpec((merged_rows, columns), lambda i, s: (0, 0))
    return pl.pallas_call(
        merge_kernel,
        grid_spec=pltpu.PrefetchScalarGridSpec(
            num_scalar_prefetch=1,
            grid=(1,),
            in_specs=[whole(a) for a in (index, kept, received, gain)] + [any_spec] * 2,
            out_specs=[out_spec, out_spec],
            scratch_shapes=[
                pltpu.VMEM(earlier.shape, jnp.bfloat16),
                pltpu.VMEM((4, 2 * columns, width), jnp.bfloat16),
                pltpu.SemaphoreType.DMA((9,)),
            ],
        ),
        out_shape=[jax.ShapeDtypeStruct((merged_rows, columns), jnp.float32)] * 2,
        compiler_params=vmem(),
        cost_estimate=pl.CostEstimate(
            flops=3_000_000_000, bytes_accessed=12_000_000, transcendentals=0
        ),
        name="merge",
    )(place, index, kept, received, gain, earlier, weights)


def place_kernel(position, own, received, out):
    feature = (own[...] + received[...]).astype(jnp.bfloat16)
    slots = lax.broadcasted_iota(jnp.int32, (out.shape[0], 1), 0)
    chosen = (slots == position[...]).astype(jnp.float32).astype(jnp.bfloat16)
    out[...] = dot(chosen, feature, NN).astype(jnp.bfloat16)


def body(
    tokens,
    segments,
    attend_gain,
    attend_weight,
    output_weight,
    mixer_gain,
    expand_weight,
    reduce_weight,
    output_gain,
    merge_weight,
    merge_index,
    owners,
):
    rows, width = tokens.shape
    head_width = attend_weight.shape[2]
    half = head_width // 2
    peers = lax.axis_size("req")
    req = lax.axis_index("req")
    par = req % 2
    tp = lax.axis_index("tp")
    core = tp % 2

    chunk_rows = 256
    per_core = rows // 2
    place = jnp.stack([par, core, core * per_core, core * per_core + chunk_rows, tp])
    with jax.named_scope("project"):
        weight = jnp.transpose(attend_weight, (1, 2, 0)).reshape(6 * half, width)
        kv_own, kv_send, q_own, q_send = project(tokens, segments[None, :], attend_gain, weight)

    with jax.named_scope("exchange_keys"):
        kv_peer = swap(kv_send, "req", 1)
        kv_before = shifted(kv_own, "req", 2)
        kv_after = shifted(kv_own, "req", -2)
        state_own = attend(place, q_own, kv_own, [kv_own], "attend_own")
        q_send, kv_peer, state_own = lax.optimization_barrier((q_send, kv_peer, state_own))
        q_peer = swap(q_send, "req", 1)
        kv_before_peer = shifted(kv_peer, "req", 2)
        kv_after_peer = shifted(kv_peer, "req", -2)

    with jax.named_scope("weights"):
        cores = [[i, i + 1] for i in range(0, lax.axis_size("tp"), 2)]
        wo = lax.all_gather(output_weight.reshape(2, half, width), "tp")
        expand = lax.all_gather(expand_weight, "tp", axis_index_groups=cores)
        reduce = lax.all_gather(reduce_weight, "tp", axis_index_groups=cores)
        merging = lax.all_gather(jnp.transpose(merge_weight), "tp", axis_index_groups=cores)

    with jax.named_scope("attention"):
        near = [kv_peer, kv_before, kv_after]
        far = [kv_before_peer, kv_after_peer]
        state_own = attend(place, q_own, kv_own, near, "attend_near", state_own)
        state_peer = attend(place, q_peer, kv_peer, [kv_own] + near, "attend_near_peer")
        for_peer = attend(place, q_peer, kv_peer, far, "attend_far_peer", state_peer, True)
        from_peer = swap(for_peer, "req", 1)
        context = attend(place, q_own, kv_own, far, "attend_far", state_own, True)

    with jax.named_scope("exchange_context"):
        sides = []
        for source in (context, from_peer):
            across = swap(source, "tp", 2)
            sides.append(
                [(source, 0), (swap(source, "tp", 1), 1), (across, 0), (swap(across, "tp", 1), 1)]
            )
        pieces = [sides[h][t] for t in range(4) for h in range(2)]

    with jax.named_scope("mixer"):
        sent, kept, received = [], [], []
        for chunk in range(2):
            s, k = mixer(place, pieces, tokens, mixer_gain, wo, expand, reduce, chunk, chunk_rows)
            kept.append(k)
            received.append(swap(s, "tp", 2))

    with jax.named_scope("merge"):
        index = jnp.transpose(merge_index) - req * rows
        earlier = gather(place, index, kept[0], received[0], output_gain)
        own, other = merge(
            place, index, kept[1], received[1], output_gain, earlier, merging
        )
        other = swap(other, "tp", 1)

    with jax.named_scope("place"):
        capacity = 2 * merge_index.shape[0] // peers
        target = owners[:, 0]
        choose = (target[:, None] == jnp.arange(peers, dtype=jnp.int32)[None, :]).astype(jnp.int32)
        slot = jnp.sum((jnp.cumsum(choose, axis=0) - 1) * choose, axis=1)
        position = (target * capacity + slot)[None, :]
        columns = own.shape[1]
        outgoing = pl.pallas_call(
            place_kernel,
            out_shape=jax.ShapeDtypeStruct((peers * capacity, columns), jnp.bfloat16),
            name="place",
        )(position, own, other)
        outgoing = outgoing.reshape(peers, capacity, columns)
        arrived = lax.all_to_all(outgoing, "req", split_axis=0, concat_axis=0, tiled=True)
    return arrived.reshape(1, peers, capacity, columns)


def solution(mesh):
    placed = (
        P("req", None),
        P("req"),
        P(),
        P(None, None, "tp"),
        P("tp", None),
        P(),
        P(None, "tp"),
        P("tp", None),
        P(),
        P(None, "tp"),
        P("req", None),
        P("req", None),
    )
    return jax.shard_map(
        body, mesh=mesh, in_specs=placed, out_specs=P("req", None, None, "tp"), check_vma=False
    )
```

```python
import functools
import math

import jax
import jax.numpy as jnp
from jax import lax
from jax.experimental import pallas as pl
from jax.experimental.pallas import tpu as pltpu
from jax.sharding import PartitionSpec as P

HD = 80
TILE = 512
MASKED = -1e30
START = -1e28
FACTOR = 1.0 / math.sqrt(HD)
SEGMENT_ROWS = 16
VROWS = 96
LANES = 256
AHEAD = 2
SMALL = 72.0


def swap(block, axis, flip):
    return lax.ppermute(block, axis, [(i, i ^ flip) for i in range(lax.axis_size(axis))])


def next_pair(i, first, size):
    other = i + 2 if i // 2 % 2 == first else i - 2
    return other if 0 <= other < size else i


def swap_pairs(block, first):
    size = lax.axis_size("req")
    return lax.ppermute(block, "req", [(i, next_pair(i, first, size)) for i in range(size)])


def alone(first):
    size = lax.axis_size("req")
    lonely = [i for i in range(size) if next_pair(i, first, size) == i]
    return sum([(lax.axis_index("req") == i).astype(jnp.int32) for i in lonely], jnp.int32(0))


def normalized(stream, gain):
    center = jnp.mean(stream, axis=-1, keepdims=True)
    moved = stream - center
    spread = jnp.mean(moved * moved, axis=-1, keepdims=True)
    return (moved * lax.rsqrt(spread + 1e-06) * gain).astype(jnp.bfloat16)


def dot(a, b, contract):
    return lax.dot_general(a, b, (contract, ((), ())), preferred_element_type=jnp.float32)


NN = ((1,), (0,))
NT = ((1,), (1,))


def row_of(gain_ref):
    return gain_ref[...].astype(jnp.float32).reshape(1, gain_ref.shape[0])


def vmem(mebibytes=60):
    return pltpu.CompilerParams(vmem_limit_bytes=mebibytes << 20)


def in_hbm(array):
    return pltpu.with_memory_space_constraint(array, pltpu.HBM)


def in_vmem(array):
    return pltpu.with_memory_space_constraint(array, pltpu.VMEM)


SCALARS = pl.BlockSpec(memory_space=pltpu.SMEM)
RESIDENT = pl.BlockSpec(memory_space=pltpu.VMEM)
ANYWHERE = pl.BlockSpec(memory_space=pl.ANY)


def load_mixer_kernel(place, *refs):
    wo_refs, we_refs, wr_refs, refs = refs[:4], refs[4:6], refs[6:8], refs[8:]
    wo, we, wr, sems = refs
    half = wo.shape[0] // 8
    copies = []
    for i in range(8):
        source = wo_refs[i // 2].at[place[0] ^ (i % 2)]
        copies.append((source, wo.at[pl.ds(i * half, half)]))
    copies += [(we_refs[i], we.at[i]) for i in range(2)]
    copies += [(wr_refs[i], wr.at[i]) for i in range(2)]
    copies = [pltpu.make_async_copy(*pair, sems.at[i]) for i, pair in enumerate(copies)]
    for copy in copies:
        copy.start()
    for copy in copies:
        copy.wait()


def load_mixer(place, wo, expand, reduce):
    half, width = wo[0].shape[1:]
    shapes = [(8 * half, width), (2,) + expand[0].shape, (2,) + reduce[0].shape]
    return pl.pallas_call(
        load_mixer_kernel,
        in_specs=[SCALARS] + [ANYWHERE] * 8,
        out_specs=[RESIDENT] * 3,
        out_shape=[pltpu.VMEM(shape, jnp.bfloat16) for shape in shapes],
        scratch_shapes=[pltpu.SemaphoreType.DMA((12,))],
        compiler_params=vmem(4),
        cost_estimate=pl.CostEstimate(flops=0, bytes_accessed=16_000_000, transcendentals=0),
        name="load_mixer",
    )(place, *[in_hbm(w) for w in (*wo, *expand, *reduce)])


def load_merge_kernel(own, other, both, sems):
    columns = own.shape[0]
    copies = [
        pltpu.make_async_copy(source, both.at[pl.ds(i * columns, columns)], sems.at[i])
        for i, source in enumerate((own, other))
    ]
    for copy in copies:
        copy.start()
    for copy in copies:
        copy.wait()


def load_merge(own, other):
    return pl.pallas_call(
        load_merge_kernel,
        in_specs=[ANYWHERE] * 2,
        out_specs=RESIDENT,
        out_shape=pltpu.VMEM((2 * own.shape[0], own.shape[1]), jnp.bfloat16),
        scratch_shapes=[pltpu.SemaphoreType.DMA((2,))],
        compiler_params=vmem(4),
        cost_estimate=pl.CostEstimate(flops=0, bytes_accessed=8_000_000, transcendentals=0),
        name="load_merge",
    )(in_hbm(own), in_hbm(other))


def project_kernel(parts, x_ref, segment_ref, gain_ref, *refs):
    w_refs, keep, send = refs[:parts], refs[parts], refs[parts + 1]
    first = lax.axis_index("req") % 2 == 0
    half = w_refs[0].shape[0] // 2
    rows = normalized(x_ref[...].astype(jnp.float32), row_of(gain_ref))
    for part in range(parts):
        out = dot(w_refs[part][...], rows, NT)
        low, high = out[:half], out[half:]
        at = slice(part * half, (part + 1) * half)
        keep[at, :] = jnp.where(first, low, high).astype(jnp.bfloat16)
        send[at, :] = jnp.where(first, high, low).astype(jnp.bfloat16)
    if parts > 1:
        number = segment_ref[...] + 1
        row = lax.broadcasted_iota(jnp.int32, (SEGMENT_ROWS, 1), 0)
        number = jnp.where(row == 0, number & 255, jnp.where(row == 1, number >> 8, 0))
        number = number.astype(jnp.float32).astype(jnp.bfloat16)
        keep[parts * half :, :] = number
        send[parts * half :, :] = number


def project(tokens, segments, gain, weight, parts, name):
    rows, width = tokens.shape
    half = weight.shape[0] // 6
    step = 256
    tall = len(parts) * half + (SEGMENT_ROWS if len(parts) > 1 else 0)
    return pl.pallas_call(
        functools.partial(project_kernel, len(parts)),
        grid=(rows // step,),
        in_specs=[
            pl.BlockSpec((step, width), lambda i: (i, 0)),
            pl.BlockSpec((1, step), lambda i: (0, i)),
            pl.BlockSpec(gain.shape, lambda i: (0,)),
        ]
        + [pl.BlockSpec((2 * half, width), lambda i, p=p: (p, 0)) for p in parts],
        out_specs=[pl.BlockSpec((tall, step), lambda i: (0, i))] * 2,
        out_shape=[jax.ShapeDtypeStruct((tall, rows), jnp.bfloat16)] * 2,
        compiler_params=vmem(),
        name=name,
    )(tokens, segments, gain, *[weight] * len(parts))


def numbers_of(ref, at):
    two = ref[:, at].astype(jnp.float32)
    return two[0:1] + 256.0 * two[1:2]


def largest_norm(first, second):
    squares = []
    for block in (first, second):
        block = block.astype(jnp.float32)
        squares.append(jnp.sum(block * block, axis=0, keepdims=True))
    return jnp.max(jnp.maximum(squares[0], squares[1]))


def attend_kernel(groups, blocks, flags, resumed, skip, last, place, *refs):
    q_refs, number_refs, refs = refs[:groups], refs[groups : 2 * groups], refs[2 * groups :]
    kv_refs, refs = refs[:blocks], refs[blocks:]
    if resumed:
        acc_in, peak_in, refs = refs[0], refs[1], refs[2:]
    if last:
        ctx_out, refs = refs[:groups], refs[groups:]
    else:
        acc_out, peak_out, refs = refs[0], refs[1], refs[2:]
    keys, values, columns, acc, peak, bounds, plain = refs
    tiles_of = kv_refs[0].shape[1] // TILE
    tiles = blocks * tiles_of
    tall = kv_refs[0].shape[0] - SEGMENT_ROWS
    steps_of = kv_refs[0].shape[1] // TILE
    j = pl.program_id(0)
    fresh = steps_of * groups - resumed

    @pl.when(j == 0)
    def _():
        for b in range(blocks):
            for t in range(tiles_of):
                n = b * tiles_of + t
                at = slice(t * TILE, (t + 1) * TILE)
                for h in range(2):
                    block = kv_refs[b][h * HD : (h + 1) * HD, at].astype(jnp.float32)
                    keys[n, h] = jnp.transpose(block).astype(jnp.bfloat16)
                    values[n, h, :HD] = kv_refs[b][(2 + h) * HD : (3 + h) * HD, at]
                    values[n, h, HD:] = jnp.ones((VROWS - HD, TILE), jnp.bfloat16)
                number = numbers_of(kv_refs[b].at[tall:], at)
                low, high = jnp.min(number), jnp.max(number)
                if b in flags:
                    low = jnp.where(place[flags[b]] == 1, -1.0, low)
                    high = jnp.where(place[flags[b]] == 1, -1.0, high)
                bounds[3 * n] = low
                bounds[3 * n + 1] = high
                bounds[3 * n + 2] = largest_norm(kv_refs[b][:HD, at], kv_refs[b][HD : 2 * HD, at])
                columns[n] = jnp.transpose(jnp.broadcast_to(number, (128, TILE)))

    def go_on():
        acc[...] = acc_in[0]
        peak[...] = peak_in[0]
        plain[0] = (jnp.max(jnp.abs(peak_in[0])) == 0.0).astype(jnp.int32)

    def start():
        acc[...] = jnp.zeros_like(acc)
        peak[...] = jnp.zeros_like(peak)
        plain[0] = 1

    if fresh:
        pl.when(j < fresh)(start)
    if resumed:
        pl.when(j >= fresh)(go_on)

    q_row = numbers_of(number_refs[0], slice(0, TILE))
    queries = q_refs[0][...]
    if groups > 1:
        q_row = jnp.where(j < steps_of, q_row, numbers_of(number_refs[1], slice(0, TILE)))
        queries = jnp.where(j < steps_of, queries, q_refs[1][...])
    q_low, q_high = jnp.min(q_row), jnp.max(q_row)
    q_norm = largest_norm(queries[:HD], queries[HD:])

    def scores_of(t, h, at, matches):
        scores = dot(keys[t, h], queries[h * HD : (h + 1) * HD, at], NN)
        return scores if matches is None else jnp.where(matches, scores, MASKED)

    def matches_of(t, at):
        column = columns[t]
        return jnp.concatenate([column] * (LANES // 128), axis=1) == q_row[:, at]

    units = [(slice(c, c + LANES), h) for c in range(0, TILE, LANES) for h in range(2)]

    def unshifted(t, masked):
        scores, probs, matches = {}, {}, None
        for i in range(len(units) + AHEAD + 1):
            if i < len(units):
                at, h = units[i]
                if masked and h == 0:
                    matches = matches_of(t, at)
                scores[i] = scores_of(t, h, at, matches)
            if 0 <= i - AHEAD < len(units):
                probs[i - AHEAD] = jnp.exp(scores.pop(i - AHEAD) * FACTOR).astype(jnp.bfloat16)
            if 0 <= i - AHEAD - 1 < len(units):
                at, h = units[i - AHEAD - 1]
                acc[h, :, at] += dot(values[t, h], probs.pop(i - AHEAD - 1), NN)

    def shifted_by_peak(t):
        for at, h in units:
            scores = scores_of(t, h, at, matches_of(t, at))
            old = jnp.where(acc[h, HD : HD + 1, at] > 0.0, peak[h : h + 1, at], START)
            new = jnp.maximum(old, jnp.max(scores, axis=0, keepdims=True))
            probs = jnp.exp((scores - new) * FACTOR).astype(jnp.bfloat16)
            shrink = jnp.exp((old - new) * FACTOR)
            peak[h : h + 1, at] = new
            acc[h, :, at] = acc[h, :, at] * shrink + dot(values[t, h], probs, NN)
        plain[0] = 0

    def visit(t, carry):
        k_low, k_high = bounds[3 * t], bounds[3 * t + 1]
        touches = (k_high >= q_low) & (k_low <= q_high)
        whole = (k_low == k_high) & (q_low == q_high)
        small = (plain[0] == 1) & (q_norm * bounds[3 * t + 2] <= SMALL * SMALL * HD)

        @pl.when(touches & small & whole)
        def _():
            unshifted(t, False)

        @pl.when(touches & small & jnp.logical_not(whole))
        def _():
            unshifted(t, True)

        @pl.when(touches & jnp.logical_not(small))
        def _():
            shifted_by_peak(t)

        return carry

    lax.fori_loop(jnp.where(j >= fresh, skip, 0), tiles, visit, 0)
    if last:

        def finish(out):
            for h in range(2):
                at = slice(h * HD, (h + 1) * HD)
                out[0, at, :] = (acc[h, :HD] / acc[h, HD : HD + 1]).astype(jnp.bfloat16)

        for g in range(groups):
            pl.when(j // steps_of == g)(functools.partial(finish, ctx_out[g]))
    else:
        acc_out[0] = acc[...]
        peak_out[0] = peak[...]


def attend(place, queries, numbers, key_values, name, flags={}, state=None, skip=0, last=False):
    half, rows = queries[0].shape
    groups, blocks = len(queries), len(key_values)
    steps_of = rows // TILE
    steps = groups * steps_of
    tiles = blocks * steps_of
    tall = numbers[0].shape[0] - SEGMENT_ROWS
    resumed = 0 if state is None else state[0].shape[0]
    whole = lambda a: pl.BlockSpec(a.shape, lambda j, s: (0,) * a.ndim)
    acc_shape, peak_shape = (2, VROWS, TILE), (2, TILE)
    q_spec = pl.BlockSpec((half, TILE), lambda j, s: (0, (j % steps_of) ^ s[1]))
    number_spec = pl.BlockSpec(
        (SEGMENT_ROWS, TILE), lambda j, s: (tall // SEGMENT_ROWS, (j % steps_of) ^ s[1])
    )
    in_specs = [q_spec] * groups + [number_spec] * groups + [whole(kv) for kv in key_values]
    operands = [*queries, *numbers, *key_values]
    if state is not None:
        behind = steps - resumed
        in_specs += [
            pl.BlockSpec((1,) + acc_shape, lambda j, s: (jnp.maximum(j - behind, 0), 0, 0, 0)),
            pl.BlockSpec((1,) + peak_shape, lambda j, s: (jnp.maximum(j - behind, 0), 0, 0)),
        ]
        operands += list(state)
    if last:
        out_specs = [
            pl.BlockSpec(
                (1, half, TILE), lambda j, s, g=g: (jnp.clip(j - g * steps_of, 0, steps_of - 1), 0, 0)
            )
            for g in range(groups)
        ]
        out_shape = [jax.ShapeDtypeStruct((steps_of, half, TILE), jnp.bfloat16)] * groups
    else:
        out_specs = [
            pl.BlockSpec((1,) + acc_shape, lambda j, s: (j, 0, 0, 0)),
            pl.BlockSpec((1,) + peak_shape, lambda j, s: (j, 0, 0)),
        ]
        out_shape = [
            jax.ShapeDtypeStruct((steps,) + acc_shape, jnp.float32),
            jax.ShapeDtypeStruct((steps,) + peak_shape, jnp.float32),
        ]
    return pl.pallas_call(
        functools.partial(attend_kernel, groups, blocks, flags, resumed, skip, last),
        grid_spec=pltpu.PrefetchScalarGridSpec(
            num_scalar_prefetch=1,
            grid=(steps,),
            in_specs=in_specs,
            out_specs=out_specs,
            scratch_shapes=[
                pltpu.VMEM((tiles, 2, TILE, HD), jnp.bfloat16),
                pltpu.VMEM((tiles, 2, VROWS, TILE), jnp.bfloat16),
                pltpu.VMEM((tiles, TILE, 128), jnp.float32),
                pltpu.VMEM(acc_shape, jnp.float32),
                pltpu.VMEM(peak_shape, jnp.float32),
                pltpu.SMEM((3 * tiles,), jnp.float32),
                pltpu.SMEM((1,), jnp.int32),
            ],
        ),
        out_shape=out_shape,
        compiler_params=vmem(),
        cost_estimate=pl.CostEstimate(flops=1_000_000, bytes_accessed=1_000_000, transcendentals=0),
        name=name,
    )(place, *operands)


def mixer_kernel(chunk, which, place, *refs):
    sources, refs = refs[:8], refs[8:]
    x_hbm, gain_ref, wo, we, wr, sent, kept, context, hidden, x, sem = refs
    rows = x.shape[0]
    half = sources[0].shape[1]
    width = we.shape[2]
    fetch = pltpu.make_async_copy(
        x_hbm.at[pl.ds(pl.multiple_of(place[2] + chunk * rows, rows), rows)], x, sem
    )
    fetch.start()
    lanes = slice(chunk * rows, (chunk + 1) * rows)
    for i in range(8):
        context[i * half : (i + 1) * half, :] = sources[i][which[i], :, lanes].astype(jnp.float32)
    inputs = jnp.transpose(context[...]).astype(jnp.bfloat16)
    fetch.wait()
    total = x[...].astype(jnp.float32) + dot(inputs, wo[...], NN)
    inputs = normalized(total, row_of(gain_ref))
    for i in range(2):
        inner = dot(inputs, we[i], NN)
        grown = 0.5 * inner * (1.0 + lax.erf(inner * (1.0 / math.sqrt(2.0))))
        hidden[:, i * width : (i + 1) * width] = grown.astype(jnp.bfloat16)
    out = dot(hidden[:, :width], wr[0], NN) + dot(hidden[:, width:], wr[1], NN)
    sent[...] = out.astype(jnp.bfloat16)
    kept[...] = total + out


def mixer(place, pieces, tokens, gain, weights, chunk, chunk_rows):
    width = tokens.shape[1]
    half = pieces[0][0].shape[1]
    hidden = weights[1].shape[2]
    return pl.pallas_call(
        functools.partial(mixer_kernel, chunk, [which for _, which in pieces]),
        in_specs=[SCALARS] + [RESIDENT] * 8 + [ANYWHERE] + [RESIDENT] * 4,
        out_specs=[RESIDENT] * 2,
        out_shape=[
            jax.ShapeDtypeStruct((chunk_rows, width), jnp.bfloat16),
            jax.ShapeDtypeStruct((chunk_rows, width), jnp.float32),
        ],
        scratch_shapes=[
            pltpu.VMEM((8 * half, chunk_rows), jnp.float32),
            pltpu.VMEM((chunk_rows, 2 * hidden), jnp.bfloat16),
            pltpu.VMEM((chunk_rows, width), jnp.bfloat16),
            pltpu.SemaphoreType.DMA,
        ],
        compiler_params=vmem(30),
        cost_estimate=pl.CostEstimate(
            flops=5_000_000_000, bytes_accessed=20_000_000, transcendentals=0
        ),
        name="mixer",
    )(place, *[source for source, _ in pieces], tokens, gain, *[in_vmem(w) for w in weights])


def one_hot_rows(index_ref, k, first, rows):
    column = jnp.transpose(jnp.broadcast_to(index_ref[k : k + 1, :], (128, index_ref.shape[1])))
    lanes = lax.broadcasted_iota(jnp.int32, (1, 128), 1)
    parts = [column == lanes + (first + 128 * n) for n in range(rows // 128)]
    return jnp.concatenate(parts, axis=1).astype(jnp.float32).astype(jnp.bfloat16)


def gather_kernel(place, index_ref, kept, received, gain_ref, merged):
    rows = kept.shape[0]
    final = normalized(kept[...] + received[...].astype(jnp.float32), row_of(gain_ref))
    for k in range(4):
        merged[k] = dot(one_hot_rows(index_ref, k, place[2], rows), final, NN).astype(jnp.bfloat16)


def gather(place, index, kept, received, gain):
    return pl.pallas_call(
        gather_kernel,
        in_specs=[SCALARS] + [RESIDENT] * 4,
        out_specs=RESIDENT,
        out_shape=pltpu.VMEM((4, index.shape[1], kept.shape[1]), jnp.bfloat16),
        compiler_params=vmem(20),
        cost_estimate=pl.CostEstimate(
            flops=1_000_000_000, bytes_accessed=5_000_000, transcendentals=0
        ),
        name="gather",
    )(place, index, kept, received, gain)


def merge_kernel(place, index_ref, kept, received, gain_ref, earlier, weights, own, other, parts):
    rows, width = kept.shape
    columns = own.shape[1]
    final = normalized(kept[...] + received[...].astype(jnp.float32), row_of(gain_ref))
    for k in range(4):
        part = dot(one_hot_rows(index_ref, k, place[3], rows), final, NN)
        part = part + earlier[k].astype(jnp.float32)
        parts[:, k * width : (k + 1) * width] = part.astype(jnp.bfloat16)
    total = dot(parts[...], weights[...], NT)
    own[...] = total[:, :columns]
    other[...] = total[:, columns:]


def merge(place, index, kept, received, gain, earlier, weights):
    merged_rows = index.shape[1]
    columns = weights.shape[0] // 2
    return pl.pallas_call(
        merge_kernel,
        in_specs=[SCALARS] + [RESIDENT] * 6,
        out_specs=[RESIDENT] * 2,
        out_shape=[jax.ShapeDtypeStruct((merged_rows, columns), jnp.float32)] * 2,
        scratch_shapes=[pltpu.VMEM((merged_rows, weights.shape[1]), jnp.bfloat16)],
        compiler_params=vmem(20),
        cost_estimate=pl.CostEstimate(
            flops=3_000_000_000, bytes_accessed=12_000_000, transcendentals=0
        ),
        name="merge",
    )(place, index, kept, received, gain, in_vmem(earlier), in_vmem(weights))


def place_kernel(position, own, received, out):
    feature = (own[...] + received[...]).astype(jnp.bfloat16)
    slots = lax.broadcasted_iota(jnp.int32, (out.shape[0], 1), 0)
    chosen = (slots == position[...]).astype(jnp.float32).astype(jnp.bfloat16)
    out[...] = dot(chosen, feature, NN).astype(jnp.bfloat16)


def body(
    tokens,
    segments,
    attend_gain,
    attend_weight,
    output_weight,
    mixer_gain,
    expand_weight,
    reduce_weight,
    output_gain,
    merge_weight,
    merge_index,
    owners,
):
    rows, width = tokens.shape
    head_width = attend_weight.shape[2]
    half = head_width // 2
    peers = lax.axis_size("req")
    req = lax.axis_index("req")
    par = req % 2
    core = lax.axis_index("tp") % 2

    chunk_rows = 256
    per_core = rows // 2
    place = jnp.stack([par, core, core * per_core, core * per_core + chunk_rows, alone(0), alone(1)])
    tie = lax.optimization_barrier
    with jax.named_scope("weights"):
        wo_own = output_weight.reshape(2, half, width)
        wo_across = swap(wo_own, "tp", 2)
        expand_other = swap(expand_weight, "tp", 1)

    with jax.named_scope("project"):
        weight = jnp.transpose(attend_weight, (1, 2, 0)).reshape(6 * half, width)
        numbers = segments[None, :]
        kv_own, kv_send = project(tokens, numbers, attend_gain, weight, (1, 2), "project_keys")
        kv_own, kv_send, expand_other, late_reduce = tie(
            (kv_own, kv_send, expand_other, reduce_weight)
        )

    with jax.named_scope("exchange_keys"):
        kv_peer = swap(kv_send, "req", 1)
        kv_even = swap_pairs(kv_own, 0)
        kv_odd = swap_pairs(kv_own, 1)
        reduce_other = swap(late_reduce, "tp", 1)
        q_own, q_send = project(tokens, numbers, attend_gain, weight, (0,), "project_queries")
        state = attend(place, [q_own], [kv_own], [kv_own], "attend_own")
        q_send, kv_peer, state, wo_across, reduce_other = tie(
            (q_send, kv_peer, state, wo_across, reduce_other)
        )
        q_peer = swap(q_send, "req", 1)
        kv_even_peer = swap_pairs(kv_peer, 0)
        kv_odd_peer = swap_pairs(kv_peer, 1)

    with jax.named_scope("slots"):
        capacity = 2 * merge_index.shape[0] // peers
        target = owners[:, 0]
        choose = (target[:, None] == jnp.arange(peers, dtype=jnp.int32)[None, :]).astype(jnp.int32)
        slot = jnp.sum((jnp.cumsum(choose, axis=0) - 1) * choose, axis=1)
        position = (target * capacity + slot)[None, :]
        index = jnp.transpose(merge_index) - req * rows

    with jax.named_scope("more_weights"):
        q_peer, kv_even, kv_odd, late_wo, wo_across, position, index = tie(
            (q_peer, kv_even, kv_odd, wo_own, wo_across, position, index)
        )
        wo_core = swap(late_wo, "tp", 1)
        wo_both = swap(wo_across, "tp", 1)

    with jax.named_scope("attention"):
        queries, numbers = [q_peer, q_own], [kv_peer, kv_own]
        near = [kv_own, kv_peer, kv_even, kv_odd]
        skip = rows // TILE
        state = attend(place, queries, numbers, near, "attend_near", {2: 4, 3: 5}, state, skip)
        state, kv_even_peer, kv_odd_peer, wo_core, wo_both = tie(
            (state, kv_even_peer, kv_odd_peer, wo_core, wo_both)
        )
        far = [kv_even_peer, kv_odd_peer]
        for_peer, context = attend(
            place, queries, numbers, far, "attend_far", {0: 4, 1: 5}, state, last=True
        )

    with jax.named_scope("exchange_context"):
        late_wo, context, for_peer = tie((wo_own, context, for_peer))
        from_peer = swap(for_peer, "req", 1)
        weights = load_mixer(
            place,
            [late_wo, wo_core, wo_across, wo_both],
            [expand_weight, expand_other],
            [reduce_weight, reduce_other],
        )
        from_peer, weights = tie((from_peer, weights))
        sides = []
        for source in (context, from_peer):
            across = swap(source, "tp", 2)
            sides.append(
                [(source, 0), (swap(source, "tp", 1), 1), (across, 0), (swap(across, "tp", 1), 1)]
            )
        pieces = [sides[h][t] for t in range(4) for h in range(2)]

    with jax.named_scope("mixer"):
        sent, kept, received = [], [], []
        for chunk in range(2):
            s, k = mixer(place, pieces, tokens, mixer_gain, weights, chunk, chunk_rows)
            sent.append(s)
            kept.append(k)
            received.append(swap(s, "tp", 2))
            if chunk == 0:
                merge_own, _ = tie((jnp.transpose(merge_weight), s))
                merge_other = swap(merge_own, "tp", 1)

    with jax.named_scope("merge"):
        merge_other, position, index, _ = tie((merge_other, position, index, sent[1]))
        weights = load_merge(merge_own, merge_other)
        earlier = gather(place, index, kept[0], received[0], output_gain)
        weights, earlier, last, position = tie((weights, earlier, received[1], position))
        own, other = merge(place, index, kept[1], last, output_gain, earlier, weights)
        other = swap(other, "tp", 1)

    with jax.named_scope("place"):
        columns = own.shape[1]
        outgoing = pl.pallas_call(
            place_kernel,
            in_specs=[RESIDENT] * 3,
            out_specs=RESIDENT,
            out_shape=jax.ShapeDtypeStruct((peers * capacity, columns), jnp.bfloat16),
            compiler_params=vmem(10),
            name="place",
        )(position, in_vmem(own), in_vmem(other))
        outgoing = outgoing.reshape(peers, capacity, columns)
        arrived = lax.all_to_all(outgoing, "req", split_axis=0, concat_axis=0, tiled=True)
    return arrived.reshape(1, peers, capacity, columns)


def solution(mesh):
    placed = (
        P("req", None),
        P("req"),
        P(),
        P(None, None, "tp"),
        P("tp", None),
        P(),
        P(None, "tp"),
        P("tp", None),
        P(),
        P(None, "tp"),
        P("req", None),
        P("req", None),
    )
    return jax.shard_map(
        body, mesh=mesh, in_specs=placed, out_specs=P("req", None, None, "tp"), check_vma=False
    )
```

```python
import functools
import math

import jax
import jax.numpy as jnp
from jax import lax
from jax.experimental import pallas as pl
from jax.experimental.pallas import tpu as pltpu
from jax.sharding import PartitionSpec as P

HD = 80
TILE = 512
MASKED = -1e30
START = -1e28
FACTOR = 1.0 / math.sqrt(HD)
SEGMENT_ROWS = 16
VROWS = 96
LANES = 256
AHEAD = 2
SMALL = 72.0


def swap(block, axis, flip):
    return lax.ppermute(block, axis, [(i, i ^ flip) for i in range(lax.axis_size(axis))])


def next_pair(i, first, size):
    other = i + 2 if i // 2 % 2 == first else i - 2
    return other if 0 <= other < size else i


def swap_pairs(block, first):
    size, width = lax.axis_size("req"), lax.axis_size("tp")
    route = []
    for i in range(size):
        other = next_pair(i, first, size)
        for t in range(width):
            route.append((i * width + t, other * width + (t if other != i else t ^ 1)))
    return lax.ppermute(block, ("req", "tp"), route)


def alone(first):
    size = lax.axis_size("req")
    lonely = [i for i in range(size) if next_pair(i, first, size) == i]
    return sum([(lax.axis_index("req") == i).astype(jnp.int32) for i in lonely], jnp.int32(0))


def normalized(stream, gain):
    center = jnp.mean(stream, axis=-1, keepdims=True)
    moved = stream - center
    spread = jnp.mean(moved * moved, axis=-1, keepdims=True)
    return (moved * lax.rsqrt(spread + 1e-06) * gain).astype(jnp.bfloat16)


def dot(a, b, contract):
    return lax.dot_general(a, b, (contract, ((), ())), preferred_element_type=jnp.float32)


NN = ((1,), (0,))
NT = ((1,), (1,))


def row_of(gain_ref):
    return gain_ref[...].astype(jnp.float32).reshape(1, gain_ref.shape[0])


def vmem(mebibytes=60):
    return pltpu.CompilerParams(vmem_limit_bytes=mebibytes << 20)


def in_hbm(array):
    return pltpu.with_memory_space_constraint(array, pltpu.HBM)


def in_vmem(array):
    return pltpu.with_memory_space_constraint(array, pltpu.VMEM)


SCALARS = pl.BlockSpec(memory_space=pltpu.SMEM)
RESIDENT = pl.BlockSpec(memory_space=pltpu.VMEM)
ANYWHERE = pl.BlockSpec(memory_space=pl.ANY)


def load_mixer_kernel(place, *refs):
    wo_refs, we_refs, wr_refs, refs = refs[:4], refs[4:6], refs[6:8], refs[8:]
    wo, we, wr, sems = refs
    half = wo.shape[0] // 8
    copies = []
    for i in range(8):
        source = wo_refs[i // 2].at[place[0] ^ (i % 2)]
        copies.append((source, wo.at[pl.ds(i * half, half)]))
    copies += [(we_refs[i], we.at[i]) for i in range(2)]
    copies += [(wr_refs[i], wr.at[i]) for i in range(2)]
    copies = [pltpu.make_async_copy(*pair, sems.at[i]) for i, pair in enumerate(copies)]
    for copy in copies:
        copy.start()
    for copy in copies:
        copy.wait()


def load_mixer(place, wo, expand, reduce):
    half, width = wo[0].shape[1:]
    shapes = [(8 * half, width), (2,) + expand[0].shape, (2,) + reduce[0].shape]
    return pl.pallas_call(
        load_mixer_kernel,
        in_specs=[SCALARS] + [ANYWHERE] * 8,
        out_specs=[RESIDENT] * 3,
        out_shape=[pltpu.VMEM(shape, jnp.bfloat16) for shape in shapes],
        scratch_shapes=[pltpu.SemaphoreType.DMA((12,))],
        compiler_params=vmem(4),
        cost_estimate=pl.CostEstimate(flops=0, bytes_accessed=16_000_000, transcendentals=0),
        name="load_mixer",
    )(place, *[in_hbm(w) for w in (*wo, *expand, *reduce)])


def load_merge_kernel(own, other, both, sems):
    columns = own.shape[0]
    copies = [
        pltpu.make_async_copy(source, both.at[pl.ds(i * columns, columns)], sems.at[i])
        for i, source in enumerate((own, other))
    ]
    for copy in copies:
        copy.start()
    for copy in copies:
        copy.wait()


def load_merge(own, other):
    return pl.pallas_call(
        load_merge_kernel,
        in_specs=[ANYWHERE] * 2,
        out_specs=RESIDENT,
        out_shape=pltpu.VMEM((2 * own.shape[0], own.shape[1]), jnp.bfloat16),
        scratch_shapes=[pltpu.SemaphoreType.DMA((2,))],
        compiler_params=vmem(4),
        cost_estimate=pl.CostEstimate(flops=0, bytes_accessed=8_000_000, transcendentals=0),
        name="load_merge",
    )(in_hbm(own), in_hbm(other))


def project_kernel(parts, x_ref, segment_ref, gain_ref, *refs):
    w_refs, keep, send = refs[:parts], refs[parts], refs[parts + 1]
    first = lax.axis_index("req") % 2 == 0
    half = w_refs[0].shape[0] // 2
    rows = normalized(x_ref[...].astype(jnp.float32), row_of(gain_ref))
    for part in range(parts):
        out = dot(w_refs[part][...], rows, NT)
        low, high = out[:half], out[half:]
        at = slice(part * half, (part + 1) * half)
        keep[at, :] = jnp.where(first, low, high).astype(jnp.bfloat16)
        send[at, :] = jnp.where(first, high, low).astype(jnp.bfloat16)
    if parts > 1:
        number = segment_ref[...] + 1
        row = lax.broadcasted_iota(jnp.int32, (SEGMENT_ROWS, 1), 0)
        number = jnp.where(row == 0, number & 255, jnp.where(row == 1, number >> 8, 0))
        number = number.astype(jnp.float32).astype(jnp.bfloat16)
        keep[parts * half :, :] = number
        send[parts * half :, :] = number


def project(tokens, segments, gain, weight, parts, name):
    rows, width = tokens.shape
    half = weight.shape[0] // 6
    step = 256
    tall = len(parts) * half + (SEGMENT_ROWS if len(parts) > 1 else 0)
    return pl.pallas_call(
        functools.partial(project_kernel, len(parts)),
        grid=(rows // step,),
        in_specs=[
            pl.BlockSpec((step, width), lambda i: (i, 0)),
            pl.BlockSpec((1, step), lambda i: (0, i)),
            pl.BlockSpec(gain.shape, lambda i: (0,)),
        ]
        + [pl.BlockSpec((2 * half, width), lambda i, p=p: (p, 0)) for p in parts],
        out_specs=[pl.BlockSpec((tall, step), lambda i: (0, i))] * 2,
        out_shape=[pltpu.HBM((tall, rows), jnp.bfloat16)] * 2,
        compiler_params=vmem(),
        name=name,
    )(tokens, segments, gain, *[weight] * len(parts))


def numbers_of(ref, at):
    two = ref[:, at].astype(jnp.float32)
    return two[0:1] + 256.0 * two[1:2]


def largest_norm(first, second):
    squares = []
    for block in (first, second):
        block = block.astype(jnp.float32)
        squares.append(jnp.sum(block * block, axis=0, keepdims=True))
    return jnp.max(jnp.maximum(squares[0], squares[1]))


def attend_kernel(groups, blocks, flags, resumed, skip, last, place, *refs):
    q_refs, number_refs, refs = refs[:groups], refs[groups : 2 * groups], refs[2 * groups :]
    kv_refs, refs = refs[:blocks], refs[blocks:]
    if resumed:
        acc_in, peak_in, refs = refs[0], refs[1], refs[2:]
    if last:
        ctx_out, refs = refs[:groups], refs[groups:]
    else:
        acc_out, peak_out, refs = refs[0], refs[1], refs[2:]
    keys, values, columns, acc, peak, bounds, plain = refs
    tiles_of = kv_refs[0].shape[1] // TILE
    tiles = blocks * tiles_of
    tall = kv_refs[0].shape[0] - SEGMENT_ROWS
    steps_of = kv_refs[0].shape[1] // TILE
    j = pl.program_id(0)
    fresh = steps_of * groups - resumed

    @pl.when(j == 0)
    def _():
        for b in range(blocks):
            for t in range(tiles_of):
                n = b * tiles_of + t
                at = slice(t * TILE, (t + 1) * TILE)
                for h in range(2):
                    block = kv_refs[b][h * HD : (h + 1) * HD, at].astype(jnp.float32)
                    keys[n, h] = jnp.transpose(block).astype(jnp.bfloat16)
                    values[n, h, :HD] = kv_refs[b][(2 + h) * HD : (3 + h) * HD, at]
                    values[n, h, HD:] = jnp.ones((VROWS - HD, TILE), jnp.bfloat16)
                number = numbers_of(kv_refs[b].at[tall:], at)
                low, high = jnp.min(number), jnp.max(number)
                if b in flags:
                    low = jnp.where(place[flags[b]] == 1, -1.0, low)
                    high = jnp.where(place[flags[b]] == 1, -1.0, high)
                bounds[3 * n] = low
                bounds[3 * n + 1] = high
                bounds[3 * n + 2] = largest_norm(kv_refs[b][:HD, at], kv_refs[b][HD : 2 * HD, at])
                columns[n] = jnp.transpose(jnp.broadcast_to(number, (128, TILE)))

    def go_on():
        acc[...] = acc_in[0]
        peak[...] = peak_in[0]
        plain[0] = (jnp.max(jnp.abs(peak_in[0])) == 0.0).astype(jnp.int32)

    def start():
        acc[...] = jnp.zeros_like(acc)
        peak[...] = jnp.zeros_like(peak)
        plain[0] = 1

    if fresh:
        pl.when(j < fresh)(start)
    if resumed:
        pl.when(j >= fresh)(go_on)

    q_row = numbers_of(number_refs[0], slice(0, TILE))
    queries = q_refs[0][...]
    if groups > 1:
        q_row = jnp.where(j < steps_of, q_row, numbers_of(number_refs[1], slice(0, TILE)))
        queries = jnp.where(j < steps_of, queries, q_refs[1][...])
    q_low, q_high = jnp.min(q_row), jnp.max(q_row)
    q_norm = largest_norm(queries[:HD], queries[HD:])

    def scores_of(t, h, at, matches):
        scores = dot(keys[t, h], queries[h * HD : (h + 1) * HD, at], NN)
        return scores if matches is None else jnp.where(matches, scores, MASKED)

    def matches_of(t, at):
        column = columns[t]
        return jnp.concatenate([column] * (LANES // 128), axis=1) == q_row[:, at]

    units = [(slice(c, c + LANES), h) for c in range(0, TILE, LANES) for h in range(2)]

    def unshifted(t, masked):
        scores, probs, matches = {}, {}, None
        for i in range(len(units) + AHEAD + 1):
            if i < len(units):
                at, h = units[i]
                if masked and h == 0:
                    matches = matches_of(t, at)
                scores[i] = scores_of(t, h, at, matches)
            if 0 <= i - AHEAD < len(units):
                probs[i - AHEAD] = jnp.exp(scores.pop(i - AHEAD) * FACTOR).astype(jnp.bfloat16)
            if 0 <= i - AHEAD - 1 < len(units):
                at, h = units[i - AHEAD - 1]
                acc[h, :, at] += dot(values[t, h], probs.pop(i - AHEAD - 1), NN)

    def shifted_by_peak(t):
        for at, h in units:
            scores = scores_of(t, h, at, matches_of(t, at))
            old = jnp.where(acc[h, HD : HD + 1, at] > 0.0, peak[h : h + 1, at], START)
            new = jnp.maximum(old, jnp.max(scores, axis=0, keepdims=True))
            probs = jnp.exp((scores - new) * FACTOR).astype(jnp.bfloat16)
            shrink = jnp.exp((old - new) * FACTOR)
            peak[h : h + 1, at] = new
            acc[h, :, at] = acc[h, :, at] * shrink + dot(values[t, h], probs, NN)
        plain[0] = 0

    def visit(t, carry):
        k_low, k_high = bounds[3 * t], bounds[3 * t + 1]
        touches = (k_high >= q_low) & (k_low <= q_high)
        whole = (k_low == k_high) & (q_low == q_high)
        small = (plain[0] == 1) & (q_norm * bounds[3 * t + 2] <= SMALL * SMALL * HD)

        @pl.when(touches & small & whole)
        def _():
            unshifted(t, False)

        @pl.when(touches & small & jnp.logical_not(whole))
        def _():
            unshifted(t, True)

        @pl.when(touches & jnp.logical_not(small))
        def _():
            shifted_by_peak(t)

        return carry

    lax.fori_loop(jnp.where(j >= fresh, skip, 0), tiles, visit, 0)
    if last:

        def finish(out):
            for h in range(2):
                at = slice(h * HD, (h + 1) * HD)
                out[0, at, :] = (acc[h, :HD] / acc[h, HD : HD + 1]).astype(jnp.bfloat16)

        for g in range(groups):
            pl.when(j // steps_of == g)(functools.partial(finish, ctx_out[g]))
    else:
        acc_out[0] = acc[...]
        peak_out[0] = peak[...]


def attend(place, queries, numbers, key_values, name, flags={}, state=None, skip=0, last=False):
    half, rows = queries[0].shape
    groups, blocks = len(queries), len(key_values)
    steps_of = rows // TILE
    steps = groups * steps_of
    tiles = blocks * steps_of
    tall = numbers[0].shape[0] - SEGMENT_ROWS
    resumed = 0 if state is None else state[0].shape[0]
    whole = lambda a: pl.BlockSpec(a.shape, lambda j, s: (0,) * a.ndim)
    acc_shape, peak_shape = (2, VROWS, TILE), (2, TILE)
    q_spec = pl.BlockSpec((half, TILE), lambda j, s: (0, (j % steps_of) ^ s[1]))
    number_spec = pl.BlockSpec(
        (SEGMENT_ROWS, TILE), lambda j, s: (tall // SEGMENT_ROWS, (j % steps_of) ^ s[1])
    )
    in_specs = [q_spec] * groups + [number_spec] * groups + [whole(kv) for kv in key_values]
    operands = [*queries, *numbers, *key_values]
    if state is not None:
        behind = steps - resumed
        in_specs += [
            pl.BlockSpec((1,) + acc_shape, lambda j, s: (jnp.maximum(j - behind, 0), 0, 0, 0)),
            pl.BlockSpec((1,) + peak_shape, lambda j, s: (jnp.maximum(j - behind, 0), 0, 0)),
        ]
        operands += list(state)
    if last:
        out_specs = [
            pl.BlockSpec(
                (1, half, TILE), lambda j, s, g=g: (jnp.clip(j - g * steps_of, 0, steps_of - 1), 0, 0)
            )
            for g in range(groups)
        ]
        out_shape = [jax.ShapeDtypeStruct((steps_of, half, TILE), jnp.bfloat16)] * groups
    else:
        out_specs = [
            pl.BlockSpec((1,) + acc_shape, lambda j, s: (j, 0, 0, 0)),
            pl.BlockSpec((1,) + peak_shape, lambda j, s: (j, 0, 0)),
        ]
        out_shape = [
            jax.ShapeDtypeStruct((steps,) + acc_shape, jnp.float32),
            jax.ShapeDtypeStruct((steps,) + peak_shape, jnp.float32),
        ]
    return pl.pallas_call(
        functools.partial(attend_kernel, groups, blocks, flags, resumed, skip, last),
        grid_spec=pltpu.PrefetchScalarGridSpec(
            num_scalar_prefetch=1,
            grid=(steps,),
            in_specs=in_specs,
            out_specs=out_specs,
            scratch_shapes=[
                pltpu.VMEM((tiles, 2, TILE, HD), jnp.bfloat16),
                pltpu.VMEM((tiles, 2, VROWS, TILE), jnp.bfloat16),
                pltpu.VMEM((tiles, TILE, 128), jnp.float32),
                pltpu.VMEM(acc_shape, jnp.float32),
                pltpu.VMEM(peak_shape, jnp.float32),
                pltpu.SMEM((3 * tiles,), jnp.float32),
                pltpu.SMEM((1,), jnp.int32),
            ],
        ),
        out_shape=out_shape,
        compiler_params=vmem(),
        cost_estimate=pl.CostEstimate(flops=1_000_000, bytes_accessed=1_000_000, transcendentals=0),
        name=name,
    )(place, *operands)


def mixer_kernel(chunk, which, place, *refs):
    sources, refs = refs[:8], refs[8:]
    x_hbm, gain_ref, wo, we, wr, sent, kept, context, hidden, x, sem = refs
    rows = x.shape[0]
    half = sources[0].shape[1]
    width = we.shape[2]
    fetch = pltpu.make_async_copy(
        x_hbm.at[pl.ds(pl.multiple_of(place[2] + chunk * rows, rows), rows)], x, sem
    )
    fetch.start()
    lanes = slice(chunk * rows, (chunk + 1) * rows)
    for i in range(8):
        context[i * half : (i + 1) * half, :] = sources[i][which[i], :, lanes].astype(jnp.float32)
    inputs = jnp.transpose(context[...]).astype(jnp.bfloat16)
    fetch.wait()
    total = x[...].astype(jnp.float32) + dot(inputs, wo[...], NN)
    inputs = normalized(total, row_of(gain_ref))
    for i in range(2):
        inner = dot(inputs, we[i], NN)
        grown = 0.5 * inner * (1.0 + lax.erf(inner * (1.0 / math.sqrt(2.0))))
        hidden[:, i * width : (i + 1) * width] = grown.astype(jnp.bfloat16)
    out = dot(hidden[:, :width], wr[0], NN) + dot(hidden[:, width:], wr[1], NN)
    sent[...] = out.astype(jnp.bfloat16)
    kept[...] = total + out


def mixer(place, pieces, tokens, gain, weights, chunk, chunk_rows):
    width = tokens.shape[1]
    half = pieces[0][0].shape[1]
    hidden = weights[1].shape[2]
    return pl.pallas_call(
        functools.partial(mixer_kernel, chunk, [which for _, which in pieces]),
        in_specs=[SCALARS] + [RESIDENT] * 8 + [ANYWHERE] + [RESIDENT] * 4,
        out_specs=[RESIDENT] * 2,
        out_shape=[
            jax.ShapeDtypeStruct((chunk_rows, width), jnp.bfloat16),
            jax.ShapeDtypeStruct((chunk_rows, width), jnp.float32),
        ],
        scratch_shapes=[
            pltpu.VMEM((8 * half, chunk_rows), jnp.float32),
            pltpu.VMEM((chunk_rows, 2 * hidden), jnp.bfloat16),
            pltpu.VMEM((chunk_rows, width), jnp.bfloat16),
            pltpu.SemaphoreType.DMA,
        ],
        compiler_params=vmem(30),
        cost_estimate=pl.CostEstimate(
            flops=5_000_000_000, bytes_accessed=20_000_000, transcendentals=0
        ),
        name="mixer",
    )(place, *[source for source, _ in pieces], tokens, gain, *[in_vmem(w) for w in weights])


def one_hot_rows(index_ref, k, first, rows):
    column = jnp.transpose(jnp.broadcast_to(index_ref[k : k + 1, :], (128, index_ref.shape[1])))
    lanes = lax.broadcasted_iota(jnp.int32, (1, 128), 1)
    parts = [column == lanes + (first + 128 * n) for n in range(rows // 128)]
    return jnp.concatenate(parts, axis=1).astype(jnp.float32).astype(jnp.bfloat16)


def gather_kernel(place, index_ref, kept, received, gain_ref, merged):
    rows = kept.shape[0]
    final = normalized(kept[...] + received[...].astype(jnp.float32), row_of(gain_ref))
    for k in range(4):
        merged[k] = dot(one_hot_rows(index_ref, k, place[2], rows), final, NN).astype(jnp.bfloat16)


def gather(place, index, kept, received, gain):
    return pl.pallas_call(
        gather_kernel,
        in_specs=[SCALARS] + [RESIDENT] * 4,
        out_specs=RESIDENT,
        out_shape=pltpu.VMEM((4, index.shape[1], kept.shape[1]), jnp.bfloat16),
        compiler_params=vmem(20),
        cost_estimate=pl.CostEstimate(
            flops=1_000_000_000, bytes_accessed=5_000_000, transcendentals=0
        ),
        name="gather",
    )(place, index, kept, received, gain)


def merge_kernel(place, index_ref, kept, received, gain_ref, earlier, weights, own, other, parts):
    rows, width = kept.shape
    columns = own.shape[1]
    final = normalized(kept[...] + received[...].astype(jnp.float32), row_of(gain_ref))
    for k in range(4):
        part = dot(one_hot_rows(index_ref, k, place[3], rows), final, NN)
        part = part + earlier[k].astype(jnp.float32)
        parts[:, k * width : (k + 1) * width] = part.astype(jnp.bfloat16)
    total = dot(parts[...], weights[...], NT)
    own[...] = total[:, :columns]
    other[...] = total[:, columns:]


def merge(place, index, kept, received, gain, earlier, weights):
    merged_rows = index.shape[1]
    columns = weights.shape[0] // 2
    return pl.pallas_call(
        merge_kernel,
        in_specs=[SCALARS] + [RESIDENT] * 6,
        out_specs=[RESIDENT] * 2,
        out_shape=[jax.ShapeDtypeStruct((merged_rows, columns), jnp.float32)] * 2,
        scratch_shapes=[pltpu.VMEM((merged_rows, weights.shape[1]), jnp.bfloat16)],
        compiler_params=vmem(20),
        cost_estimate=pl.CostEstimate(
            flops=3_000_000_000, bytes_accessed=12_000_000, transcendentals=0
        ),
        name="merge",
    )(place, index, kept, received, gain, in_vmem(earlier), in_vmem(weights))


def place_kernel(position, own, received, out):
    feature = (own[...] + received[...]).astype(jnp.bfloat16)
    slots = lax.broadcasted_iota(jnp.int32, (out.shape[0], 1), 0)
    chosen = (slots == position[...]).astype(jnp.float32).astype(jnp.bfloat16)
    out[...] = dot(chosen, feature, NN).astype(jnp.bfloat16)


def body(
    tokens,
    segments,
    attend_gain,
    attend_weight,
    output_weight,
    mixer_gain,
    expand_weight,
    reduce_weight,
    output_gain,
    merge_weight,
    merge_index,
    owners,
):
    rows, width = tokens.shape
    head_width = attend_weight.shape[2]
    half = head_width // 2
    peers = lax.axis_size("req")
    req = lax.axis_index("req")
    par = req % 2
    core = lax.axis_index("tp") % 2

    chunk_rows = 256
    per_core = rows // 2
    place = jnp.stack([par, core, core * per_core, core * per_core + chunk_rows, alone(0), alone(1)])
    tie = lax.optimization_barrier
    with jax.named_scope("weights"):
        wo_own = output_weight.reshape(2, half, width)
        wo_core = swap(wo_own, "tp", 1)
        expand_other = swap(expand_weight, "tp", 1)

    with jax.named_scope("project"):
        weight = jnp.transpose(attend_weight, (1, 2, 0)).reshape(6 * half, width)
        numbers = segments[None, :]
        kv_own, kv_send = project(tokens, numbers, attend_gain, weight, (1, 2), "project_keys")
        kv_own, kv_send, expand_other, wo_core = tie((kv_own, kv_send, expand_other, wo_core))

    with jax.named_scope("exchange_keys"):
        kv_peer = swap(kv_send, "req", 1)
        kv_even = swap_pairs(kv_own, 0)
        kv_odd = swap_pairs(kv_own, 1)
        wo_across = swap(wo_own, "tp", 2)
        q_own, q_send = project(tokens, numbers, attend_gain, weight, (0,), "project_queries")
        q_peer = swap(q_send, "req", 1)
        state = attend(place, [q_own], [kv_own], [kv_own], "attend_own")
        kv_odd, kv_even, kv_peer, state, wo_across, late_reduce, late_wo = tie(
            (kv_odd, kv_even, kv_peer, state, wo_across, reduce_weight, wo_core)
        )
        kv_even_peer = swap_pairs(kv_peer, 0)
        kv_odd_peer = swap_pairs(kv_peer, 1)
        reduce_other = swap(late_reduce, "tp", 1)
        wo_both = swap(late_wo, "tp", 2)

    with jax.named_scope("slots"):
        capacity = 2 * merge_index.shape[0] // peers
        target = owners[:, 0]
        choose = (target[:, None] == jnp.arange(peers, dtype=jnp.int32)[None, :]).astype(jnp.int32)
        slot = jnp.sum((jnp.cumsum(choose, axis=0) - 1) * choose, axis=1)
        position = (target * capacity + slot)[None, :]
        index = jnp.transpose(merge_index) - req * rows

        q_peer, position, index = tie((q_peer, position, index))

    with jax.named_scope("attention"):
        queries, numbers = [q_peer, q_own], [kv_peer, kv_own]
        near = [kv_own, kv_peer, kv_even, kv_odd]
        state = attend(place, queries, numbers, near, "attend_near", {2: 4, 3: 5}, state, rows // TILE)
        state, kv_even_peer, kv_odd_peer, reduce_other, wo_both = tie(
            (state, kv_even_peer, kv_odd_peer, reduce_other, wo_both)
        )
        far = [kv_even_peer, kv_odd_peer]
        for_peer, context = attend(
            place, queries, numbers, far, "attend_far", {0: 4, 1: 5}, state, last=True
        )

    with jax.named_scope("exchange_context"):
        late_wo, context, for_peer = tie((wo_own, context, for_peer))
        from_peer = swap(for_peer, "req", 1)
        weights = load_mixer(
            place,
            [late_wo, wo_core, wo_across, wo_both],
            [expand_weight, expand_other],
            [reduce_weight, reduce_other],
        )
        from_peer, weights = tie((from_peer, weights))
        sides = []
        for source in (context, from_peer):
            across = swap(source, "tp", 2)
            sides.append(
                [(source, 0), (swap(source, "tp", 1), 1), (across, 0), (swap(across, "tp", 1), 1)]
            )
        pieces = [sides[h][t] for t in range(4) for h in range(2)]

    with jax.named_scope("mixer"):
        sent, kept, received = [], [], []
        for chunk in range(2):
            s, k = mixer(place, pieces, tokens, mixer_gain, weights, chunk, chunk_rows)
            sent.append(s)
            kept.append(k)
            received.append(swap(s, "tp", 2))
            if chunk == 0:
                merge_own, _ = tie((jnp.transpose(merge_weight), s))
                merge_other = swap(merge_own, "tp", 1)

    with jax.named_scope("merge"):
        merge_other, position, index, _ = tie((merge_other, position, index, sent[1]))
        weights = load_merge(merge_own, merge_other)
        earlier = gather(place, index, kept[0], received[0], output_gain)
        weights, earlier, last, position = tie((weights, earlier, received[1], position))
        own, other = merge(place, index, kept[1], last, output_gain, earlier, weights)
        other = swap(other, "tp", 1)

    with jax.named_scope("place"):
        columns = own.shape[1]
        outgoing = pl.pallas_call(
            place_kernel,
            in_specs=[RESIDENT] * 3,
            out_specs=RESIDENT,
            out_shape=jax.ShapeDtypeStruct((peers * capacity, columns), jnp.bfloat16),
            compiler_params=vmem(10),
            name="place",
        )(position, in_vmem(own), in_vmem(other))
        outgoing = outgoing.reshape(peers, capacity, columns)
        arrived = lax.all_to_all(outgoing, "req", split_axis=0, concat_axis=0, tiled=True)
    return arrived.reshape(1, peers, capacity, columns)


def solution(mesh):
    placed = (
        P("req", None),
        P("req"),
        P(),
        P(None, None, "tp"),
        P("tp", None),
        P(),
        P(None, "tp"),
        P("tp", None),
        P(),
        P(None, "tp"),
        P("req", None),
        P("req", None),
    )
    return jax.shard_map(
        body, mesh=mesh, in_specs=placed, out_specs=P("req", None, None, "tp"), check_vma=False
    )
```

```python
import functools
import math

import jax
import jax.numpy as jnp
from jax import lax
from jax.experimental import pallas as pl
from jax.experimental.pallas import tpu as pltpu
from jax.sharding import PartitionSpec as P

HD = 80
TILE = 512
MASKED = -1e30
START = -1e28
FACTOR = 1.0 / math.sqrt(HD)
SEGMENT_ROWS = 16
VROWS = 96
LANES = 256
AHEAD = 2
SMALL = 72.0


def swap(block, axis, flip):
    return lax.ppermute(block, axis, [(i, i ^ flip) for i in range(lax.axis_size(axis))])


def next_pair(i, first, size):
    other = i + 2 if i // 2 % 2 == first else i - 2
    return other if 0 <= other < size else i


def swap_pairs(block, first):
    size, width = lax.axis_size("req"), lax.axis_size("tp")
    route = []
    for i in range(size):
        other = next_pair(i, first, size)
        for t in range(width):
            route.append((i * width + t, other * width + (t if other != i else t ^ 1)))
    return lax.ppermute(block, ("req", "tp"), route)


def alone(first):
    size = lax.axis_size("req")
    lonely = [i for i in range(size) if next_pair(i, first, size) == i]
    return sum([(lax.axis_index("req") == i).astype(jnp.int32) for i in lonely], jnp.int32(0))


def normalized(stream, gain):
    center = jnp.mean(stream, axis=-1, keepdims=True)
    moved = stream - center
    spread = jnp.mean(moved * moved, axis=-1, keepdims=True)
    return (moved * lax.rsqrt(spread + 1e-06) * gain).astype(jnp.bfloat16)


def dot(a, b, contract):
    return lax.dot_general(a, b, (contract, ((), ())), preferred_element_type=jnp.float32)


NN = ((1,), (0,))
NT = ((1,), (1,))


def row_of(gain_ref):
    return gain_ref[...].astype(jnp.float32).reshape(1, gain_ref.shape[0])


def vmem(mebibytes=60):
    return pltpu.CompilerParams(vmem_limit_bytes=mebibytes << 20)


def in_hbm(array):
    return pltpu.with_memory_space_constraint(array, pltpu.HBM)


def in_vmem(array):
    return pltpu.with_memory_space_constraint(array, pltpu.VMEM)


SCALARS = pl.BlockSpec(memory_space=pltpu.SMEM)
RESIDENT = pl.BlockSpec(memory_space=pltpu.VMEM)
ANYWHERE = pl.BlockSpec(memory_space=pl.ANY)


def load_mixer_kernel(place, *refs):
    wo_refs, we_refs, wr_refs, refs = refs[:4], refs[4:6], refs[6:8], refs[8:]
    wo, we, wr, sems = refs
    half = wo.shape[0] // 8
    copies = []
    for i in range(8):
        source = wo_refs[i // 2].at[place[0] ^ (i % 2)]
        copies.append((source, wo.at[pl.ds(i * half, half)]))
    copies += [(we_refs[i], we.at[i]) for i in range(2)]
    copies += [(wr_refs[i], wr.at[i]) for i in range(2)]
    copies = [pltpu.make_async_copy(*pair, sems.at[i]) for i, pair in enumerate(copies)]
    for copy in copies:
        copy.start()
    for copy in copies:
        copy.wait()


def load_mixer(place, wo, expand, reduce):
    half, width = wo[0].shape[1:]
    shapes = [(8 * half, width), (2,) + expand[0].shape, (2,) + reduce[0].shape]
    return pl.pallas_call(
        load_mixer_kernel,
        in_specs=[SCALARS] + [ANYWHERE] * 8,
        out_specs=[RESIDENT] * 3,
        out_shape=[pltpu.VMEM(shape, jnp.bfloat16) for shape in shapes],
        scratch_shapes=[pltpu.SemaphoreType.DMA((12,))],
        compiler_params=vmem(4),
        cost_estimate=pl.CostEstimate(flops=0, bytes_accessed=16_000_000, transcendentals=0),
        name="load_mixer",
    )(place, *[in_hbm(w) for w in (*wo, *expand, *reduce)])


def load_merge_kernel(own, other, both, sems):
    columns = own.shape[0]
    copies = [
        pltpu.make_async_copy(source, both.at[pl.ds(i * columns, columns)], sems.at[i])
        for i, source in enumerate((own, other))
    ]
    for copy in copies:
        copy.start()
    for copy in copies:
        copy.wait()


def load_merge(own, other):
    return pl.pallas_call(
        load_merge_kernel,
        in_specs=[ANYWHERE] * 2,
        out_specs=RESIDENT,
        out_shape=pltpu.VMEM((2 * own.shape[0], own.shape[1]), jnp.bfloat16),
        scratch_shapes=[pltpu.SemaphoreType.DMA((2,))],
        compiler_params=vmem(4),
        cost_estimate=pl.CostEstimate(flops=0, bytes_accessed=8_000_000, transcendentals=0),
        name="load_merge",
    )(in_hbm(own), in_hbm(other))


def project_kernel(parts, x_ref, segment_ref, gain_ref, *refs):
    w_refs, keep, send = refs[:parts], refs[parts], refs[parts + 1]
    first = lax.axis_index("req") % 2 == 0
    half = w_refs[0].shape[0] // 2
    rows = normalized(x_ref[...].astype(jnp.float32), row_of(gain_ref))
    for part in range(parts):
        out = dot(w_refs[part][...], rows, NT)
        low, high = out[:half], out[half:]
        at = slice(part * half, (part + 1) * half)
        keep[at, :] = jnp.where(first, low, high).astype(jnp.bfloat16)
        send[at, :] = jnp.where(first, high, low).astype(jnp.bfloat16)
    if parts > 1:
        number = segment_ref[...] + 1
        row = lax.broadcasted_iota(jnp.int32, (SEGMENT_ROWS, 1), 0)
        number = jnp.where(row == 0, number & 255, jnp.where(row == 1, number >> 8, 0))
        number = number.astype(jnp.float32).astype(jnp.bfloat16)
        keep[parts * half :, :] = number
        send[parts * half :, :] = number


def project(tokens, segments, gain, weight, parts, name):
    rows, width = tokens.shape
    half = weight.shape[0] // 6
    step = 256
    tall = len(parts) * half + (SEGMENT_ROWS if len(parts) > 1 else 0)
    return pl.pallas_call(
        functools.partial(project_kernel, len(parts)),
        grid=(rows // step,),
        in_specs=[
            pl.BlockSpec((step, width), lambda i: (i, 0)),
            pl.BlockSpec((1, step), lambda i: (0, i)),
            pl.BlockSpec(gain.shape, lambda i: (0,)),
        ]
        + [pl.BlockSpec((2 * half, width), lambda i, p=p: (p, 0)) for p in parts],
        out_specs=[pl.BlockSpec((tall, step), lambda i: (0, i))] * 2,
        out_shape=[pltpu.HBM((tall, rows), jnp.bfloat16)] * 2,
        compiler_params=vmem(),
        name=name,
    )(tokens, segments, gain, *[weight] * len(parts))


def numbers_of(ref, at):
    two = ref[:, at].astype(jnp.float32)
    return two[0:1] + 256.0 * two[1:2]


def largest_norm(first, second):
    squares = []
    for block in (first, second):
        block = block.astype(jnp.float32)
        squares.append(jnp.sum(block * block, axis=0, keepdims=True))
    return jnp.max(jnp.maximum(squares[0], squares[1]))


def attend_kernel(groups, blocks, flags, resumed, skip, last, place, *refs):
    q_refs, number_refs, refs = refs[:groups], refs[groups : 2 * groups], refs[2 * groups :]
    kv_refs, refs = refs[:blocks], refs[blocks:]
    if resumed:
        acc_in, peak_in, refs = refs[0], refs[1], refs[2:]
    if last:
        ctx_out, refs = refs[:groups], refs[groups:]
    else:
        acc_out, peak_out, refs = refs[0], refs[1], refs[2:]
    keys, values, columns, acc, peak, bounds, plain = refs
    tiles_of = kv_refs[0].shape[1] // TILE
    tiles = blocks * tiles_of
    tall = kv_refs[0].shape[0] - SEGMENT_ROWS
    steps_of = kv_refs[0].shape[1] // TILE
    j = pl.program_id(0)
    fresh = steps_of * groups - resumed

    @pl.when(j == 0)
    def _():
        for b in range(blocks):
            for t in range(tiles_of):
                n = b * tiles_of + t
                at = slice(t * TILE, (t + 1) * TILE)
                for h in range(2):
                    block = kv_refs[b][h * HD : (h + 1) * HD, at].astype(jnp.float32)
                    keys[n, h] = jnp.transpose(block).astype(jnp.bfloat16)
                    values[n, h, :HD] = kv_refs[b][(2 + h) * HD : (3 + h) * HD, at]
                    values[n, h, HD:] = jnp.ones((VROWS - HD, TILE), jnp.bfloat16)
                number = numbers_of(kv_refs[b].at[tall:], at)
                low, high = jnp.min(number), jnp.max(number)
                if b in flags:
                    low = jnp.where(place[flags[b]] == 1, -1.0, low)
                    high = jnp.where(place[flags[b]] == 1, -1.0, high)
                bounds[3 * n] = low
                bounds[3 * n + 1] = high
                bounds[3 * n + 2] = largest_norm(kv_refs[b][:HD, at], kv_refs[b][HD : 2 * HD, at])
                columns[n] = jnp.transpose(jnp.broadcast_to(number, (128, TILE)))

    def go_on():
        acc[...] = acc_in[0]
        peak[...] = peak_in[0]
        plain[0] = (jnp.max(jnp.abs(peak_in[0])) == 0.0).astype(jnp.int32)

    def start():
        acc[...] = jnp.zeros_like(acc)
        peak[...] = jnp.zeros_like(peak)
        plain[0] = 1

    if fresh:
        pl.when(j < fresh)(start)
    if resumed:
        pl.when(j >= fresh)(go_on)

    q_row = numbers_of(number_refs[0], slice(0, TILE))
    queries = q_refs[0][...]
    if groups > 1:
        q_row = jnp.where(j < steps_of, q_row, numbers_of(number_refs[1], slice(0, TILE)))
        queries = jnp.where(j < steps_of, queries, q_refs[1][...])
    q_low, q_high = jnp.min(q_row), jnp.max(q_row)
    q_norm = largest_norm(queries[:HD], queries[HD:])

    def scores_of(t, h, at, matches):
        scores = dot(keys[t, h], queries[h * HD : (h + 1) * HD, at], NN)
        return scores if matches is None else jnp.where(matches, scores, MASKED)

    def matches_of(t, at):
        column = columns[t]
        return jnp.concatenate([column] * (LANES // 128), axis=1) == q_row[:, at]

    units = [(slice(c, c + LANES), h) for c in range(0, TILE, LANES) for h in range(2)]

    def unshifted(t, masked):
        scores, probs, matches = {}, {}, None
        for i in range(len(units) + AHEAD + 1):
            if i < len(units):
                at, h = units[i]
                if masked and h == 0:
                    matches = matches_of(t, at)
                scores[i] = scores_of(t, h, at, matches)
            if 0 <= i - AHEAD < len(units):
                probs[i - AHEAD] = jnp.exp(scores.pop(i - AHEAD) * FACTOR).astype(jnp.bfloat16)
            if 0 <= i - AHEAD - 1 < len(units):
                at, h = units[i - AHEAD - 1]
                acc[h, :, at] += dot(values[t, h], probs.pop(i - AHEAD - 1), NN)

    def shifted_by_peak(t):
        for at, h in units:
            scores = scores_of(t, h, at, matches_of(t, at))
            old = jnp.where(acc[h, HD : HD + 1, at] > 0.0, peak[h : h + 1, at], START)
            new = jnp.maximum(old, jnp.max(scores, axis=0, keepdims=True))
            probs = jnp.exp((scores - new) * FACTOR).astype(jnp.bfloat16)
            shrink = jnp.exp((old - new) * FACTOR)
            peak[h : h + 1, at] = new
            acc[h, :, at] = acc[h, :, at] * shrink + dot(values[t, h], probs, NN)
        plain[0] = 0

    def visit(t, carry):
        k_low, k_high = bounds[3 * t], bounds[3 * t + 1]
        touches = (k_high >= q_low) & (k_low <= q_high)
        whole = (k_low == k_high) & (q_low == q_high)
        small = (plain[0] == 1) & (q_norm * bounds[3 * t + 2] <= SMALL * SMALL * HD)

        @pl.when(touches & small & whole)
        def _():
            unshifted(t, False)

        @pl.when(touches & small & jnp.logical_not(whole))
        def _():
            unshifted(t, True)

        @pl.when(touches & jnp.logical_not(small))
        def _():
            shifted_by_peak(t)

        return carry

    lax.fori_loop(jnp.where(j >= fresh, skip, 0), tiles, visit, 0)
    if last:

        def finish(out):
            for h in range(2):
                at = slice(h * HD, (h + 1) * HD)
                out[0, at, :] = (acc[h, :HD] / acc[h, HD : HD + 1]).astype(jnp.bfloat16)

        for g in range(groups):
            pl.when(j // steps_of == g)(functools.partial(finish, ctx_out[g]))
    else:
        acc_out[0] = acc[...]
        peak_out[0] = peak[...]


def attend(place, queries, numbers, key_values, name, flags={}, state=None, skip=0, last=False):
    half, rows = queries[0].shape
    groups, blocks = len(queries), len(key_values)
    steps_of = rows // TILE
    steps = groups * steps_of
    tiles = blocks * steps_of
    tall = numbers[0].shape[0] - SEGMENT_ROWS
    resumed = 0 if state is None else state[0].shape[0]
    whole = lambda a: pl.BlockSpec(a.shape, lambda j, s: (0,) * a.ndim)
    acc_shape, peak_shape = (2, VROWS, TILE), (2, TILE)
    q_spec = pl.BlockSpec((half, TILE), lambda j, s: (0, (j % steps_of) ^ s[1]))
    number_spec = pl.BlockSpec(
        (SEGMENT_ROWS, TILE), lambda j, s: (tall // SEGMENT_ROWS, (j % steps_of) ^ s[1])
    )
    in_specs = [q_spec] * groups + [number_spec] * groups + [whole(kv) for kv in key_values]
    operands = [*queries, *numbers, *key_values]
    if state is not None:
        behind = steps - resumed
        in_specs += [
            pl.BlockSpec((1,) + acc_shape, lambda j, s: (jnp.maximum(j - behind, 0), 0, 0, 0)),
            pl.BlockSpec((1,) + peak_shape, lambda j, s: (jnp.maximum(j - behind, 0), 0, 0)),
        ]
        operands += list(state)
    if last:
        out_specs = [
            pl.BlockSpec(
                (1, half, TILE), lambda j, s, g=g: (jnp.clip(j - g * steps_of, 0, steps_of - 1), 0, 0)
            )
            for g in range(groups)
        ]
        out_shape = [jax.ShapeDtypeStruct((steps_of, half, TILE), jnp.bfloat16)] * groups
    else:
        out_specs = [
            pl.BlockSpec((1,) + acc_shape, lambda j, s: (j, 0, 0, 0)),
            pl.BlockSpec((1,) + peak_shape, lambda j, s: (j, 0, 0)),
        ]
        out_shape = [
            jax.ShapeDtypeStruct((steps,) + acc_shape, jnp.float32),
            jax.ShapeDtypeStruct((steps,) + peak_shape, jnp.float32),
        ]
    return pl.pallas_call(
        functools.partial(attend_kernel, groups, blocks, flags, resumed, skip, last),
        grid_spec=pltpu.PrefetchScalarGridSpec(
            num_scalar_prefetch=1,
            grid=(steps,),
            in_specs=in_specs,
            out_specs=out_specs,
            scratch_shapes=[
                pltpu.VMEM((tiles, 2, TILE, HD), jnp.bfloat16),
                pltpu.VMEM((tiles, 2, VROWS, TILE), jnp.bfloat16),
                pltpu.VMEM((tiles, TILE, 128), jnp.float32),
                pltpu.VMEM(acc_shape, jnp.float32),
                pltpu.VMEM(peak_shape, jnp.float32),
                pltpu.SMEM((3 * tiles,), jnp.float32),
                pltpu.SMEM((1,), jnp.int32),
            ],
        ),
        out_shape=out_shape,
        compiler_params=vmem(),
        cost_estimate=pl.CostEstimate(flops=1_000_000, bytes_accessed=1_000_000, transcendentals=0),
        name=name,
    )(place, *operands)


def mixer_kernel(first, which, place, *refs):
    sources, refs = refs[:8], refs[8:]
    x_hbm, gain_ref, wo, we, wr, sent, kept, context, hidden, x, sem = refs
    rows = x.shape[0]
    half = sources[0].shape[1]
    width = we.shape[2]
    fetch = pltpu.make_async_copy(
        x_hbm.at[pl.ds(pl.multiple_of(place[2] + first, 128), rows)], x, sem
    )
    fetch.start()
    lanes = slice(first, first + rows)
    for i in range(8):
        context[i * half : (i + 1) * half, :] = sources[i][which[i], :, lanes].astype(jnp.float32)
    inputs = jnp.transpose(context[...]).astype(jnp.bfloat16)
    fetch.wait()
    total = x[...].astype(jnp.float32) + dot(inputs, wo[...], NN)
    inputs = normalized(total, row_of(gain_ref))
    for i in range(2):
        inner = dot(inputs, we[i], NN)
        grown = 0.5 * inner * (1.0 + lax.erf(inner * (1.0 / math.sqrt(2.0))))
        hidden[:, i * width : (i + 1) * width] = grown.astype(jnp.bfloat16)
    out = dot(hidden[:, :width], wr[0], NN) + dot(hidden[:, width:], wr[1], NN)
    sent[...] = out.astype(jnp.bfloat16)
    kept[...] = total + out


def mixer(place, pieces, tokens, gain, weights, first, chunk_rows):
    width = tokens.shape[1]
    half = pieces[0][0].shape[1]
    hidden = weights[1].shape[2]
    return pl.pallas_call(
        functools.partial(mixer_kernel, first, [which for _, which in pieces]),
        in_specs=[SCALARS] + [RESIDENT] * 8 + [ANYWHERE] + [RESIDENT] * 4,
        out_specs=[RESIDENT] * 2,
        out_shape=[
            jax.ShapeDtypeStruct((chunk_rows, width), jnp.bfloat16),
            jax.ShapeDtypeStruct((chunk_rows, width), jnp.float32),
        ],
        scratch_shapes=[
            pltpu.VMEM((8 * half, chunk_rows), jnp.float32),
            pltpu.VMEM((chunk_rows, 2 * hidden), jnp.bfloat16),
            pltpu.VMEM((chunk_rows, width), jnp.bfloat16),
            pltpu.SemaphoreType.DMA,
        ],
        compiler_params=vmem(30),
        cost_estimate=pl.CostEstimate(
            flops=5_000_000_000, bytes_accessed=20_000_000, transcendentals=0
        ),
        name="mixer",
    )(place, *[source for source, _ in pieces], tokens, gain, *[in_vmem(w) for w in weights])


def one_hot_rows(index_ref, k, first, rows):
    column = jnp.transpose(jnp.broadcast_to(index_ref[k : k + 1, :], (128, index_ref.shape[1])))
    lanes = lax.broadcasted_iota(jnp.int32, (1, 128), 1)
    parts = [column == lanes + (first + 128 * n) for n in range(rows // 128)]
    return jnp.concatenate(parts, axis=1).astype(jnp.float32).astype(jnp.bfloat16)


def gather_kernel(first, place, index_ref, kept, received, gain_ref, *refs):
    merged = refs[-1]
    rows = kept.shape[0]
    final = normalized(kept[...] + received[...].astype(jnp.float32), row_of(gain_ref))
    for k in range(4):
        part = dot(one_hot_rows(index_ref, k, place[2] + first, rows), final, NN)
        if len(refs) > 1:
            part = part + refs[0][k].astype(jnp.float32)
        merged[k] = part.astype(jnp.bfloat16)


def gather(place, index, kept, received, gain, first, earlier):
    return pl.pallas_call(
        functools.partial(gather_kernel, first),
        in_specs=[SCALARS] + [RESIDENT] * (4 + len(earlier)),
        out_specs=RESIDENT,
        out_shape=pltpu.VMEM((4, index.shape[1], kept.shape[1]), jnp.bfloat16),
        compiler_params=vmem(20),
        cost_estimate=pl.CostEstimate(
            flops=1_000_000_000, bytes_accessed=5_000_000, transcendentals=0
        ),
        name="gather",
    )(place, index, kept, received, gain, *[in_vmem(a) for a in earlier])


def merge_kernel(
    first, place, index_ref, kept, received, gain_ref, earlier, weights, own, other, parts
):
    rows, width = kept.shape
    columns = own.shape[1]
    final = normalized(kept[...] + received[...].astype(jnp.float32), row_of(gain_ref))
    for k in range(4):
        part = dot(one_hot_rows(index_ref, k, place[2] + first, rows), final, NN)
        part = part + earlier[k].astype(jnp.float32)
        parts[:, k * width : (k + 1) * width] = part.astype(jnp.bfloat16)
    total = dot(parts[...], weights[...], NT)
    own[...] = total[:, :columns]
    other[...] = total[:, columns:]


def merge(place, index, kept, received, gain, first, earlier, weights):
    merged_rows = index.shape[1]
    columns = weights.shape[0] // 2
    return pl.pallas_call(
        functools.partial(merge_kernel, first),
        in_specs=[SCALARS] + [RESIDENT] * 6,
        out_specs=[RESIDENT] * 2,
        out_shape=[jax.ShapeDtypeStruct((merged_rows, columns), jnp.float32)] * 2,
        scratch_shapes=[pltpu.VMEM((merged_rows, weights.shape[1]), jnp.bfloat16)],
        compiler_params=vmem(20),
        cost_estimate=pl.CostEstimate(
            flops=3_000_000_000, bytes_accessed=12_000_000, transcendentals=0
        ),
        name="merge",
    )(place, index, kept, received, gain, in_vmem(earlier), in_vmem(weights))


def place_kernel(position, own, received, out):
    feature = (own[...] + received[...]).astype(jnp.bfloat16)
    slots = lax.broadcasted_iota(jnp.int32, (out.shape[0], 1), 0)
    chosen = (slots == position[...]).astype(jnp.float32).astype(jnp.bfloat16)
    out[...] = dot(chosen, feature, NN).astype(jnp.bfloat16)


def body(
    tokens,
    segments,
    attend_gain,
    attend_weight,
    output_weight,
    mixer_gain,
    expand_weight,
    reduce_weight,
    output_gain,
    merge_weight,
    merge_index,
    owners,
):
    rows, width = tokens.shape
    head_width = attend_weight.shape[2]
    half = head_width // 2
    peers = lax.axis_size("req")
    req = lax.axis_index("req")
    par = req % 2
    core = lax.axis_index("tp") % 2

    per_core = rows // 2
    chunks = [(0, 128), (128, per_core - 256), (per_core - 128, 128)]
    place = jnp.stack([par, core, core * per_core, req, alone(0), alone(1)])
    tie = lax.optimization_barrier
    with jax.named_scope("weights"):
        wo_own = output_weight.reshape(2, half, width)
        wo_core = swap(wo_own, "tp", 1)
        expand_other = swap(expand_weight, "tp", 1)

    with jax.named_scope("project"):
        weight = jnp.transpose(attend_weight, (1, 2, 0)).reshape(6 * half, width)
        numbers = segments[None, :]
        kv_own, kv_send = project(tokens, numbers, attend_gain, weight, (1, 2), "project_keys")
        kv_own, kv_send, expand_other, wo_core = tie((kv_own, kv_send, expand_other, wo_core))

    with jax.named_scope("exchange_keys"):
        kv_peer = swap(kv_send, "req", 1)
        kv_even = swap_pairs(kv_own, 0)
        kv_odd = swap_pairs(kv_own, 1)
        wo_across = swap(wo_own, "tp", 2)
        q_own, q_send = project(tokens, numbers, attend_gain, weight, (0,), "project_queries")
        q_peer = swap(q_send, "req", 1)
        state = attend(place, [q_own], [kv_own], [kv_own], "attend_own")
        kv_odd, kv_even, kv_peer, state, wo_across, late_reduce, late_wo = tie(
            (kv_odd, kv_even, kv_peer, state, wo_across, reduce_weight, wo_core)
        )
        kv_even_peer = swap_pairs(kv_peer, 0)
        kv_odd_peer = swap_pairs(kv_peer, 1)
        reduce_other = swap(late_reduce, "tp", 1)
        wo_both = swap(late_wo, "tp", 2)

    with jax.named_scope("slots"):
        capacity = 2 * merge_index.shape[0] // peers
        target = owners[:, 0]
        choose = (target[:, None] == jnp.arange(peers, dtype=jnp.int32)[None, :]).astype(jnp.int32)
        slot = jnp.sum((jnp.cumsum(choose, axis=0) - 1) * choose, axis=1)
        position = (target * capacity + slot)[None, :]
        index = jnp.transpose(merge_index) - req * rows

        q_peer, position, index = tie((q_peer, position, index))

    with jax.named_scope("attention"):
        queries, numbers = [q_peer, q_own], [kv_peer, kv_own]
        near = [kv_own, kv_peer, kv_even, kv_odd]
        state = attend(place, queries, numbers, near, "attend_near", {2: 4, 3: 5}, state, rows // TILE)
        state, kv_even_peer, kv_odd_peer, reduce_other, wo_both = tie(
            (state, kv_even_peer, kv_odd_peer, reduce_other, wo_both)
        )
        far = [kv_even_peer, kv_odd_peer]
        for_peer, context = attend(
            place, queries, numbers, far, "attend_far", {0: 4, 1: 5}, state, last=True
        )

    with jax.named_scope("exchange_context"):
        late_wo, context, for_peer = tie((wo_own, context, for_peer))
        from_peer = swap(for_peer, "req", 1)
        weights = load_mixer(
            place,
            [late_wo, wo_core, wo_across, wo_both],
            [expand_weight, expand_other],
            [reduce_weight, reduce_other],
        )
        from_peer, weights = tie((from_peer, weights))
        sides = []
        for source in (context, from_peer):
            across = swap(source, "tp", 2)
            sides.append(
                [(source, 0), (swap(source, "tp", 1), 1), (across, 0), (swap(across, "tp", 1), 1)]
            )
        pieces = [sides[h][t] for t in range(4) for h in range(2)]

    with jax.named_scope("mixer"):
        sent, kept, received = [], [], []
        for first, size in chunks:
            s, k = mixer(place, pieces, tokens, mixer_gain, weights, first, size)
            sent.append(s)
            kept.append(k)
            received.append(swap(s, "tp", 2))
            if first == 0:
                merge_own, _ = tie((jnp.transpose(merge_weight), s))
                merge_other = swap(merge_own, "tp", 1)

    with jax.named_scope("merge"):
        merge_other, position, index, _ = tie((merge_other, position, index, sent[-1]))
        weights = load_merge(merge_own, merge_other)
        earlier = []
        for c, (first, _) in enumerate(chunks[:-1]):
            earlier = [
                gather(place, index, kept[c], received[c], output_gain, first, earlier)
            ]
        weights, earlier, last, position = tie((weights, earlier[0], received[-1], position))
        first = chunks[-1][0]
        own, other = merge(
            place, index, kept[-1], last, output_gain, first, earlier, weights
        )
        other = swap(other, "tp", 1)

    with jax.named_scope("place"):
        columns = own.shape[1]
        outgoing = pl.pallas_call(
            place_kernel,
            in_specs=[RESIDENT] * 3,
            out_specs=RESIDENT,
            out_shape=jax.ShapeDtypeStruct((peers * capacity, columns), jnp.bfloat16),
            compiler_params=vmem(10),
            name="place",
        )(position, in_vmem(own), in_vmem(other))
        outgoing = outgoing.reshape(peers, capacity, columns)
        arrived = lax.all_to_all(outgoing, "req", split_axis=0, concat_axis=0, tiled=True)
    return arrived.reshape(1, peers, capacity, columns)


def solution(mesh):
    placed = (
        P("req", None),
        P("req"),
        P(),
        P(None, None, "tp"),
        P("tp", None),
        P(),
        P(None, "tp"),
        P("tp", None),
        P(),
        P(None, "tp"),
        P("req", None),
        P("req", None),
    )
    return jax.shard_map(
        body, mesh=mesh, in_specs=placed, out_specs=P("req", None, None, "tp"), check_vma=False
    )
```

```python
import functools
import math

import jax
import jax.numpy as jnp
from jax import lax
from jax.experimental import pallas as pl
from jax.experimental.pallas import tpu as pltpu
from jax.sharding import PartitionSpec as P

HD = 80
TILE = 512
MASKED = -1e30
START = -1e28
FACTOR = 1.0 / math.sqrt(HD)
SEGMENT_ROWS = 16
VROWS = 96
LANES = 256
AHEAD = 2
SMALL = 72.0


def swap(block, axis, flip):
    return lax.ppermute(block, axis, [(i, i ^ flip) for i in range(lax.axis_size(axis))])


def next_pair(i, first, size):
    other = i + 2 if i // 2 % 2 == first else i - 2
    return other if 0 <= other < size else i


def swap_pairs(block, first):
    size, width = lax.axis_size("req"), lax.axis_size("tp")
    route = []
    for i in range(size):
        other = next_pair(i, first, size)
        for t in range(width):
            route.append((i * width + t, other * width + (t if other != i else t ^ 1)))
    return lax.ppermute(block, ("req", "tp"), route)


def alone(first):
    size = lax.axis_size("req")
    lonely = [i for i in range(size) if next_pair(i, first, size) == i]
    return sum([(lax.axis_index("req") == i).astype(jnp.int32) for i in lonely], jnp.int32(0))


def normalized(stream, gain):
    center = jnp.mean(stream, axis=-1, keepdims=True)
    moved = stream - center
    spread = jnp.mean(moved * moved, axis=-1, keepdims=True)
    return (moved * lax.rsqrt(spread + 1e-06) * gain).astype(jnp.bfloat16)


def dot(a, b, contract):
    return lax.dot_general(a, b, (contract, ((), ())), preferred_element_type=jnp.float32)


NN = ((1,), (0,))
NT = ((1,), (1,))


def row_of(gain_ref):
    return gain_ref[...].astype(jnp.float32).reshape(1, gain_ref.shape[0])


def vmem(mebibytes=60):
    return pltpu.CompilerParams(vmem_limit_bytes=mebibytes << 20)


def in_hbm(array):
    return pltpu.with_memory_space_constraint(array, pltpu.HBM)


def in_vmem(array):
    return pltpu.with_memory_space_constraint(array, pltpu.VMEM)


SCALARS = pl.BlockSpec(memory_space=pltpu.SMEM)
RESIDENT = pl.BlockSpec(memory_space=pltpu.VMEM)
ANYWHERE = pl.BlockSpec(memory_space=pl.ANY)


def load_mixer_kernel(place, *refs):
    wo_refs, we_refs, wr_refs, refs = refs[:4], refs[4:6], refs[6:8], refs[8:]
    wo, we, wr, sems = refs
    half = wo.shape[0] // 8
    copies = []
    for i in range(8):
        source = wo_refs[i // 2].at[place[0] ^ (i % 2)]
        copies.append((source, wo.at[pl.ds(i * half, half)]))
    copies += [(we_refs[i], we.at[i]) for i in range(2)]
    copies += [(wr_refs[i], wr.at[i]) for i in range(2)]
    copies = [pltpu.make_async_copy(*pair, sems.at[i]) for i, pair in enumerate(copies)]
    for copy in copies:
        copy.start()
    for copy in copies:
        copy.wait()


def load_mixer(place, wo, expand, reduce):
    half, width = wo[0].shape[1:]
    shapes = [(8 * half, width), (2,) + expand[0].shape, (2,) + reduce[0].shape]
    return pl.pallas_call(
        load_mixer_kernel,
        in_specs=[SCALARS] + [ANYWHERE] * 8,
        out_specs=[RESIDENT] * 3,
        out_shape=[pltpu.VMEM(shape, jnp.bfloat16) for shape in shapes],
        scratch_shapes=[pltpu.SemaphoreType.DMA((12,))],
        compiler_params=vmem(4),
        cost_estimate=pl.CostEstimate(flops=0, bytes_accessed=16_000_000, transcendentals=0),
        name="load_mixer",
    )(place, *[in_hbm(w) for w in (*wo, *expand, *reduce)])


def load_merge_kernel(own, other, both, sems):
    columns = own.shape[0]
    copies = [
        pltpu.make_async_copy(source, both.at[pl.ds(i * columns, columns)], sems.at[i])
        for i, source in enumerate((own, other))
    ]
    for copy in copies:
        copy.start()
    for copy in copies:
        copy.wait()


def load_merge(own, other):
    return pl.pallas_call(
        load_merge_kernel,
        in_specs=[ANYWHERE] * 2,
        out_specs=RESIDENT,
        out_shape=pltpu.VMEM((2 * own.shape[0], own.shape[1]), jnp.bfloat16),
        scratch_shapes=[pltpu.SemaphoreType.DMA((2,))],
        compiler_params=vmem(4),
        cost_estimate=pl.CostEstimate(flops=0, bytes_accessed=8_000_000, transcendentals=0),
        name="load_merge",
    )(in_hbm(own), in_hbm(other))


def project_kernel(parts, x_ref, segment_ref, gain_ref, *refs):
    w_refs, keep, send = refs[:parts], refs[parts], refs[parts + 1]
    first = lax.axis_index("req") % 2 == 0
    half = w_refs[0].shape[0] // 2
    rows = normalized(x_ref[...].astype(jnp.float32), row_of(gain_ref))
    for part in range(parts):
        out = dot(w_refs[part][...], rows, NT)
        low, high = out[:half], out[half:]
        at = slice(part * half, (part + 1) * half)
        keep[at, :] = jnp.where(first, low, high).astype(jnp.bfloat16)
        send[at, :] = jnp.where(first, high, low).astype(jnp.bfloat16)
    if parts > 1:
        number = segment_ref[...] + 1
        row = lax.broadcasted_iota(jnp.int32, (SEGMENT_ROWS, 1), 0)
        number = jnp.where(row == 0, number & 255, jnp.where(row == 1, number >> 8, 0))
        number = number.astype(jnp.float32).astype(jnp.bfloat16)
        keep[parts * half :, :] = number
        send[parts * half :, :] = number


def project(tokens, segments, gain, weight, parts, name):
    rows, width = tokens.shape
    half = weight.shape[0] // 6
    step = 256
    tall = len(parts) * half + (SEGMENT_ROWS if len(parts) > 1 else 0)
    return pl.pallas_call(
        functools.partial(project_kernel, len(parts)),
        grid=(rows // step,),
        in_specs=[
            pl.BlockSpec((step, width), lambda i: (i, 0)),
            pl.BlockSpec((1, step), lambda i: (0, i)),
            pl.BlockSpec(gain.shape, lambda i: (0,)),
        ]
        + [pl.BlockSpec((2 * half, width), lambda i, p=p: (p, 0)) for p in parts],
        out_specs=[pl.BlockSpec((tall, step), lambda i: (0, i))] * 2,
        out_shape=[pltpu.HBM((tall, rows), jnp.bfloat16)] * 2,
        compiler_params=vmem(),
        name=name,
    )(tokens, segments, gain, *[weight] * len(parts))


def numbers_of(ref, at):
    two = ref[:, at].astype(jnp.float32)
    return two[0:1] + 256.0 * two[1:2]


def largest_norm(first, second):
    squares = []
    for block in (first, second):
        block = block.astype(jnp.float32)
        squares.append(jnp.sum(block * block, axis=0, keepdims=True))
    return jnp.max(jnp.maximum(squares[0], squares[1]))


def attend_kernel(blocks, flags, resumed, skips, last, place, *refs):
    groups = len(resumed)
    q_refs, number_refs, refs = refs[:groups], refs[groups : 2 * groups], refs[2 * groups :]
    kv_refs, refs = refs[:blocks], refs[blocks:]
    state_refs = []
    for old in resumed:
        state_refs.append(refs[:2] if old else None)
        refs = refs[2:] if old else refs
    outs, refs = refs[: groups * (1 if last else 2)], refs[groups * (1 if last else 2) :]
    keys, values, columns, acc, peak, bounds, plain = refs
    tiles_of = kv_refs[0].shape[1] // TILE
    tiles = blocks * tiles_of
    tall = kv_refs[0].shape[0] - SEGMENT_ROWS

    for b in range(blocks):
        for t in range(tiles_of):
            n = b * tiles_of + t
            at = slice(t * TILE, (t + 1) * TILE)
            for h in range(2):
                block = kv_refs[b][h * HD : (h + 1) * HD, at].astype(jnp.float32)
                keys[n, h] = jnp.transpose(block).astype(jnp.bfloat16)
                values[n, h, :HD] = kv_refs[b][(2 + h) * HD : (3 + h) * HD, at]
                values[n, h, HD:] = jnp.ones((VROWS - HD, TILE), jnp.bfloat16)
            number = numbers_of(kv_refs[b].at[tall:], at)
            low, high = jnp.min(number), jnp.max(number)
            if b in flags:
                low = jnp.where(place[flags[b]] == 1, -1.0, low)
                high = jnp.where(place[flags[b]] == 1, -1.0, high)
            bounds[3 * n] = low
            bounds[3 * n + 1] = high
            bounds[3 * n + 2] = largest_norm(kv_refs[b][:HD, at], kv_refs[b][HD : 2 * HD, at])
            columns[n] = jnp.transpose(jnp.broadcast_to(number, (128, TILE)))

    units = [(slice(c, c + LANES), h) for c in range(0, TILE, LANES) for h in range(2)]

    def attend_tile(g, j):
        if resumed[g]:
            acc[...] = state_refs[g][0][j]
            peak[...] = state_refs[g][1][j]
            plain[0] = (jnp.max(jnp.abs(state_refs[g][1][j])) == 0.0).astype(jnp.int32)
        else:
            acc[...] = jnp.zeros_like(acc)
            peak[...] = jnp.zeros_like(peak)
            plain[0] = 1
        mine = pl.ds(pl.multiple_of((j ^ place[1]) * TILE, TILE), TILE)
        q_row = numbers_of(number_refs[g].at[tall:], mine)
        queries = q_refs[g][:, mine]
        q_low, q_high = jnp.min(q_row), jnp.max(q_row)
        q_norm = largest_norm(queries[:HD], queries[HD:])

        def scores_of(t, h, at, matches):
            scores = dot(keys[t, h], queries[h * HD : (h + 1) * HD, at], NN)
            return scores if matches is None else jnp.where(matches, scores, MASKED)

        def matches_of(t, at):
            column = columns[t]
            return jnp.concatenate([column] * (LANES // 128), axis=1) == q_row[:, at]

        def unshifted(t, masked):
            scores, probs, matches = {}, {}, None
            for i in range(len(units) + AHEAD + 1):
                if i < len(units):
                    at, h = units[i]
                    if masked and h == 0:
                        matches = matches_of(t, at)
                    scores[i] = scores_of(t, h, at, matches)
                if 0 <= i - AHEAD < len(units):
                    probs[i - AHEAD] = jnp.exp(scores.pop(i - AHEAD) * FACTOR).astype(jnp.bfloat16)
                if 0 <= i - AHEAD - 1 < len(units):
                    at, h = units[i - AHEAD - 1]
                    acc[h, :, at] += dot(values[t, h], probs.pop(i - AHEAD - 1), NN)

        def shifted_by_peak(t):
            for at, h in units:
                scores = scores_of(t, h, at, matches_of(t, at))
                old = jnp.where(acc[h, HD : HD + 1, at] > 0.0, peak[h : h + 1, at], START)
                new = jnp.maximum(old, jnp.max(scores, axis=0, keepdims=True))
                probs = jnp.exp((scores - new) * FACTOR).astype(jnp.bfloat16)
                shrink = jnp.exp((old - new) * FACTOR)
                peak[h : h + 1, at] = new
                acc[h, :, at] = acc[h, :, at] * shrink + dot(values[t, h], probs, NN)
            plain[0] = 0

        def visit(t, carry):
            k_low, k_high = bounds[3 * t], bounds[3 * t + 1]
            touches = (k_high >= q_low) & (k_low <= q_high)
            whole = (k_low == k_high) & (q_low == q_high)
            small = (plain[0] == 1) & (q_norm * bounds[3 * t + 2] <= SMALL * SMALL * HD)

            @pl.when(touches & small & whole)
            def _():
                unshifted(t, False)

            @pl.when(touches & small & jnp.logical_not(whole))
            def _():
                unshifted(t, True)

            @pl.when(touches & jnp.logical_not(small))
            def _():
                shifted_by_peak(t)

            return carry

        lax.fori_loop(skips[g] * tiles_of, tiles, visit, 0)
        if last:
            for h in range(2):
                at = slice(h * HD, (h + 1) * HD)
                outs[g][j, at, :] = (acc[h, :HD] / acc[h, HD : HD + 1]).astype(jnp.bfloat16)
        else:
            outs[2 * g][j] = acc[...]
            outs[2 * g + 1][j] = peak[...]

    for g in range(groups):

        def step(j, carry, g=g):
            attend_tile(g, j)
            return carry

        lax.fori_loop(0, tiles_of, step, 0)


def attend(place, queries, numbers, key_values, name, flags, states, skips, last=False):
    half, rows = queries[0].shape
    groups, blocks = len(queries), len(key_values)
    tiles_of = rows // TILE
    tiles = blocks * tiles_of
    acc_shape, peak_shape = (2, VROWS, TILE), (2, TILE)
    operands = [*queries, *numbers, *key_values]
    for state in states:
        operands += [] if state is None else list(state)
    if last:
        out_shape = [pltpu.VMEM((tiles_of, half, TILE), jnp.bfloat16)] * groups
    else:
        out_shape = [
            pltpu.VMEM((tiles_of,) + acc_shape, jnp.float32),
            pltpu.VMEM((tiles_of,) + peak_shape, jnp.float32),
        ] * groups
    resumed = [state is not None for state in states]
    out = pl.pallas_call(
        functools.partial(attend_kernel, blocks, flags, resumed, skips, last),
        in_specs=[SCALARS] + [RESIDENT] * len(operands),
        out_specs=[RESIDENT] * len(out_shape),
        out_shape=out_shape,
        scratch_shapes=[
            pltpu.VMEM((tiles, 2, TILE, HD), jnp.bfloat16),
            pltpu.VMEM((tiles, 2, VROWS, TILE), jnp.bfloat16),
            pltpu.VMEM((tiles, TILE, 128), jnp.float32),
            pltpu.VMEM(acc_shape, jnp.float32),
            pltpu.VMEM(peak_shape, jnp.float32),
            pltpu.SMEM((3 * tiles,), jnp.float32),
            pltpu.SMEM((1,), jnp.int32),
        ],
        compiler_params=vmem(24),
        cost_estimate=pl.CostEstimate(flops=1_000_000, bytes_accessed=1_000_000, transcendentals=0),
        name=name,
    )(place, *[in_vmem(a) for a in operands])
    return list(out) if last else [out[2 * g : 2 * g + 2] for g in range(groups)]


def mixer_kernel(first, which, place, *refs):
    sources, refs = refs[:8], refs[8:]
    x_hbm, gain_ref, wo, we, wr, sent, kept, context, hidden, x, sem = refs
    rows = x.shape[0]
    half = sources[0].shape[1]
    width = we.shape[2]
    fetch = pltpu.make_async_copy(
        x_hbm.at[pl.ds(pl.multiple_of(place[2] + first, 128), rows)], x, sem
    )
    fetch.start()
    lanes = slice(first, first + rows)
    for i in range(8):
        context[i * half : (i + 1) * half, :] = sources[i][which[i], :, lanes].astype(jnp.float32)
    inputs = jnp.transpose(context[...]).astype(jnp.bfloat16)
    fetch.wait()
    total = x[...].astype(jnp.float32) + dot(inputs, wo[...], NN)
    inputs = normalized(total, row_of(gain_ref))
    for i in range(2):
        inner = dot(inputs, we[i], NN)
        grown = 0.5 * inner * (1.0 + lax.erf(inner * (1.0 / math.sqrt(2.0))))
        hidden[:, i * width : (i + 1) * width] = grown.astype(jnp.bfloat16)
    out = dot(hidden[:, :width], wr[0], NN) + dot(hidden[:, width:], wr[1], NN)
    sent[...] = out.astype(jnp.bfloat16)
    kept[...] = total + out


def mixer(place, pieces, tokens, gain, weights, first, chunk_rows):
    width = tokens.shape[1]
    half = pieces[0][0].shape[1]
    hidden = weights[1].shape[2]
    return pl.pallas_call(
        functools.partial(mixer_kernel, first, [which for _, which in pieces]),
        in_specs=[SCALARS] + [RESIDENT] * 8 + [ANYWHERE] + [RESIDENT] * 4,
        out_specs=[RESIDENT] * 2,
        out_shape=[
            jax.ShapeDtypeStruct((chunk_rows, width), jnp.bfloat16),
            jax.ShapeDtypeStruct((chunk_rows, width), jnp.float32),
        ],
        scratch_shapes=[
            pltpu.VMEM((8 * half, chunk_rows), jnp.float32),
            pltpu.VMEM((chunk_rows, 2 * hidden), jnp.bfloat16),
            pltpu.VMEM((chunk_rows, width), jnp.bfloat16),
            pltpu.SemaphoreType.DMA,
        ],
        compiler_params=vmem(30),
        cost_estimate=pl.CostEstimate(
            flops=5_000_000_000, bytes_accessed=20_000_000, transcendentals=0
        ),
        name="mixer",
    )(place, *[source for source, _ in pieces], tokens, gain, *[in_vmem(w) for w in weights])


def one_hot_rows(index_ref, k, first, rows):
    column = jnp.transpose(jnp.broadcast_to(index_ref[k : k + 1, :], (128, index_ref.shape[1])))
    lanes = lax.broadcasted_iota(jnp.int32, (1, 128), 1)
    parts = [column == lanes + (first + 128 * n) for n in range(rows // 128)]
    return jnp.concatenate(parts, axis=1).astype(jnp.float32).astype(jnp.bfloat16)


def gather_kernel(first, place, index_ref, kept, received, gain_ref, *refs):
    merged = refs[-1]
    rows = kept.shape[0]
    final = normalized(kept[...] + received[...].astype(jnp.float32), row_of(gain_ref))
    for k in range(4):
        part = dot(one_hot_rows(index_ref, k, place[2] + first, rows), final, NN)
        if len(refs) > 1:
            part = part + refs[0][k].astype(jnp.float32)
        merged[k] = part.astype(jnp.bfloat16)


def gather(place, index, kept, received, gain, first, earlier):
    return pl.pallas_call(
        functools.partial(gather_kernel, first),
        in_specs=[SCALARS] + [RESIDENT] * (4 + len(earlier)),
        out_specs=RESIDENT,
        out_shape=pltpu.VMEM((4, index.shape[1], kept.shape[1]), jnp.bfloat16),
        compiler_params=vmem(20),
        cost_estimate=pl.CostEstimate(
            flops=1_000_000_000, bytes_accessed=5_000_000, transcendentals=0
        ),
        name="gather",
    )(place, index, kept, received, gain, *[in_vmem(a) for a in earlier])


def merge_kernel(
    first, place, index_ref, kept, received, gain_ref, earlier, weights, own, other, parts
):
    rows, width = kept.shape
    columns = own.shape[1]
    final = normalized(kept[...] + received[...].astype(jnp.float32), row_of(gain_ref))
    for k in range(4):
        part = dot(one_hot_rows(index_ref, k, place[2] + first, rows), final, NN)
        part = part + earlier[k].astype(jnp.float32)
        parts[:, k * width : (k + 1) * width] = part.astype(jnp.bfloat16)
    total = dot(parts[...], weights[...], NT)
    own[...] = total[:, :columns]
    other[...] = total[:, columns:]


def merge(place, index, kept, received, gain, first, earlier, weights):
    merged_rows = index.shape[1]
    columns = weights.shape[0] // 2
    return pl.pallas_call(
        functools.partial(merge_kernel, first),
        in_specs=[SCALARS] + [RESIDENT] * 6,
        out_specs=[RESIDENT] * 2,
        out_shape=[jax.ShapeDtypeStruct((merged_rows, columns), jnp.float32)] * 2,
        scratch_shapes=[pltpu.VMEM((merged_rows, weights.shape[1]), jnp.bfloat16)],
        compiler_params=vmem(20),
        cost_estimate=pl.CostEstimate(
            flops=3_000_000_000, bytes_accessed=12_000_000, transcendentals=0
        ),
        name="merge",
    )(place, index, kept, received, gain, in_vmem(earlier), in_vmem(weights))


def place_kernel(position, own, received, out):
    feature = (own[...] + received[...]).astype(jnp.bfloat16)
    slots = lax.broadcasted_iota(jnp.int32, (out.shape[0], 1), 0)
    chosen = (slots == position[...]).astype(jnp.float32).astype(jnp.bfloat16)
    out[...] = dot(chosen, feature, NN).astype(jnp.bfloat16)


def body(
    tokens,
    segments,
    attend_gain,
    attend_weight,
    output_weight,
    mixer_gain,
    expand_weight,
    reduce_weight,
    output_gain,
    merge_weight,
    merge_index,
    owners,
):
    rows, width = tokens.shape
    head_width = attend_weight.shape[2]
    half = head_width // 2
    peers = lax.axis_size("req")
    req = lax.axis_index("req")
    par = req % 2
    core = lax.axis_index("tp") % 2

    per_core = rows // 2
    chunks = [(0, 128), (128, per_core - 256), (per_core - 128, 128)]
    place = jnp.stack([par, core, core * per_core, req, alone(0), alone(1)])
    tie = lax.optimization_barrier
    with jax.named_scope("weights"):
        wo_own = output_weight.reshape(2, half, width)
        wo_core = swap(wo_own, "tp", 1)
        expand_other = swap(expand_weight, "tp", 1)

    with jax.named_scope("project"):
        weight = jnp.transpose(attend_weight, (1, 2, 0)).reshape(6 * half, width)
        numbers = segments[None, :]
        kv_own, kv_send = project(tokens, numbers, attend_gain, weight, (1, 2), "project_keys")
        kv_own, kv_send, expand_other, wo_core = tie((kv_own, kv_send, expand_other, wo_core))

    with jax.named_scope("exchange_keys"):
        kv_peer = swap(kv_send, "req", 1)
        kv_even = swap_pairs(kv_own, 0)
        kv_odd = swap_pairs(kv_own, 1)
        wo_across = swap(wo_own, "tp", 2)
        q_own, q_send = project(tokens, numbers, attend_gain, weight, (0,), "project_queries")
        q_peer = swap(q_send, "req", 1)
        (state,) = attend(place, [q_own], [kv_own], [kv_own], "attend_own", {}, [None], [0])
        kv_odd, kv_even, kv_peer, state, wo_across, late_reduce, late_wo = tie(
            (kv_odd, kv_even, kv_peer, state, wo_across, reduce_weight, wo_core)
        )
        kv_even_peer = swap_pairs(kv_peer, 0)
        kv_odd_peer = swap_pairs(kv_peer, 1)
        reduce_other = swap(late_reduce, "tp", 1)
        wo_both = swap(late_wo, "tp", 2)

    with jax.named_scope("slots"):
        capacity = 2 * merge_index.shape[0] // peers
        target = owners[:, 0]
        choose = (target[:, None] == jnp.arange(peers, dtype=jnp.int32)[None, :]).astype(jnp.int32)
        slot = jnp.sum((jnp.cumsum(choose, axis=0) - 1) * choose, axis=1)
        position = (target * capacity + slot)[None, :]
        index = jnp.transpose(merge_index) - req * rows

        q_peer, position, index = tie((q_peer, position, index))

    with jax.named_scope("attention"):
        queries, numbers = [q_peer, q_own], [kv_peer, kv_own]
        near = [kv_own, kv_peer, kv_even, kv_odd]
        states = [None, state]
        states = attend(
            place, queries, numbers, near, "attend_near", {2: 4, 3: 5}, states, [0, 1]
        )
        states, kv_even_peer, kv_odd_peer, reduce_other, wo_both = tie(
            (states, kv_even_peer, kv_odd_peer, reduce_other, wo_both)
        )
        far = [kv_even_peer, kv_odd_peer]
        for_peer, context = attend(
            place, queries, numbers, far, "attend_far", {0: 4, 1: 5}, states, [0, 0], True
        )

    with jax.named_scope("exchange_context"):
        late_wo, context, for_peer = tie((wo_own, context, for_peer))
        from_peer = swap(for_peer, "req", 1)
        weights = load_mixer(
            place,
            [late_wo, wo_core, wo_across, wo_both],
            [expand_weight, expand_other],
            [reduce_weight, reduce_other],
        )
        from_peer, weights = tie((from_peer, weights))
        sides = []
        for source in (context, from_peer):
            across = swap(source, "tp", 2)
            sides.append(
                [(source, 0), (swap(source, "tp", 1), 1), (across, 0), (swap(across, "tp", 1), 1)]
            )
        pieces = [sides[h][t] for t in range(4) for h in range(2)]

    with jax.named_scope("mixer"):
        sent, kept, received = [], [], []
        for first, size in chunks:
            s, k = mixer(place, pieces, tokens, mixer_gain, weights, first, size)
            sent.append(s)
            kept.append(k)
            received.append(swap(s, "tp", 2))
            if first == 0:
                merge_own, _ = tie((jnp.transpose(merge_weight), s))
                merge_other = swap(merge_own, "tp", 1)

    with jax.named_scope("merge"):
        merge_other, position, index, _ = tie((merge_other, position, index, sent[-1]))
        weights = load_merge(merge_own, merge_other)
        earlier = []
        for c, (first, _) in enumerate(chunks[:-1]):
            earlier = [
                gather(place, index, kept[c], received[c], output_gain, first, earlier)
            ]
        weights, earlier, last, position = tie((weights, earlier[0], received[-1], position))
        first = chunks[-1][0]
        own, other = merge(
            place, index, kept[-1], last, output_gain, first, earlier, weights
        )
        other = swap(other, "tp", 1)

    with jax.named_scope("place"):
        columns = own.shape[1]
        outgoing = pl.pallas_call(
            place_kernel,
            in_specs=[RESIDENT] * 3,
            out_specs=RESIDENT,
            out_shape=jax.ShapeDtypeStruct((peers * capacity, columns), jnp.bfloat16),
            compiler_params=vmem(10),
            name="place",
        )(position, in_vmem(own), in_vmem(other))
        outgoing = outgoing.reshape(peers, capacity, columns)
        arrived = lax.all_to_all(outgoing, "req", split_axis=0, concat_axis=0, tiled=True)
    return arrived.reshape(1, peers, capacity, columns)


def solution(mesh):
    placed = (
        P("req", None),
        P("req"),
        P(),
        P(None, None, "tp"),
        P("tp", None),
        P(),
        P(None, "tp"),
        P("tp", None),
        P(),
        P(None, "tp"),
        P("req", None),
        P("req", None),
    )
    return jax.shard_map(
        body, mesh=mesh, in_specs=placed, out_specs=P("req", None, None, "tp"), check_vma=False
    )
```

```python
import functools
import math

import jax
import jax.numpy as jnp
from jax import lax
from jax.experimental import pallas as pl
from jax.experimental.pallas import tpu as pltpu
from jax.sharding import PartitionSpec as P

HD = 80
TILE = 512
MASKED = -1e30
START = -1e28
FACTOR = 1.0 / math.sqrt(HD)
SEGMENT_ROWS = 16
VROWS = 96
LANES = 256
AHEAD = 2
SMALL = 72.0


def swap(block, axis, flip):
    return lax.ppermute(block, axis, [(i, i ^ flip) for i in range(lax.axis_size(axis))])


def next_pair(i, first, size):
    other = i + 2 if i // 2 % 2 == first else i - 2
    return other if 0 <= other < size else i


def swap_pairs(block, first):
    size, width = lax.axis_size("req"), lax.axis_size("tp")
    route = []
    for i in range(size):
        other = next_pair(i, first, size)
        for t in range(width):
            route.append((i * width + t, other * width + (t if other != i else t ^ 1)))
    return lax.ppermute(block, ("req", "tp"), route)


def alone(first):
    size = lax.axis_size("req")
    lonely = [i for i in range(size) if next_pair(i, first, size) == i]
    return sum([(lax.axis_index("req") == i).astype(jnp.int32) for i in lonely], jnp.int32(0))


def normalized(stream, gain):
    center = jnp.mean(stream, axis=-1, keepdims=True)
    moved = stream - center
    spread = jnp.mean(moved * moved, axis=-1, keepdims=True)
    return (moved * lax.rsqrt(spread + 1e-06) * gain).astype(jnp.bfloat16)


def dot(a, b, contract):
    return lax.dot_general(a, b, (contract, ((), ())), preferred_element_type=jnp.float32)


NN = ((1,), (0,))
NT = ((1,), (1,))


def row_of(gain_ref):
    return gain_ref[...].astype(jnp.float32).reshape(1, gain_ref.shape[0])


def vmem(mebibytes=60):
    return pltpu.CompilerParams(vmem_limit_bytes=mebibytes << 20)


def in_hbm(array):
    return pltpu.with_memory_space_constraint(array, pltpu.HBM)


def in_vmem(array):
    return pltpu.with_memory_space_constraint(array, pltpu.VMEM)


SCALARS = pl.BlockSpec(memory_space=pltpu.SMEM)
RESIDENT = pl.BlockSpec(memory_space=pltpu.VMEM)
ANYWHERE = pl.BlockSpec(memory_space=pl.ANY)


def load_mixer_kernel(place, *refs):
    wo_refs, we_refs, wr_refs, refs = refs[:4], refs[4:6], refs[6:8], refs[8:]
    wo, we, wr, sems = refs
    half = wo.shape[0] // 8
    copies = []
    for i in range(8):
        source = wo_refs[i // 2].at[place[0] ^ (i % 2)]
        copies.append((source, wo.at[pl.ds(i * half, half)]))
    copies += [(we_refs[i], we.at[i]) for i in range(2)]
    copies += [(wr_refs[i], wr.at[i]) for i in range(2)]
    copies = [pltpu.make_async_copy(*pair, sems.at[i]) for i, pair in enumerate(copies)]
    for copy in copies:
        copy.start()
    for copy in copies:
        copy.wait()


def load_mixer(place, wo, expand, reduce):
    half, width = wo[0].shape[1:]
    shapes = [(8 * half, width), (2,) + expand[0].shape, (2,) + reduce[0].shape]
    return pl.pallas_call(
        load_mixer_kernel,
        in_specs=[SCALARS] + [ANYWHERE] * 8,
        out_specs=[RESIDENT] * 3,
        out_shape=[pltpu.VMEM(shape, jnp.bfloat16) for shape in shapes],
        scratch_shapes=[pltpu.SemaphoreType.DMA((12,))],
        compiler_params=vmem(4),
        cost_estimate=pl.CostEstimate(flops=0, bytes_accessed=16_000_000, transcendentals=0),
        name="load_mixer",
    )(place, *[in_hbm(w) for w in (*wo, *expand, *reduce)])


def load_merge_kernel(own, other, both, sems):
    columns = own.shape[0]
    copies = [
        pltpu.make_async_copy(source, both.at[pl.ds(i * columns, columns)], sems.at[i])
        for i, source in enumerate((own, other))
    ]
    for copy in copies:
        copy.start()
    for copy in copies:
        copy.wait()


def load_merge(own, other):
    return pl.pallas_call(
        load_merge_kernel,
        in_specs=[ANYWHERE] * 2,
        out_specs=RESIDENT,
        out_shape=pltpu.VMEM((2 * own.shape[0], own.shape[1]), jnp.bfloat16),
        scratch_shapes=[pltpu.SemaphoreType.DMA((2,))],
        compiler_params=vmem(4),
        cost_estimate=pl.CostEstimate(flops=0, bytes_accessed=8_000_000, transcendentals=0),
        name="load_merge",
    )(in_hbm(own), in_hbm(other))


def project_kernel(parts, x_ref, segment_ref, gain_ref, *refs):
    w_refs, keep, send = refs[:parts], refs[parts], refs[parts + 1]
    first = lax.axis_index("req") % 2 == 0
    half = w_refs[0].shape[0] // 2
    rows = normalized(x_ref[...].astype(jnp.float32), row_of(gain_ref))
    for part in range(parts):
        out = dot(w_refs[part][...], rows, NT)
        low, high = out[:half], out[half:]
        at = slice(part * half, (part + 1) * half)
        keep[at, :] = jnp.where(first, low, high).astype(jnp.bfloat16)
        send[at, :] = jnp.where(first, high, low).astype(jnp.bfloat16)
    if parts > 1:
        number = segment_ref[...] + 1
        row = lax.broadcasted_iota(jnp.int32, (SEGMENT_ROWS, 1), 0)
        number = jnp.where(row == 0, number & 255, jnp.where(row == 1, number >> 8, 0))
        number = number.astype(jnp.float32).astype(jnp.bfloat16)
        keep[parts * half :, :] = number
        send[parts * half :, :] = number


def project(tokens, segments, gain, weight, parts, name):
    rows, width = tokens.shape
    half = weight.shape[0] // 6
    step = 256
    tall = len(parts) * half + (SEGMENT_ROWS if len(parts) > 1 else 0)
    return pl.pallas_call(
        functools.partial(project_kernel, len(parts)),
        grid=(rows // step,),
        in_specs=[
            pl.BlockSpec((step, width), lambda i: (i, 0)),
            pl.BlockSpec((1, step), lambda i: (0, i)),
            pl.BlockSpec(gain.shape, lambda i: (0,)),
        ]
        + [pl.BlockSpec((2 * half, width), lambda i, p=p: (p, 0)) for p in parts],
        out_specs=[pl.BlockSpec((tall, step), lambda i: (0, i))] * 2,
        out_shape=[pltpu.HBM((tall, rows), jnp.bfloat16)] * 2,
        compiler_params=vmem(),
        name=name,
    )(tokens, segments, gain, *[weight] * len(parts))


def numbers_of(ref, at):
    two = ref[:, at].astype(jnp.float32)
    return two[0:1] + 256.0 * two[1:2]


def largest_norm(first, second):
    squares = []
    for block in (first, second):
        block = block.astype(jnp.float32)
        squares.append(jnp.sum(block * block, axis=0, keepdims=True))
    return jnp.max(jnp.maximum(squares[0], squares[1]))


def attend_kernel(blocks, flags, resumed, skips, last, place, *refs):
    groups = len(resumed)
    q_refs, number_refs, refs = refs[:groups], refs[groups : 2 * groups], refs[2 * groups :]
    kv_refs, refs = refs[:blocks], refs[blocks:]
    state_refs = []
    for old in resumed:
        state_refs.append(refs[:2] if old else None)
        refs = refs[2:] if old else refs
    outs, refs = refs[: groups * (1 if last else 2)], refs[groups * (1 if last else 2) :]
    keys, values, columns, acc, peak, bounds, plain = refs
    tiles_of = kv_refs[0].shape[1] // TILE
    tiles = blocks * tiles_of
    tall = kv_refs[0].shape[0] - SEGMENT_ROWS

    for b in range(blocks):
        for t in range(tiles_of):
            n = b * tiles_of + t
            at = slice(t * TILE, (t + 1) * TILE)
            for h in range(2):
                block = kv_refs[b][h * HD : (h + 1) * HD, at].astype(jnp.float32)
                keys[n, h] = jnp.transpose(block).astype(jnp.bfloat16)
                values[n, h, :HD] = kv_refs[b][(2 + h) * HD : (3 + h) * HD, at]
                values[n, h, HD:] = jnp.ones((VROWS - HD, TILE), jnp.bfloat16)
            number = numbers_of(kv_refs[b].at[tall:], at)
            low, high = jnp.min(number), jnp.max(number)
            if b in flags:
                low = jnp.where(place[flags[b]] == 1, -1.0, low)
                high = jnp.where(place[flags[b]] == 1, -1.0, high)
            bounds[3 * n] = low
            bounds[3 * n + 1] = high
            bounds[3 * n + 2] = largest_norm(kv_refs[b][:HD, at], kv_refs[b][HD : 2 * HD, at])
            columns[n] = jnp.transpose(jnp.broadcast_to(number, (128, TILE)))

    units = [(slice(c, c + LANES), h) for c in range(0, TILE, LANES) for h in range(2)]

    def attend_tile(g, j):
        if resumed[g]:
            acc[...] = state_refs[g][0][j]
            peak[...] = state_refs[g][1][j]
            plain[0] = (jnp.max(jnp.abs(state_refs[g][1][j])) == 0.0).astype(jnp.int32)
        else:
            acc[...] = jnp.zeros_like(acc)
            peak[...] = jnp.zeros_like(peak)
            plain[0] = 1
        mine = pl.ds(pl.multiple_of((j ^ place[1]) * TILE, TILE), TILE)
        q_row = numbers_of(number_refs[g].at[tall:], mine)
        queries = q_refs[g][:, mine]
        q_low, q_high = jnp.min(q_row), jnp.max(q_row)
        q_norm = largest_norm(queries[:HD], queries[HD:])

        def scores_of(t, h, at, matches):
            scores = dot(keys[t, h], queries[h * HD : (h + 1) * HD, at], NN)
            return scores if matches is None else jnp.where(matches, scores, MASKED)

        def matches_of(t, at):
            column = columns[t]
            return jnp.concatenate([column] * (LANES // 128), axis=1) == q_row[:, at]

        def unshifted(t, masked):
            scores, probs, matches = {}, {}, None
            for i in range(len(units) + AHEAD + 1):
                if i < len(units):
                    at, h = units[i]
                    if masked and h == 0:
                        matches = matches_of(t, at)
                    scores[i] = scores_of(t, h, at, matches)
                if 0 <= i - AHEAD < len(units):
                    probs[i - AHEAD] = jnp.exp(scores.pop(i - AHEAD) * FACTOR).astype(jnp.bfloat16)
                if 0 <= i - AHEAD - 1 < len(units):
                    at, h = units[i - AHEAD - 1]
                    acc[h, :, at] += dot(values[t, h], probs.pop(i - AHEAD - 1), NN)

        def shifted_by_peak(t):
            for at, h in units:
                scores = scores_of(t, h, at, matches_of(t, at))
                old = jnp.where(acc[h, HD : HD + 1, at] > 0.0, peak[h : h + 1, at], START)
                new = jnp.maximum(old, jnp.max(scores, axis=0, keepdims=True))
                probs = jnp.exp((scores - new) * FACTOR).astype(jnp.bfloat16)
                shrink = jnp.exp((old - new) * FACTOR)
                peak[h : h + 1, at] = new
                acc[h, :, at] = acc[h, :, at] * shrink + dot(values[t, h], probs, NN)
            plain[0] = 0

        def visit(t, carry):
            k_low, k_high = bounds[3 * t], bounds[3 * t + 1]
            touches = (k_high >= q_low) & (k_low <= q_high)
            whole = (k_low == k_high) & (q_low == q_high)
            small = (plain[0] == 1) & (q_norm * bounds[3 * t + 2] <= SMALL * SMALL * HD)

            @pl.when(touches & small & whole)
            def _():
                unshifted(t, False)

            @pl.when(touches & small & jnp.logical_not(whole))
            def _():
                unshifted(t, True)

            @pl.when(touches & jnp.logical_not(small))
            def _():
                shifted_by_peak(t)

            return carry

        lax.fori_loop(skips[g] * tiles_of, tiles, visit, 0)
        if last:
            for h in range(2):
                at = slice(h * HD, (h + 1) * HD)
                outs[g][j, at, :] = (acc[h, :HD] / acc[h, HD : HD + 1]).astype(jnp.bfloat16)
        else:
            outs[2 * g][j] = acc[...]
            outs[2 * g + 1][j] = peak[...]

    for g in range(groups):

        def step(j, carry, g=g):
            attend_tile(g, j)
            return carry

        lax.fori_loop(0, tiles_of, step, 0)


def attend(place, queries, numbers, key_values, name, flags, states, skips, last=False):
    half, rows = queries[0].shape
    groups, blocks = len(queries), len(key_values)
    tiles_of = rows // TILE
    tiles = blocks * tiles_of
    acc_shape, peak_shape = (2, VROWS, TILE), (2, TILE)
    operands = [*queries, *numbers, *key_values]
    for state in states:
        operands += [] if state is None else list(state)
    if last:
        out_shape = [pltpu.VMEM((tiles_of, half, TILE), jnp.bfloat16)] * groups
    else:
        out_shape = [
            pltpu.VMEM((tiles_of,) + acc_shape, jnp.float32),
            pltpu.VMEM((tiles_of,) + peak_shape, jnp.float32),
        ] * groups
    resumed = [state is not None for state in states]
    out = pl.pallas_call(
        functools.partial(attend_kernel, blocks, flags, resumed, skips, last),
        in_specs=[SCALARS] + [RESIDENT] * len(operands),
        out_specs=[RESIDENT] * len(out_shape),
        out_shape=out_shape,
        scratch_shapes=[
            pltpu.VMEM((tiles, 2, TILE, HD), jnp.bfloat16),
            pltpu.VMEM((tiles, 2, VROWS, TILE), jnp.bfloat16),
            pltpu.VMEM((tiles, TILE, 128), jnp.float32),
            pltpu.VMEM(acc_shape, jnp.float32),
            pltpu.VMEM(peak_shape, jnp.float32),
            pltpu.SMEM((3 * tiles,), jnp.float32),
            pltpu.SMEM((1,), jnp.int32),
        ],
        compiler_params=vmem(24),
        cost_estimate=pl.CostEstimate(flops=1_000_000, bytes_accessed=1_000_000, transcendentals=0),
        name=name,
    )(place, *[in_vmem(a) for a in operands])
    return list(out) if last else [out[2 * g : 2 * g + 2] for g in range(groups)]


def mixer_kernel(first, which, place, *refs):
    sources, refs = refs[:8], refs[8:]
    x_hbm, gain_ref, wo, we, wr, sent, kept, context, hidden, x, sem = refs
    rows = x.shape[0]
    half = sources[0].shape[1]
    width = we.shape[2]
    fetch = pltpu.make_async_copy(
        x_hbm.at[pl.ds(pl.multiple_of(place[2] + first, 128), rows)], x, sem
    )
    fetch.start()
    lanes = slice(first, first + rows)
    for i in range(8):
        context[i * half : (i + 1) * half, :] = sources[i][which[i], :, lanes].astype(jnp.float32)
    inputs = jnp.transpose(context[...]).astype(jnp.bfloat16)
    fetch.wait()
    total = x[...].astype(jnp.float32) + dot(inputs, wo[...], NN)
    inputs = normalized(total, row_of(gain_ref))
    for i in range(2):
        inner = dot(inputs, we[i], NN)
        grown = 0.5 * inner * (1.0 + lax.erf(inner * (1.0 / math.sqrt(2.0))))
        hidden[:, i * width : (i + 1) * width] = grown.astype(jnp.bfloat16)
    out = dot(hidden[:, :width], wr[0], NN) + dot(hidden[:, width:], wr[1], NN)
    sent[...] = out.astype(jnp.bfloat16)
    kept[...] = total + out


def mixer(place, pieces, tokens, gain, weights, first, chunk_rows):
    width = tokens.shape[1]
    half = pieces[0][0].shape[1]
    hidden = weights[1].shape[2]
    return pl.pallas_call(
        functools.partial(mixer_kernel, first, [which for _, which in pieces]),
        in_specs=[SCALARS] + [RESIDENT] * 8 + [ANYWHERE] + [RESIDENT] * 4,
        out_specs=[RESIDENT] * 2,
        out_shape=[
            jax.ShapeDtypeStruct((chunk_rows, width), jnp.bfloat16),
            jax.ShapeDtypeStruct((chunk_rows, width), jnp.float32),
        ],
        scratch_shapes=[
            pltpu.VMEM((8 * half, chunk_rows), jnp.float32),
            pltpu.VMEM((chunk_rows, 2 * hidden), jnp.bfloat16),
            pltpu.VMEM((chunk_rows, width), jnp.bfloat16),
            pltpu.SemaphoreType.DMA,
        ],
        compiler_params=vmem(30),
        cost_estimate=pl.CostEstimate(
            flops=5_000_000_000, bytes_accessed=20_000_000, transcendentals=0
        ),
        name="mixer",
    )(place, *[source for source, _ in pieces], tokens, gain, *[in_vmem(w) for w in weights])


def one_hot_rows(index_ref, k, first, rows):
    column = jnp.transpose(jnp.broadcast_to(index_ref[k : k + 1, :], (128, index_ref.shape[1])))
    lanes = lax.broadcasted_iota(jnp.int32, (1, 128), 1)
    parts = [column == lanes + (first + 128 * n) for n in range(rows // 128)]
    return jnp.concatenate(parts, axis=1).astype(jnp.float32).astype(jnp.bfloat16)


def gather_kernel(first, place, index_ref, kept, received, gain_ref, *refs):
    merged = refs[-1]
    rows = kept.shape[0]
    final = normalized(kept[...] + received[...].astype(jnp.float32), row_of(gain_ref))
    for k in range(4):
        part = dot(one_hot_rows(index_ref, k, place[2] + first, rows), final, NN)
        if len(refs) > 1:
            part = part + refs[0][k].astype(jnp.float32)
        merged[k] = part.astype(jnp.bfloat16)


def gather(place, index, kept, received, gain, first, earlier):
    return pl.pallas_call(
        functools.partial(gather_kernel, first),
        in_specs=[SCALARS] + [RESIDENT] * (4 + len(earlier)),
        out_specs=RESIDENT,
        out_shape=pltpu.VMEM((4, index.shape[1], kept.shape[1]), jnp.bfloat16),
        compiler_params=vmem(20),
        cost_estimate=pl.CostEstimate(
            flops=1_000_000_000, bytes_accessed=5_000_000, transcendentals=0
        ),
        name="gather",
    )(place, index, kept, received, gain, *[in_vmem(a) for a in earlier])


def merge_kernel(
    first, place, index_ref, kept, received, gain_ref, earlier, weights, own, other, parts
):
    rows, width = kept.shape
    columns = own.shape[1]
    final = normalized(kept[...] + received[...].astype(jnp.float32), row_of(gain_ref))
    for k in range(4):
        part = dot(one_hot_rows(index_ref, k, place[2] + first, rows), final, NN)
        part = part + earlier[k].astype(jnp.float32)
        parts[:, k * width : (k + 1) * width] = part.astype(jnp.bfloat16)
    total = dot(parts[...], weights[...], NT)
    own[...] = total[:, :columns]
    other[...] = total[:, columns:]


def merge(place, index, kept, received, gain, first, earlier, weights):
    merged_rows = index.shape[1]
    columns = weights.shape[0] // 2
    return pl.pallas_call(
        functools.partial(merge_kernel, first),
        in_specs=[SCALARS] + [RESIDENT] * 6,
        out_specs=[RESIDENT] * 2,
        out_shape=[jax.ShapeDtypeStruct((merged_rows, columns), jnp.float32)] * 2,
        scratch_shapes=[pltpu.VMEM((merged_rows, weights.shape[1]), jnp.bfloat16)],
        compiler_params=vmem(20),
        cost_estimate=pl.CostEstimate(
            flops=3_000_000_000, bytes_accessed=12_000_000, transcendentals=0
        ),
        name="merge",
    )(place, index, kept, received, gain, in_vmem(earlier), in_vmem(weights))


def place_kernel(position, own, received, out):
    feature = (own[...] + received[...]).astype(jnp.bfloat16)
    slots = lax.broadcasted_iota(jnp.int32, (out.shape[0], 1), 0)
    chosen = (slots == position[...]).astype(jnp.float32).astype(jnp.bfloat16)
    out[...] = dot(chosen, feature, NN).astype(jnp.bfloat16)


def body(
    tokens,
    segments,
    attend_gain,
    attend_weight,
    output_weight,
    mixer_gain,
    expand_weight,
    reduce_weight,
    output_gain,
    merge_weight,
    merge_index,
    owners,
):
    rows, width = tokens.shape
    head_width = attend_weight.shape[2]
    half = head_width // 2
    peers = lax.axis_size("req")
    req = lax.axis_index("req")
    par = req % 2
    core = lax.axis_index("tp") % 2

    per_core = rows // 2
    chunks = [(0, 128), (128, per_core - 256), (per_core - 128, 128)]
    place = jnp.stack([par, core, core * per_core, req, alone(0), alone(1)])
    tie = lax.optimization_barrier
    with jax.named_scope("weights"):
        wo_own = output_weight.reshape(2, half, width)
        wo_core = swap(wo_own, "tp", 1)
        expand_other = swap(expand_weight, "tp", 1)

    with jax.named_scope("project"):
        weight = jnp.transpose(attend_weight, (1, 2, 0)).reshape(6 * half, width)
        numbers = segments[None, :]
        kv_own, kv_send = project(tokens, numbers, attend_gain, weight, (1, 2), "project_keys")
        kv_own, kv_send, expand_other, wo_core = tie((kv_own, kv_send, expand_other, wo_core))

    with jax.named_scope("slots"):
        capacity = 2 * merge_index.shape[0] // peers
        target = owners[:, 0]
        choose = (target[:, None] == jnp.arange(peers, dtype=jnp.int32)[None, :]).astype(jnp.int32)
        slot = jnp.sum((jnp.cumsum(choose, axis=0) - 1) * choose, axis=1)
        position = (target * capacity + slot)[None, :]
        index = jnp.transpose(merge_index) - req * rows

    with jax.named_scope("exchange_keys"):
        kv_peer = swap(kv_send, "req", 1)
        kv_even = swap_pairs(kv_own, 0)
        kv_odd = swap_pairs(kv_own, 1)
        wo_across = swap(wo_own, "tp", 2)
        q_own, q_send = project(tokens, numbers, attend_gain, weight, (0,), "project_queries")
        q_peer = swap(q_send, "req", 1)
        (state,) = attend(place, [q_own], [kv_own], [kv_own], "attend_own", {}, [None], [0])
        kv_odd, kv_even, kv_peer, state, wo_across, late_reduce, late_wo, position, index = tie(
            (kv_odd, kv_even, kv_peer, state, wo_across, reduce_weight, wo_core, position, index)
        )
        kv_even_peer = swap_pairs(kv_peer, 0)
        kv_odd_peer = swap_pairs(kv_peer, 1)
        reduce_other = swap(late_reduce, "tp", 1)
        wo_both = swap(late_wo, "tp", 2)


    with jax.named_scope("attention"):
        queries, numbers = [q_peer, q_own], [kv_peer, kv_own]
        near = [kv_own, kv_peer, kv_even, kv_odd]
        states = [None, state]
        states = attend(
            place, queries, numbers, near, "attend_near", {2: 4, 3: 5}, states, [0, 1]
        )
        states, kv_even_peer, kv_odd_peer, reduce_other, wo_both = tie(
            (states, kv_even_peer, kv_odd_peer, reduce_other, wo_both)
        )
        far = [kv_even_peer, kv_odd_peer]
        for_peer, context = attend(
            place, queries, numbers, far, "attend_far", {0: 4, 1: 5}, states, [0, 0], True
        )

    with jax.named_scope("exchange_context"):
        late_wo, context, for_peer = tie((wo_own, context, for_peer))
        from_peer = swap(for_peer, "req", 1)
        weights = load_mixer(
            place,
            [late_wo, wo_core, wo_across, wo_both],
            [expand_weight, expand_other],
            [reduce_weight, reduce_other],
        )
        from_peer, weights = tie((from_peer, weights))
        sides = []
        for source in (context, from_peer):
            across = swap(source, "tp", 2)
            sides.append(
                [(source, 0), (swap(source, "tp", 1), 1), (across, 0), (swap(across, "tp", 1), 1)]
            )
        pieces = [sides[h][t] for t in range(4) for h in range(2)]

    with jax.named_scope("mixer"):
        sent, kept, received = [], [], []
        for first, size in chunks:
            s, k = mixer(place, pieces, tokens, mixer_gain, weights, first, size)
            sent.append(s)
            kept.append(k)
            received.append(swap(s, "tp", 2))
            if first == 0:
                merge_own, _ = tie((jnp.transpose(merge_weight), s))
                merge_other = swap(merge_own, "tp", 1)

    with jax.named_scope("merge"):
        merge_other, position, index, _ = tie((merge_other, position, index, sent[-1]))
        weights = load_merge(merge_own, merge_other)
        earlier = []
        for c, (first, _) in enumerate(chunks[:-1]):
            earlier = [
                gather(place, index, kept[c], received[c], output_gain, first, earlier)
            ]
        weights, earlier, last, position = tie((weights, earlier[0], received[-1], position))
        first = chunks[-1][0]
        own, other = merge(
            place, index, kept[-1], last, output_gain, first, earlier, weights
        )
        other = swap(other, "tp", 1)

    with jax.named_scope("place"):
        columns = own.shape[1]
        outgoing = pl.pallas_call(
            place_kernel,
            in_specs=[RESIDENT] * 3,
            out_specs=RESIDENT,
            out_shape=jax.ShapeDtypeStruct((peers * capacity, columns), jnp.bfloat16),
            compiler_params=vmem(10),
            name="place",
        )(position, in_vmem(own), in_vmem(other))
        outgoing = outgoing.reshape(peers, capacity, columns)
        arrived = lax.all_to_all(outgoing, "req", split_axis=0, concat_axis=0, tiled=True)
    return arrived.reshape(1, peers, capacity, columns)


def solution(mesh):
    placed = (
        P("req", None),
        P("req"),
        P(),
        P(None, None, "tp"),
        P("tp", None),
        P(),
        P(None, "tp"),
        P("tp", None),
        P(),
        P(None, "tp"),
        P("req", None),
        P("req", None),
    )
    return jax.shard_map(
        body, mesh=mesh, in_specs=placed, out_specs=P("req", None, None, "tp"), check_vma=False
    )
```

```python
import functools
import math

import jax
import jax.numpy as jnp
from jax import lax
from jax.experimental import pallas as pl
from jax.experimental.pallas import tpu as pltpu
from jax.sharding import PartitionSpec as P

HD = 80
TILE = 512
MASKED = -1e30
START = -1e28
FACTOR = 1.0 / math.sqrt(HD)
SEGMENT_ROWS = 16
VROWS = 96
LANES = 256
AHEAD = 2
SMALL = 72.0


def swap(block, axis, flip):
    return lax.ppermute(block, axis, [(i, i ^ flip) for i in range(lax.axis_size(axis))])


def next_pair(i, first, size):
    other = i + 2 if i // 2 % 2 == first else i - 2
    return other if 0 <= other < size else i


def swap_pairs(block, first):
    size, width = lax.axis_size("req"), lax.axis_size("tp")
    route = []
    for i in range(size):
        other = next_pair(i, first, size)
        for t in range(width):
            route.append((i * width + t, other * width + (t if other != i else t ^ 1)))
    return lax.ppermute(block, ("req", "tp"), route)


def alone(first):
    size = lax.axis_size("req")
    lonely = [i for i in range(size) if next_pair(i, first, size) == i]
    return sum([(lax.axis_index("req") == i).astype(jnp.int32) for i in lonely], jnp.int32(0))


def normalized(stream, gain):
    center = jnp.mean(stream, axis=-1, keepdims=True)
    moved = stream - center
    spread = jnp.mean(moved * moved, axis=-1, keepdims=True)
    return (moved * lax.rsqrt(spread + 1e-06) * gain).astype(jnp.bfloat16)


def dot(a, b, contract):
    return lax.dot_general(a, b, (contract, ((), ())), preferred_element_type=jnp.float32)


NN = ((1,), (0,))
NT = ((1,), (1,))


def row_of(gain_ref):
    return gain_ref[...].astype(jnp.float32).reshape(1, gain_ref.shape[0])


def vmem(mebibytes=60):
    return pltpu.CompilerParams(vmem_limit_bytes=mebibytes << 20)


def in_hbm(array):
    return pltpu.with_memory_space_constraint(array, pltpu.HBM)


def in_vmem(array):
    return pltpu.with_memory_space_constraint(array, pltpu.VMEM)


SCALARS = pl.BlockSpec(memory_space=pltpu.SMEM)
RESIDENT = pl.BlockSpec(memory_space=pltpu.VMEM)
ANYWHERE = pl.BlockSpec(memory_space=pl.ANY)


def load_mixer_kernel(place, *refs):
    wo_refs, we_refs, wr_refs, refs = refs[:4], refs[4:6], refs[6:8], refs[8:]
    wo, we, wr, sems = refs
    half = wo.shape[0] // 8
    copies = []
    for i in range(8):
        source = wo_refs[i // 2].at[place[0] ^ (i % 2)]
        copies.append((source, wo.at[pl.ds(i * half, half)]))
    copies += [(we_refs[i], we.at[i]) for i in range(2)]
    copies += [(wr_refs[i], wr.at[i]) for i in range(2)]
    copies = [pltpu.make_async_copy(*pair, sems.at[i]) for i, pair in enumerate(copies)]
    for copy in copies:
        copy.start()
    for copy in copies:
        copy.wait()


def load_mixer(place, wo, expand, reduce):
    half, width = wo[0].shape[1:]
    shapes = [(8 * half, width), (2,) + expand[0].shape, (2,) + reduce[0].shape]
    return pl.pallas_call(
        load_mixer_kernel,
        in_specs=[SCALARS] + [ANYWHERE] * 8,
        out_specs=[RESIDENT] * 3,
        out_shape=[pltpu.VMEM(shape, jnp.bfloat16) for shape in shapes],
        scratch_shapes=[pltpu.SemaphoreType.DMA((12,))],
        compiler_params=vmem(4),
        cost_estimate=pl.CostEstimate(flops=0, bytes_accessed=16_000_000, transcendentals=0),
        name="load_mixer",
    )(place, *[in_hbm(w) for w in (*wo, *expand, *reduce)])


def load_merge_kernel(own, other, both, sems):
    columns = own.shape[0]
    copies = [
        pltpu.make_async_copy(source, both.at[pl.ds(i * columns, columns)], sems.at[i])
        for i, source in enumerate((own, other))
    ]
    for copy in copies:
        copy.start()
    for copy in copies:
        copy.wait()


def load_merge(own, other):
    return pl.pallas_call(
        load_merge_kernel,
        in_specs=[ANYWHERE] * 2,
        out_specs=RESIDENT,
        out_shape=pltpu.VMEM((2 * own.shape[0], own.shape[1]), jnp.bfloat16),
        scratch_shapes=[pltpu.SemaphoreType.DMA((2,))],
        compiler_params=vmem(4),
        cost_estimate=pl.CostEstimate(flops=0, bytes_accessed=8_000_000, transcendentals=0),
        name="load_merge",
    )(in_hbm(own), in_hbm(other))


def project_kernel(parts, x_ref, segment_ref, gain_ref, *refs):
    w_refs, keep, send = refs[:parts], refs[parts], refs[parts + 1]
    first = lax.axis_index("req") % 2 == 0
    half = w_refs[0].shape[0] // 2
    rows = normalized(x_ref[...].astype(jnp.float32), row_of(gain_ref))
    for part in range(parts):
        out = dot(w_refs[part][...], rows, NT)
        low, high = out[:half], out[half:]
        at = slice(part * half, (part + 1) * half)
        keep[at, :] = jnp.where(first, low, high).astype(jnp.bfloat16)
        send[at, :] = jnp.where(first, high, low).astype(jnp.bfloat16)
    if parts > 1:
        number = segment_ref[...] + 1
        row = lax.broadcasted_iota(jnp.int32, (SEGMENT_ROWS, 1), 0)
        number = jnp.where(row == 0, number & 255, jnp.where(row == 1, number >> 8, 0))
        number = number.astype(jnp.float32).astype(jnp.bfloat16)
        keep[parts * half :, :] = number
        send[parts * half :, :] = number


def project(tokens, segments, gain, weight, parts, name):
    rows, width = tokens.shape
    half = weight.shape[0] // 6
    step = 256
    tall = len(parts) * half + (SEGMENT_ROWS if len(parts) > 1 else 0)
    return pl.pallas_call(
        functools.partial(project_kernel, len(parts)),
        grid=(rows // step,),
        in_specs=[
            pl.BlockSpec((step, width), lambda i: (i, 0)),
            pl.BlockSpec((1, step), lambda i: (0, i)),
            pl.BlockSpec(gain.shape, lambda i: (0,)),
        ]
        + [pl.BlockSpec((2 * half, width), lambda i, p=p: (p, 0)) for p in parts],
        out_specs=[pl.BlockSpec((tall, step), lambda i: (0, i))] * 2,
        out_shape=[pltpu.HBM((tall, rows), jnp.bfloat16)] * 2,
        compiler_params=vmem(),
        name=name,
    )(tokens, segments, gain, *[weight] * len(parts))


def numbers_of(ref, at):
    two = ref[:, at].astype(jnp.float32)
    return two[0:1] + 256.0 * two[1:2]


def largest_norm(first, second):
    squares = []
    for block in (first, second):
        block = block.astype(jnp.float32)
        squares.append(jnp.sum(block * block, axis=0, keepdims=True))
    return jnp.max(jnp.maximum(squares[0], squares[1]))


def attend_kernel(blocks, flags, resumed, skips, last, place, *refs):
    groups = len(resumed)
    q_refs, number_refs, refs = refs[:groups], refs[groups : 2 * groups], refs[2 * groups :]
    kv_refs, refs = refs[:blocks], refs[blocks:]
    state_refs = []
    for old in resumed:
        state_refs.append(refs[:2] if old else None)
        refs = refs[2:] if old else refs
    outs, refs = refs[: groups * (1 if last else 2)], refs[groups * (1 if last else 2) :]
    keys, values, columns, acc, peak, bounds, plain = refs
    tiles_of = kv_refs[0].shape[1] // TILE
    tiles = blocks * tiles_of
    tall = kv_refs[0].shape[0] - SEGMENT_ROWS

    for b in range(blocks):
        for t in range(tiles_of):
            n = b * tiles_of + t
            at = slice(t * TILE, (t + 1) * TILE)
            for h in range(2):
                block = kv_refs[b][h * HD : (h + 1) * HD, at].astype(jnp.float32)
                keys[n, h] = jnp.transpose(block).astype(jnp.bfloat16)
                values[n, h, :HD] = kv_refs[b][(2 + h) * HD : (3 + h) * HD, at]
                values[n, h, HD:] = jnp.ones((VROWS - HD, TILE), jnp.bfloat16)
            number = numbers_of(kv_refs[b].at[tall:], at)
            low, high = jnp.min(number), jnp.max(number)
            if b in flags:
                low = jnp.where(place[flags[b]] == 1, -1.0, low)
                high = jnp.where(place[flags[b]] == 1, -1.0, high)
            bounds[3 * n] = low
            bounds[3 * n + 1] = high
            bounds[3 * n + 2] = largest_norm(kv_refs[b][:HD, at], kv_refs[b][HD : 2 * HD, at])
            columns[n] = jnp.transpose(jnp.broadcast_to(number, (128, TILE)))

    units = [(slice(c, c + LANES), h) for c in range(0, TILE, LANES) for h in range(2)]

    def attend_tile(g, j):
        if resumed[g]:
            acc[...] = state_refs[g][0][j]
            peak[...] = state_refs[g][1][j]
            plain[0] = (jnp.max(jnp.abs(state_refs[g][1][j])) == 0.0).astype(jnp.int32)
        else:
            acc[...] = jnp.zeros_like(acc)
            peak[...] = jnp.zeros_like(peak)
            plain[0] = 1
        mine = pl.ds(pl.multiple_of((j ^ place[1]) * TILE, TILE), TILE)
        q_row = numbers_of(number_refs[g].at[tall:], mine)
        queries = q_refs[g][:, mine]
        q_low, q_high = jnp.min(q_row), jnp.max(q_row)
        q_norm = largest_norm(queries[:HD], queries[HD:])

        def scores_of(t, h, at, matches):
            scores = dot(keys[t, h], queries[h * HD : (h + 1) * HD, at], NN)
            return scores if matches is None else jnp.where(matches, scores, MASKED)

        def matches_of(t, at):
            column = columns[t]
            return jnp.concatenate([column] * (LANES // 128), axis=1) == q_row[:, at]

        def unshifted(t, masked):
            scores, probs, matches = {}, {}, None
            for i in range(len(units) + AHEAD + 1):
                if i < len(units):
                    at, h = units[i]
                    if masked and h == 0:
                        matches = matches_of(t, at)
                    scores[i] = scores_of(t, h, at, matches)
                if 0 <= i - AHEAD < len(units):
                    probs[i - AHEAD] = jnp.exp(scores.pop(i - AHEAD) * FACTOR).astype(jnp.bfloat16)
                if 0 <= i - AHEAD - 1 < len(units):
                    at, h = units[i - AHEAD - 1]
                    acc[h, :, at] += dot(values[t, h], probs.pop(i - AHEAD - 1), NN)

        def shifted_by_peak(t):
            for at, h in units:
                scores = scores_of(t, h, at, matches_of(t, at))
                old = jnp.where(acc[h, HD : HD + 1, at] > 0.0, peak[h : h + 1, at], START)
                new = jnp.maximum(old, jnp.max(scores, axis=0, keepdims=True))
                probs = jnp.exp((scores - new) * FACTOR).astype(jnp.bfloat16)
                shrink = jnp.exp((old - new) * FACTOR)
                peak[h : h + 1, at] = new
                acc[h, :, at] = acc[h, :, at] * shrink + dot(values[t, h], probs, NN)
            plain[0] = 0

        def visit(t, carry):
            k_low, k_high = bounds[3 * t], bounds[3 * t + 1]
            touches = (k_high >= q_low) & (k_low <= q_high)
            whole = (k_low == k_high) & (q_low == q_high)
            small = (plain[0] == 1) & (q_norm * bounds[3 * t + 2] <= SMALL * SMALL * HD)

            @pl.when(touches & small & whole)
            def _():
                unshifted(t, False)

            @pl.when(touches & small & jnp.logical_not(whole))
            def _():
                unshifted(t, True)

            @pl.when(touches & jnp.logical_not(small))
            def _():
                shifted_by_peak(t)

            return carry

        lax.fori_loop(skips[g] * tiles_of, tiles, visit, 0)
        if last:
            for h in range(2):
                at = slice(h * HD, (h + 1) * HD)
                outs[g][j, at, :] = (acc[h, :HD] / acc[h, HD : HD + 1]).astype(jnp.bfloat16)
        else:
            outs[2 * g][j] = acc[...]
            outs[2 * g + 1][j] = peak[...]

    for g in range(groups):

        def step(j, carry, g=g):
            attend_tile(g, j)
            return carry

        lax.fori_loop(0, tiles_of, step, 0)


def attend(place, queries, numbers, key_values, name, flags, states, skips, last=False):
    half, rows = queries[0].shape
    groups, blocks = len(queries), len(key_values)
    tiles_of = rows // TILE
    tiles = blocks * tiles_of
    acc_shape, peak_shape = (2, VROWS, TILE), (2, TILE)
    operands = [*queries, *numbers, *key_values]
    for state in states:
        operands += [] if state is None else list(state)
    if last:
        out_shape = [pltpu.VMEM((tiles_of, half, TILE), jnp.bfloat16)] * groups
    else:
        out_shape = [
            pltpu.VMEM((tiles_of,) + acc_shape, jnp.float32),
            pltpu.VMEM((tiles_of,) + peak_shape, jnp.float32),
        ] * groups
    resumed = [state is not None for state in states]
    out = pl.pallas_call(
        functools.partial(attend_kernel, blocks, flags, resumed, skips, last),
        in_specs=[SCALARS] + [RESIDENT] * len(operands),
        out_specs=[RESIDENT] * len(out_shape),
        out_shape=out_shape,
        scratch_shapes=[
            pltpu.VMEM((tiles, 2, TILE, HD), jnp.bfloat16),
            pltpu.VMEM((tiles, 2, VROWS, TILE), jnp.bfloat16),
            pltpu.VMEM((tiles, TILE, 128), jnp.float32),
            pltpu.VMEM(acc_shape, jnp.float32),
            pltpu.VMEM(peak_shape, jnp.float32),
            pltpu.SMEM((3 * tiles,), jnp.float32),
            pltpu.SMEM((1,), jnp.int32),
        ],
        compiler_params=vmem(24),
        cost_estimate=pl.CostEstimate(flops=1_000_000, bytes_accessed=1_000_000, transcendentals=0),
        name=name,
    )(place, *[in_vmem(a) for a in operands])
    return list(out) if last else [out[2 * g : 2 * g + 2] for g in range(groups)]


def mixer_kernel(first, which, place, *refs):
    sources, refs = refs[:8], refs[8:]
    x_hbm, gain_ref, wo, we, wr, sent, kept, context, hidden, x, sem = refs
    rows = x.shape[0]
    half = sources[0].shape[1]
    width = we.shape[2]
    fetch = pltpu.make_async_copy(
        x_hbm.at[pl.ds(pl.multiple_of(place[2] + first, 128), rows)], x, sem
    )
    fetch.start()
    lanes = slice(first, first + rows)
    for i in range(8):
        context[i * half : (i + 1) * half, :] = sources[i][which[i], :, lanes].astype(jnp.float32)
    inputs = jnp.transpose(context[...]).astype(jnp.bfloat16)
    fetch.wait()
    total = x[...].astype(jnp.float32) + dot(inputs, wo[...], NN)
    inputs = normalized(total, row_of(gain_ref))
    for i in range(2):
        inner = dot(inputs, we[i], NN)
        grown = 0.5 * inner * (1.0 + lax.erf(inner * (1.0 / math.sqrt(2.0))))
        hidden[:, i * width : (i + 1) * width] = grown.astype(jnp.bfloat16)
    out = dot(hidden[:, :width], wr[0], NN) + dot(hidden[:, width:], wr[1], NN)
    sent[...] = out.astype(jnp.bfloat16)
    kept[...] = total + out


def mixer(place, pieces, tokens, gain, weights, first, chunk_rows):
    width = tokens.shape[1]
    half = pieces[0][0].shape[1]
    hidden = weights[1].shape[2]
    return pl.pallas_call(
        functools.partial(mixer_kernel, first, [which for _, which in pieces]),
        in_specs=[SCALARS] + [RESIDENT] * 8 + [ANYWHERE] + [RESIDENT] * 4,
        out_specs=[RESIDENT] * 2,
        out_shape=[
            jax.ShapeDtypeStruct((chunk_rows, width), jnp.bfloat16),
            jax.ShapeDtypeStruct((chunk_rows, width), jnp.float32),
        ],
        scratch_shapes=[
            pltpu.VMEM((8 * half, chunk_rows), jnp.float32),
            pltpu.VMEM((chunk_rows, 2 * hidden), jnp.bfloat16),
            pltpu.VMEM((chunk_rows, width), jnp.bfloat16),
            pltpu.SemaphoreType.DMA,
        ],
        compiler_params=vmem(30),
        cost_estimate=pl.CostEstimate(
            flops=5_000_000_000, bytes_accessed=20_000_000, transcendentals=0
        ),
        name="mixer",
    )(place, *[source for source, _ in pieces], tokens, gain, *[in_vmem(w) for w in weights])


def one_hot_rows(index_ref, k, first, rows):
    column = jnp.transpose(jnp.broadcast_to(index_ref[k : k + 1, :], (128, index_ref.shape[1])))
    lanes = lax.broadcasted_iota(jnp.int32, (1, 128), 1)
    parts = [column == lanes + (first + 128 * n) for n in range(rows // 128)]
    return jnp.concatenate(parts, axis=1).astype(jnp.float32).astype(jnp.bfloat16)


def gather_kernel(first, place, index_ref, kept, received, gain_ref, *refs):
    merged = refs[-1]
    rows = kept.shape[0]
    final = normalized(kept[...] + received[...].astype(jnp.float32), row_of(gain_ref))
    for k in range(4):
        part = dot(one_hot_rows(index_ref, k, place[2] + first, rows), final, NN)
        if len(refs) > 1:
            part = part + refs[0][k].astype(jnp.float32)
        merged[k] = part.astype(jnp.bfloat16)


def gather(place, index, kept, received, gain, first, earlier):
    return pl.pallas_call(
        functools.partial(gather_kernel, first),
        in_specs=[SCALARS] + [RESIDENT] * (4 + len(earlier)),
        out_specs=RESIDENT,
        out_shape=pltpu.VMEM((4, index.shape[1], kept.shape[1]), jnp.bfloat16),
        compiler_params=vmem(20),
        cost_estimate=pl.CostEstimate(
            flops=1_000_000_000, bytes_accessed=5_000_000, transcendentals=0
        ),
        name="gather",
    )(place, index, kept, received, gain, *[in_vmem(a) for a in earlier])


def merge_kernel(
    first, place, index_ref, kept, received, gain_ref, earlier, weights, own, other, parts
):
    rows, width = kept.shape
    columns = own.shape[1]
    final = normalized(kept[...] + received[...].astype(jnp.float32), row_of(gain_ref))
    for k in range(4):
        part = dot(one_hot_rows(index_ref, k, place[2] + first, rows), final, NN)
        part = part + earlier[k].astype(jnp.float32)
        parts[:, k * width : (k + 1) * width] = part.astype(jnp.bfloat16)
    total = dot(parts[...], weights[...], NT)
    own[...] = total[:, :columns]
    other[...] = total[:, columns:]


def merge(place, index, kept, received, gain, first, earlier, weights):
    merged_rows = index.shape[1]
    columns = weights.shape[0] // 2
    return pl.pallas_call(
        functools.partial(merge_kernel, first),
        in_specs=[SCALARS] + [RESIDENT] * 6,
        out_specs=[RESIDENT] * 2,
        out_shape=[jax.ShapeDtypeStruct((merged_rows, columns), jnp.float32)] * 2,
        scratch_shapes=[pltpu.VMEM((merged_rows, weights.shape[1]), jnp.bfloat16)],
        compiler_params=vmem(20),
        cost_estimate=pl.CostEstimate(
            flops=3_000_000_000, bytes_accessed=12_000_000, transcendentals=0
        ),
        name="merge",
    )(place, index, kept, received, gain, in_vmem(earlier), in_vmem(weights))


def place_kernel(position, own, received, out):
    feature = (own[...] + received[...]).astype(jnp.bfloat16)
    slots = lax.broadcasted_iota(jnp.int32, (out.shape[0], 1), 0)
    chosen = (slots == position[...]).astype(jnp.float32).astype(jnp.bfloat16)
    out[...] = dot(chosen, feature, NN).astype(jnp.bfloat16)


def body(
    tokens,
    segments,
    attend_gain,
    attend_weight,
    output_weight,
    mixer_gain,
    expand_weight,
    reduce_weight,
    output_gain,
    merge_weight,
    merge_index,
    owners,
):
    rows, width = tokens.shape
    head_width = attend_weight.shape[2]
    half = head_width // 2
    peers = lax.axis_size("req")
    req = lax.axis_index("req")
    par = req % 2
    core = lax.axis_index("tp") % 2

    per_core = rows // 2
    chunks = [(first, 128) for first in range(0, per_core, 128)]
    place = jnp.stack([par, core, core * per_core, req, alone(0), alone(1)])
    tie = lax.optimization_barrier
    with jax.named_scope("weights"):
        wo_own = output_weight.reshape(2, half, width)
        wo_core = swap(wo_own, "tp", 1)
        expand_other = swap(expand_weight, "tp", 1)

    with jax.named_scope("project"):
        weight = jnp.transpose(attend_weight, (1, 2, 0)).reshape(6 * half, width)
        numbers = segments[None, :]
        kv_own, kv_send = project(tokens, numbers, attend_gain, weight, (1, 2), "project_keys")
        kv_own, kv_send, expand_other, wo_core = tie((kv_own, kv_send, expand_other, wo_core))

    with jax.named_scope("slots"):
        capacity = 2 * merge_index.shape[0] // peers
        target = owners[:, 0]
        choose = (target[:, None] == jnp.arange(peers, dtype=jnp.int32)[None, :]).astype(jnp.int32)
        slot = jnp.sum((jnp.cumsum(choose, axis=0) - 1) * choose, axis=1)
        position = (target * capacity + slot)[None, :]
        index = jnp.transpose(merge_index) - req * rows

    with jax.named_scope("exchange_keys"):
        kv_peer = swap(kv_send, "req", 1)
        kv_even = swap_pairs(kv_own, 0)
        kv_odd = swap_pairs(kv_own, 1)
        wo_across = swap(wo_own, "tp", 2)
        q_own, q_send = project(tokens, numbers, attend_gain, weight, (0,), "project_queries")
        q_peer = swap(q_send, "req", 1)
        (state,) = attend(place, [q_own], [kv_own], [kv_own], "attend_own", {}, [None], [0])
        kv_odd, kv_even, kv_peer, state, wo_across, late_reduce, late_wo, position, index = tie(
            (kv_odd, kv_even, kv_peer, state, wo_across, reduce_weight, wo_core, position, index)
        )
        kv_even_peer = swap_pairs(kv_peer, 0)
        kv_odd_peer = swap_pairs(kv_peer, 1)
        reduce_other = swap(late_reduce, "tp", 1)
        wo_both = swap(late_wo, "tp", 2)


    with jax.named_scope("attention"):
        queries, numbers = [q_peer, q_own], [kv_peer, kv_own]
        near = [kv_own, kv_peer, kv_even, kv_odd]
        states = [None, state]
        states = attend(
            place, queries, numbers, near, "attend_near", {2: 4, 3: 5}, states, [0, 1]
        )
        states, kv_even_peer, kv_odd_peer, reduce_other, wo_both = tie(
            (states, kv_even_peer, kv_odd_peer, reduce_other, wo_both)
        )
        far = [kv_even_peer, kv_odd_peer]
        for_peer, context = attend(
            place, queries, numbers, far, "attend_far", {0: 4, 1: 5}, states, [0, 0], True
        )

    with jax.named_scope("exchange_context"):
        late_wo, context, for_peer = tie((wo_own, context, for_peer))
        from_peer = swap(for_peer, "req", 1)
        weights = load_mixer(
            place,
            [late_wo, wo_core, wo_across, wo_both],
            [expand_weight, expand_other],
            [reduce_weight, reduce_other],
        )
        from_peer, weights = tie((from_peer, weights))
        sides = []
        for source in (context, from_peer):
            across = swap(source, "tp", 2)
            sides.append(
                [(source, 0), (swap(source, "tp", 1), 1), (across, 0), (swap(across, "tp", 1), 1)]
            )
        pieces = [sides[h][t] for t in range(4) for h in range(2)]

    with jax.named_scope("mixer"):
        sent, kept, received = [], [], []
        for first, size in chunks:
            s, k = mixer(place, pieces, tokens, mixer_gain, weights, first, size)
            sent.append(s)
            kept.append(k)
            received.append(swap(s, "tp", 2))
            if first == 0:
                merge_own, _ = tie((jnp.transpose(merge_weight), s))
                merge_other = swap(merge_own, "tp", 1)

    with jax.named_scope("merge"):
        merge_other, position, index, _ = tie((merge_other, position, index, sent[-1]))
        weights = load_merge(merge_own, merge_other)
        earlier = []
        for c, (first, _) in enumerate(chunks[:-1]):
            earlier = [
                gather(place, index, kept[c], received[c], output_gain, first, earlier)
            ]
        weights, earlier, last, position = tie((weights, earlier[0], received[-1], position))
        first = chunks[-1][0]
        own, other = merge(
            place, index, kept[-1], last, output_gain, first, earlier, weights
        )
        other = swap(other, "tp", 1)

    with jax.named_scope("place"):
        columns = own.shape[1]
        outgoing = pl.pallas_call(
            place_kernel,
            in_specs=[RESIDENT] * 3,
            out_specs=RESIDENT,
            out_shape=jax.ShapeDtypeStruct((peers * capacity, columns), jnp.bfloat16),
            compiler_params=vmem(10),
            name="place",
        )(position, in_vmem(own), in_vmem(other))
        outgoing = outgoing.reshape(peers, capacity, columns)
        arrived = lax.all_to_all(outgoing, "req", split_axis=0, concat_axis=0, tiled=True)
    return arrived.reshape(1, peers, capacity, columns)


def solution(mesh):
    placed = (
        P("req", None),
        P("req"),
        P(),
        P(None, None, "tp"),
        P("tp", None),
        P(),
        P(None, "tp"),
        P("tp", None),
        P(),
        P(None, "tp"),
        P("req", None),
        P("req", None),
    )
    return jax.shard_map(
        body, mesh=mesh, in_specs=placed, out_specs=P("req", None, None, "tp"), check_vma=False
    )
```
